32 devices in a mesh: dp: 4 (over y, x), fsdp: 8 (over z, core).
Axes of the slice: x: 2, y: 2, z: 4, core: 2. Of those that a mesh axis runs over, the one named last changes fastest.
Arguments:
- images: bfloat16 [128, 282, 768], P(('dp', 'fsdp')), may hold values from -18 to 18
- grid_sizes: int32 [128, 2], P(('dp', 'fsdp')), may hold values from 8 to 24, as said below
- keep_flags: int32 [128, 2], P(('dp', 'fsdp')), may hold values 0 or 1
- attn_gain: bfloat16 [768], P('fsdp'), may hold values from 0.25 to 1.75
- attn_shift: bfloat16 [768], P('fsdp'), may hold values from -4 to 4
- attend_weight: bfloat16 [768, 2304], P(None, 'fsdp'), may hold values from -0.3125 to 0.3125
- query_bias: bfloat16 [768], P('fsdp'), may hold values from -6 to 6
- value_bias: bfloat16 [768], P('fsdp'), may hold values from -6 to 6
- output_weight: bfloat16 [768, 768], P('fsdp'), may hold values from -1.25 to 1.25
- output_bias: bfloat16 [768], P('fsdp'), may hold values from -4 to 4
- mlp_gain: bfloat16 [768], P('fsdp'), may hold values from 0.25 to 1.75
- mlp_shift: bfloat16 [768], P('fsdp'), may hold values from -4 to 4
- up_weight: bfloat16 [768, 3072], P(None, 'fsdp'), may hold values from -0.21875 to 0.21875
- up_bias: bfloat16 [3072], P('fsdp'), may hold values from -6 to 6
- down_weight: bfloat16 [3072, 768], P('fsdp'), may hold values from -0.15625 to 0.15625
- down_bias: bfloat16 [768], P('fsdp'), may hold values from -4 to 4
- cotangent: bfloat16 [128, 282, 768], P(('dp', 'fsdp')), may hold values from -6 to 6
Outputs:
- output: bfloat16 [128, 282, 768], P(('dp', 'fsdp'))
- grad_images: float32 [128, 282, 768], P(('dp', 'fsdp'))
- grad_attn_gain: float32 [768], P('fsdp')
- grad_attn_shift: float32 [768], P('fsdp')
- grad_attend_weight: float32 [768, 2304], P(None, 'fsdp')
- grad_query_bias: float32 [768], P('fsdp')
- grad_value_bias: float32 [768], P('fsdp')
- grad_output_weight: float32 [768, 768], P('fsdp')
- grad_output_bias: float32 [768], P('fsdp')
- grad_mlp_gain: float32 [768], P('fsdp')
- grad_mlp_shift: float32 [768], P('fsdp')
- grad_up_weight: float32 [768, 3072], P(None, 'fsdp')
- grad_up_bias: float32 [3072], P('fsdp')
- grad_down_weight: float32 [3072, 768], P('fsdp')
- grad_down_bias: float32 [768], P('fsdp')
- root_means: float32 [3], replicated
The draws below stay inside these ranges and needn't reach their ends.
Inputs may be any that keep to these rules, and one draw needn't show every extreme that they name: `grid_sizes`: each image has rows from 8 to 20 and cols at most min(24, 280 // rows) and at least min(24, 280 // rows) - 2; its first rows * cols + 2 token slots are valid, at most 282. Image 0 has 20 x 14, filling all 282 slots; image 1 has 8 rows.
All inputs are finite; a program needn't handle non-finite values. No bound on the sum of `keep_flags` on one device may be relied on, other than what follows from the above.
Results may differ from the reference program's by a relative error of at most 0.015.
The reference program's roundings to bfloat16 on the way count: a program that leaves them out, or rounds other values in their place, can miss the bound.
Values may be sent and summed in bfloat16 or wider, within the bound.
No kernel may reach another device: no remote copies, remote signals or barrier semaphores. Data moves between devices by JAX's collectives and lax.ppermute only.
A program may use at most 192 MiB of HBM per device.

```python
import math
import jax
import jax.numpy as jnp
from jax import lax

D = 768
HEADS = 12
HEAD_DIM = 64
FF = 3072
IMG_BLOCK = 2
ROW_LO = 8
ROW_HI = 20
COL_HI = 24
COL_TALL = 14
PATCHES = 280
SEQ = 282
IMAGES = 128


def draw_grid_sizes(key, part):
    first_key, second_key = jax.random.split(jax.random.fold_in(key, 11))
    rows = jax.random.randint(first_key, (IMAGES,), ROW_LO, ROW_HI + 1)
    top_cols = jnp.minimum(COL_HI, PATCHES // rows)
    cols = top_cols - jax.random.randint(second_key, (IMAGES,), 0, 3)
    rows = rows.at[0].set(ROW_HI).at[1].set(ROW_LO)
    cols = cols.at[0].set(COL_TALL).at[1].set(min(COL_HI, PATCHES // ROW_LO))
    return jnp.stack([rows, cols], 1).astype(jnp.int32)


def draw_images(key, part):
    inner_key = jax.random.fold_in(key, 23)
    position = jnp.arange(IMAGES, dtype=jnp.float32) / max(IMAGES - 1, 1)
    entries = jax.random.truncated_normal(inner_key, -6.0, 6.0, (IMAGES, SEQ, D), jnp.float32)
    scales = jnp.exp(position * 1.0986123)
    return (entries * scales[:, None, None]).astype(jnp.bfloat16)


def place_ends(values, own_key, least, top_value):
    shape = values.shape
    index_at = [jax.random.randint(jax.random.fold_in(own_key, axis), (), 0, shape[axis]) for axis in range(len(shape))]
    values = values.at[tuple(index_at)].set(least)
    longest = shape.index(max(shape))
    index_at[longest] = (index_at[longest] + 1) % shape[longest]
    return values.at[tuple(index_at)].set(top_value)


def block_levels(stream_key, dims, cuts, low, largest):
    gain, own = 1.0, jax.random.fold_in(stream_key, 6)
    for dim, shards_of in cuts:
        draws = jnp.exp(jax.random.uniform(jax.random.fold_in(own, dim), (shards_of,), jnp.float32, low / len(cuts), largest / len(cuts)))
        gain = gain * jnp.repeat(draws, dims[dim] // shards_of).reshape([-1 if axis == dim else 1 for axis in range(len(dims))])
    return gain


def normal_values(stream_key, dims, width, bound, cuts=(), kind=jnp.bfloat16):
    values = width * jax.random.normal(stream_key, dims, jnp.float32)
    if cuts:
        values = values * block_levels(stream_key, dims, cuts, -0.22, 0.18)
    return jnp.clip(values, -bound, bound).astype(kind)


def setup_inputs(seed: int = 0) -> dict:
    arg_keys = jax.random.split(jax.random.key(seed), 18)
    return {
        "images": draw_images(jax.random.fold_in(arg_keys[17], 71), 0),
        "grid_sizes": draw_grid_sizes(jax.random.fold_in(arg_keys[17], 71), 0),
        "keep_flags": place_ends((jax.random.randint(arg_keys[2], (IMAGES, 2), 0, 10) < 9).astype(jnp.int32), jax.random.fold_in(arg_keys[2], 1), 0, 1),
        "attn_gain": jnp.clip(1.0 + 0.15 * jax.random.normal(arg_keys[3], (D,), jnp.float32), 0.25, 1.75).astype(jnp.bfloat16),
        "attn_shift": normal_values(arg_keys[4], (D,), 0.3, 4.0, ((0, 8),)),
        "attend_weight": normal_values(arg_keys[5], (D, 3 * D), (D // 2) ** -0.5, 0.3125, ((1, 8),)),
        "query_bias": normal_values(arg_keys[6], (D,), 0.5, 6.0, ((0, 8),)),
        "value_bias": normal_values(arg_keys[7], (D,), 0.5, 6.0, ((0, 8),)),
        "output_weight": normal_values(arg_keys[8], (D, D), (D // 32) ** -0.5, 1.25, ((0, 8),)),
        "output_bias": normal_values(arg_keys[9], (D,), 0.3, 4.0, ((0, 8),)),
        "mlp_gain": jnp.clip(1.0 + 0.15 * jax.random.normal(arg_keys[10], (D,), jnp.float32), 0.25, 1.75).astype(jnp.bfloat16),
        "mlp_shift": normal_values(arg_keys[11], (D,), 0.3, 4.0, ((0, 8),)),
        "up_weight": normal_values(arg_keys[12], (D, FF), D ** -0.5, 0.21875, ((1, 8),)),
        "up_bias": normal_values(arg_keys[13], (FF,), 0.5, 6.0, ((0, 8),)),
        "down_weight": normal_values(arg_keys[14], (FF, D), (FF // 2) ** -0.5, 0.15625, ((0, 8),)),
        "down_bias": normal_values(arg_keys[15], (D,), 0.3, 4.0, ((0, 8),)),
        "cotangent": normal_values(arg_keys[16], (IMAGES, SEQ, D), 1.0, 6.0, ((0, 32),)),
    }


EPS = 1e-06
KEEP_PROB = 0.9
MASKED = -1e+30

@jax.custom_vjp
def low(v):
    return lax.optimization_barrier(v.astype(jnp.bfloat16)).astype(jnp.float32)

@jax.custom_vjp
def low_back(v):
    return v

def low_keep(v):
    return (low(v), None)

def low_pass(kept, grad):
    return (grad,)

def back_keep(v):
    return (v, None)

def back_low(kept, grad):
    return (low(grad),)
low.defvjp(low_keep, low_pass)
low_back.defvjp(back_keep, back_low)

def matmul(formula, left, right):
    return jnp.einsum(formula, left, right, precision=lax.Precision.HIGHEST)

def layer_norm(values, gain_vec, bias_vec):
    center = values - lax.optimization_barrier(jnp.mean(values, -1, keepdims=True))
    return center * lax.rsqrt(lax.optimization_barrier(jnp.mean(center * center, -1, keepdims=True)) + EPS) * gain_vec + bias_vec

def forward(inputs, params, valid, depth_scale):
    gain_first, shift_first, attend_whole, bias_query, bias_value, output_whole, bias_output, gain_second, shift_second, up_whole, bias_up, down_whole, bias_down = params
    image_count, seq_len, feature_dim = inputs.shape
    ln_first = low(layer_norm(inputs, gain_first, shift_first))
    bias_joint = jnp.concatenate([bias_query, jnp.zeros_like(bias_query), bias_value])
    joint = low_back(low(matmul('bld,de->ble', ln_first, attend_whole) + bias_joint))
    joint = joint.reshape(image_count, seq_len, 3, HEADS, HEAD_DIM)
    query = joint[:, :, 0]
    keys_in = joint[:, :, 1]
    values_in = joint[:, :, 2]
    scores = low_back(matmul('bqhe,bkhe->bhqk', query, keys_in) * (1.0 / math.sqrt(HEAD_DIM)))
    scores = jnp.where(valid[:, None, None, :] > 0, scores, MASKED)
    top_score = lax.optimization_barrier(jnp.max(scores, -1, keepdims=True))
    unnormed = jnp.exp(scores - top_score)
    probability = unnormed / lax.optimization_barrier(jnp.sum(unnormed, -1, keepdims=True))
    mixed = matmul('bhqk,bkhe->bqhe', low(probability), values_in).reshape(image_count, seq_len, feature_dim)
    mixed = low_back(low(mixed))
    attn_out = low_back(matmul('bld,de->ble', mixed, output_whole) + bias_output)
    middle = inputs + depth_scale[:, 0, None, None] * attn_out
    ln_second = low(layer_norm(middle, gain_second, shift_second))
    hidden_pre = low_back(matmul('bld,df->blf', ln_second, up_whole) + bias_up)
    activated = low(jax.nn.gelu(hidden_pre, approximate=False))
    mlp_out = low_back(matmul('blf,fd->bld', activated, down_whole) + bias_down)
    row_mask = valid[:, :, None]
    result = row_mask * (middle + depth_scale[:, 1, None, None] * mlp_out)
    sums = jnp.stack([jnp.sum(row_mask * middle * middle), jnp.sum(row_mask * attn_out * attn_out), jnp.sum(row_mask * mlp_out * mlp_out), jnp.sum(valid)])
    return (result, sums)

def reference(images, grid_sizes, keep_flags, attn_gain, attn_shift, attend_weight, query_bias, value_bias, output_weight, output_bias, mlp_gain, mlp_shift, up_weight, up_bias, down_weight, down_bias, cotangent):
    group = 4 * IMG_BLOCK
    steps_count = IMAGES // group
    params = tuple((weight.astype(jnp.float32) for weight in (attn_gain, attn_shift, attend_weight, query_bias, value_bias, output_weight, output_bias, mlp_gain, mlp_shift, up_weight, up_bias, down_weight, down_bias)))
    counts = grid_sizes[:, 0] * grid_sizes[:, 1] + 2
    valid = (jnp.arange(SEQ)[None, :] < counts[:, None]).astype(jnp.float32)
    depth_scale = keep_flags.astype(jnp.float32) / KEEP_PROB
    checked = jax.checkpoint(forward)

    def group_view(array):
        return array.reshape((steps_count, group) + array.shape[1:])

    def advance(carry, item):
        grad_total, sums_total = carry
        inputs, cot_block, valid_block, scale_block = item

        def apply(inp_block, param_block):
            return checked(inp_block, param_block, valid_block, scale_block)
        result, pull, sums = jax.vjp(apply, inputs, params, has_aux=True)
        grad_in, grad_params = pull(cot_block)
        grad_total = jax.tree.map(jnp.add, grad_total, grad_params)
        return ((grad_total, sums_total + sums), (result.astype(jnp.bfloat16), grad_in))
    zeros = jax.tree.map(jnp.zeros_like, params)
    (grads, sums), (outputs, grad_images) = lax.scan(advance, (zeros, jnp.zeros((4,), jnp.float32)), (group_view(images.astype(jnp.float32)), group_view(cotangent.astype(jnp.float32)), group_view(valid), group_view(depth_scale)))
    root_means = jnp.sqrt(sums[:3] / (sums[3] * D))
    return (outputs.reshape(IMAGES, SEQ, D), grad_images.reshape(IMAGES, SEQ, D), grads[0], grads[1], grads[2], grads[3], grads[4], grads[5], grads[6], grads[7], grads[8], grads[9], grads[10], grads[11], grads[12], root_means)
```

```python
import functools

import jax
import jax.numpy as jnp
from jax import lax
from jax.experimental import pallas as pl
from jax.experimental.pallas import tpu as pltpu
from jax.sharding import PartitionSpec as P

HEAD_DIM = 64
EPS = 1e-06
KEEP_PROB = 0.9
MASKED = -1e30
INV_ROOT_TWO = 0.7071067811865476
INV_ROOT_TWO_PI = 0.3989422804014327
F32 = jnp.float32
BF16 = jnp.bfloat16
MIB = 1024 * 1024


def nn(left, right):
    return lax.dot_general(left, right, (((1,), (0,)), ((), ())), preferred_element_type=F32)


def nt(left, right):
    return lax.dot_general(left, right, (((1,), (1,)), ((), ())), preferred_element_type=F32)


def tn(left, right):
    return lax.dot_general(left, right, (((0,), (0,)), ((), ())), preferred_element_type=F32)


def mean_row(values):
    return jnp.sum(values, -1, keepdims=True) * (1.0 / values.shape[-1])


def normalize(values):
    center = values - mean_row(values)
    rstd = lax.rsqrt(mean_row(center * center) + EPS)
    return center * rstd, rstd


def col_sum(values):
    return jnp.sum(values, 0, keepdims=True)


def params(limit, steps=1):
    return pltpu.CompilerParams(
        dimension_semantics=("arbitrary",) * steps, vmem_limit_bytes=limit * MIB
    )


def whole(shape, buffers=1):
    zeros = (0,) * len(shape)
    return pl.BlockSpec(shape, lambda *_: zeros, pipeline_mode=pl.Buffered(buffers))


def by_image(shape):
    rest = (0,) * len(shape)
    return pl.BlockSpec((1,) + shape, lambda i, *_: (i,) + rest)


SMEM = pl.BlockSpec(memory_space=pltpu.SMEM)


def front_kernel(seq, pad, counts, depth, x_ref, cot_ref, w_ref, gain_ref, shift_ref, bias_ref,
                 a1_ref, gm_ref, qkv_ref, o_ref, lse_ref, xs, lse_s):
    i = pl.program_id(0)
    width = x_ref.shape[-1]
    pairs = width // 128
    count = counts[i]
    rows = lax.broadcasted_iota(jnp.int32, (pad, 1), 0)
    xs[pad - 8:pad, :] = jnp.zeros((8, width), F32)
    xs[0:seq, :] = cot_ref[0].astype(F32)
    gm_ref[0] = jnp.where(rows < count, xs[...] * depth[i, 1], 0.0).astype(BF16)
    xs[0:seq, :] = x_ref[0].astype(F32)
    normed, _ = normalize(xs[...])
    a1 = (normed * gain_ref[...] + shift_ref[...]).astype(BF16)
    a1_ref[0] = a1
    for c in range(0, 3 * width, 384):
        qkv_ref[0, :, c:c + 384] = (nt(a1, w_ref[c:c + 384, :]) + bias_ref[:, c:c + 384]).astype(BF16)
    ok = lax.broadcasted_iota(jnp.int32, (pad, pad), 1) < count
    lane = lax.broadcasted_iota(jnp.int32, (pad, 128), 1)
    lse_s[...] = jnp.zeros((pad, 128), F32)

    def pair(p):
        at = pl.multiple_of(p * 128, 128)
        q = qkv_ref[0, :, pl.ds(at, 128)] * 0.125
        k = qkv_ref[0, :, pl.ds(width + at, 128)]
        v = qkv_ref[0, :, pl.ds(2 * width + at, 128)]
        total = jnp.zeros((pad, 128), F32)
        for half in range(2):
            mine = (lane >= 64) if half else (lane < 64)
            scores = jnp.where(ok, nt(jnp.where(mine, q, 0), k), MASKED)
            top = jnp.max(scores, -1, keepdims=True)
            e = jnp.exp(scores - top)
            s = jnp.sum(e, -1, keepdims=True)
            prob = (e * (1.0 / s)).astype(BF16)
            total = total + nn(prob, jnp.where(mine, v, 0))
            lse_s[...] = jnp.where(lane == 2 * p + half, top + jnp.log(s), lse_s[...])
        o_ref[0, :, pl.ds(at, 128)] = total.astype(BF16)

    for p in range(pairs):
        pair(p)
    lse_ref[0] = jnp.transpose(lse_s[...])[0:16, :]


def front(counts, depth, images, cot, w, gain, shift, bias, pad):
    n, seq, width = images.shape
    grid_spec = pltpu.PrefetchScalarGridSpec(
        num_scalar_prefetch=2,
        grid=(n,),
        in_specs=[
            by_image((seq, width)), by_image((seq, width)),
            whole(w.shape), whole(gain.shape), whole(shift.shape), whole(bias.shape),
        ],
        out_specs=[
            by_image((pad, width)), by_image((pad, width)), by_image((pad, 3 * width)),
            by_image((pad, width)), by_image((16, pad)),
        ],
        scratch_shapes=[pltpu.VMEM((pad, width), F32), pltpu.VMEM((pad, 128), F32)],
    )
    return pl.pallas_call(
        functools.partial(front_kernel, seq, pad),
        out_shape=[
            jax.ShapeDtypeStruct((n, pad, width), BF16),
            jax.ShapeDtypeStruct((n, pad, width), BF16),
            jax.ShapeDtypeStruct((n, pad, 3 * width), BF16),
            jax.ShapeDtypeStruct((n, pad, width), BF16),
            jax.ShapeDtypeStruct((n, 16, pad), F32),
        ],
        grid_spec=grid_spec,
        compiler_params=params(40),
        cost_estimate=pl.CostEstimate(
            flops=2 * n * pad * width * (3 * width + 4 * pad), bytes_accessed=20 * MIB,
            transcendentals=n * 12 * pad * pad),
        name="front",
    )(counts, depth, images, cot, w, gain, shift, bias)


def middle_kernel(seq, pad, counts, depth, o_ref, x_ref, w_ref, bias_ref, gain_ref, shift_ref,
                  x1_ref, a2_ref, sums_ref, xs):
    i = pl.program_id(0)
    width = x_ref.shape[-1]
    rows = lax.broadcasted_iota(jnp.int32, (pad, 1), 0)
    ok = rows < counts[i]
    xs[pad - 8:pad, :] = jnp.zeros((8, width), F32)
    xs[0:seq, :] = x_ref[0].astype(F32)
    attn = nn(o_ref[0], w_ref[...]) + bias_ref[...]
    x1 = xs[...] + depth[i, 0] * attn
    x1_ref[0] = x1
    sums_ref[0, 0:1, :] = col_sum(jnp.where(ok, x1 * x1, 0.0))
    sums_ref[0, 1:2, :] = col_sum(jnp.where(ok, attn * attn, 0.0))
    sums_ref[0, 2:8, :] = jnp.zeros((6, width), F32)
    normed, _ = normalize(x1)
    a2_ref[0] = (normed * gain_ref[...] + shift_ref[...]).astype(BF16)


def middle(counts, depth, o, images, w, bias, gain, shift, pad):
    n, seq, width = images.shape
    grid_spec = pltpu.PrefetchScalarGridSpec(
        num_scalar_prefetch=2,
        grid=(n,),
        in_specs=[
            by_image((pad, width)), by_image((seq, width)),
            whole(w.shape), whole(bias.shape), whole(gain.shape), whole(shift.shape),
        ],
        out_specs=[by_image((pad, width)), by_image((pad, width)), by_image((8, width))],
        scratch_shapes=[pltpu.VMEM((pad, width), F32)],
    )
    return pl.pallas_call(
        functools.partial(middle_kernel, seq, pad),
        out_shape=[
            jax.ShapeDtypeStruct((n, pad, width), F32),
            jax.ShapeDtypeStruct((n, pad, width), BF16),
            jax.ShapeDtypeStruct((n, 8, width), F32),
        ],
        grid_spec=grid_spec,
        compiler_params=params(24),
        cost_estimate=pl.CostEstimate(
            flops=2 * n * pad * width * width, bytes_accessed=10 * MIB, transcendentals=0),
        name="middle",
    )(counts, depth, o, images, w, bias, gain, shift)


def gelu_pair(u):
    size = jnp.abs(u)
    t = 1.0 / (1.0 + (0.3275911 * INV_ROOT_TWO) * size)
    bell = jnp.exp(-0.5 * (u * u))
    series = t * (0.5 * 0.254829592 + t * (0.5 * -0.284496736 + t * (
        0.5 * 1.421413741 + t * (0.5 * -1.453152027 + t * (0.5 * 1.061405429)))))
    tail = series * bell
    phi = jnp.where(u >= 0, 1.0 - tail, tail)
    return u * phi, phi + u * (bell * INV_ROOT_TWO_PI)


def feed_kernel(seq, pad, counts, depth, a2_ref, gm_ref, up_ref, down_ref, bu_ref, x1_ref, cot_ref,
                bd_ref, gain_ref,
                dup_ref, ddown_ref, gbu_ref, y_ref, gx_ref, ga_ref, vec_ref,
                a2t, gmt, mlp, ga2, hs, gus, cs):
    j = pl.program_id(0)
    n = x1_ref.shape[0]

    @pl.when(j == 0)
    def _():
        a2t[...] = jnp.transpose(a2_ref[...])
        gmt[...] = jnp.transpose(gm_ref[...])
        mlp[...] = jnp.zeros_like(mlp)
        ga2[...] = jnp.zeros_like(ga2)

    gbu = jnp.zeros(bu_ref.shape[1:], F32)
    for i in range(n):
        at = slice(i * pad, (i + 1) * pad)
        u = nt(a2_ref[at, :], up_ref[...]) + bu_ref[0]
        t = nt(gm_ref[at, :], down_ref[...])
        act, slope = gelu_pair(u)
        h = act.astype(BF16)
        gu = (t * slope).astype(BF16)
        hs[at, :] = h
        gus[at, :] = gu
        gbu = gbu + col_sum(gu.astype(F32))
        mlp[at, :] += nn(h, down_ref[...])
        ga2[at, :] += nn(gu, up_ref[...])
    gbu_ref[0] = gbu
    dup_ref[0] = nn(a2t[...], gus[...]).astype(BF16)
    ddown_ref[0] = nn(gmt[...], hs[...]).astype(BF16)

    @pl.when(j == pl.num_programs(0) - 1)
    def _():
        width = x1_ref.shape[-1]
        rows = lax.broadcasted_iota(jnp.int32, (pad, 1), 0)
        cs[pad - 8:pad, :] = jnp.zeros((8, width), F32)
        msum = jnp.zeros((1, width), F32)
        ggain = jnp.zeros((1, width), F32)
        gshift = jnp.zeros((1, width), F32)
        gdown = jnp.zeros((1, width), F32)
        gout = jnp.zeros((1, width), F32)
        for i in range(n):
            at = slice(i * pad, (i + 1) * pad)
            ok = rows < counts[i]
            x1 = x1_ref[i]
            out = mlp[at, :] + bd_ref[...]
            msum = msum + col_sum(jnp.where(ok, out * out, 0.0))
            y_ref[i] = jnp.where(ok, x1 + depth[i, 1] * out, 0.0).astype(BF16)[0:seq]
            cs[0:seq, :] = cot_ref[i].astype(F32)
            g = jnp.where(ok, cs[...], 0.0)
            gdown = gdown + col_sum(gm_ref[at, :].astype(F32))
            back = ga2[at, :]
            normed, rstd = normalize(x1)
            ggain = ggain + col_sum(back * normed)
            gshift = gshift + col_sum(back)
            e = back * gain_ref[...]
            gx = g + rstd * (e - mean_row(e) - normed * mean_row(e * normed))
            gx_ref[i] = gx
            ga = (depth[i, 0] * gx).astype(BF16)
            ga_ref[i] = ga
            gout = gout + col_sum(ga.astype(F32))
        vec_ref[0:1, :] = ggain
        vec_ref[1:2, :] = gshift
        vec_ref[2:3, :] = gdown
        vec_ref[3:4, :] = gout
        vec_ref[4:5, :] = msum
        vec_ref[5:8, :] = jnp.zeros((3, width), F32)


def feed(counts, depth, a2, gm, up, down, bu, x1, cot, bd, gain, seq, pad, block):
    rows, width = a2.shape
    n = rows // pad
    hidden = up.shape[0]
    steps = hidden // block
    at = lambda j, *_: (j, 0)
    at3 = lambda j, *_: (j, 0, 0)
    grid_spec = pltpu.PrefetchScalarGridSpec(
        num_scalar_prefetch=2,
        grid=(steps,),
        in_specs=[
            whole(a2.shape), whole(gm.shape),
            pl.BlockSpec((block, width), at), pl.BlockSpec((block, width), at),
            pl.BlockSpec((1, 1, block), at3),
            whole(x1.shape), whole(cot.shape), whole(bd.shape), whole(gain.shape),
        ],
        out_specs=[
            pl.BlockSpec((1, width, block), at3), pl.BlockSpec((1, width, block), at3),
            pl.BlockSpec((1, 1, block), at3),
            whole((n, seq, width)), whole((n, pad, width)), whole((n, pad, width)), whole((8, width)),
        ],
        scratch_shapes=[
            pltpu.VMEM((width, rows), BF16), pltpu.VMEM((width, rows), BF16),
            pltpu.VMEM((rows, width), F32), pltpu.VMEM((rows, width), F32),
            pltpu.VMEM((rows, block), BF16), pltpu.VMEM((rows, block), BF16),
            pltpu.VMEM((pad, width), F32),
        ],
    )
    return pl.pallas_call(
        functools.partial(feed_kernel, seq, pad),
        out_shape=[
            jax.ShapeDtypeStruct((steps, width, block), BF16),
            jax.ShapeDtypeStruct((steps, width, block), BF16),
            jax.ShapeDtypeStruct((steps, 1, block), F32),
            jax.ShapeDtypeStruct((n, seq, width), BF16),
            jax.ShapeDtypeStruct((n, pad, width), F32),
            jax.ShapeDtypeStruct((n, pad, width), BF16),
            jax.ShapeDtypeStruct((8, width), F32),
        ],
        grid_spec=grid_spec,
        compiler_params=params(60),
        cost_estimate=pl.CostEstimate(
            flops=12 * rows * width * hidden, bytes_accessed=40 * MIB, transcendentals=rows * hidden),
        name="feed",
    )(counts, depth, a2, gm, up, down, bu.reshape(steps, 1, block), x1, cot, bd, gain)


def back_kernel(pad, counts, ga_ref, w_ref, qkv_ref, lse_ref, g_ref, go):
    i = pl.program_id(0)
    width = ga_ref.shape[-1]
    count = counts[i]
    go[...] = nt(ga_ref[0], w_ref[...]).astype(BF16)
    ok = lax.broadcasted_iota(jnp.int32, (pad, pad), 0) < count
    lane = lax.broadcasted_iota(jnp.int32, (pad, 128), 1)

    def pair(p):
        at = pl.multiple_of(p * 128, 128)
        q = qkv_ref[0, :, pl.ds(at, 128)] * 0.125
        k = qkv_ref[0, :, pl.ds(width + at, 128)]
        v = qkv_ref[0, :, pl.ds(2 * width + at, 128)]
        g = go[:, pl.ds(at, 128)]
        gq = jnp.zeros((pad, 128), F32)
        gk = jnp.zeros((pad, 128), F32)
        gv = jnp.zeros((pad, 128), F32)
        for half in range(2):
            mine = (lane >= 64) if half else (lane < 64)
            qm = jnp.where(mine, q, 0)
            km = jnp.where(mine, k, 0) * 0.125
            gmine = jnp.where(mine, g, 0)
            scores = nt(k, qm)
            row = lse_ref[0, 2 * p + half:2 * p + half + 1, :]
            prob = jnp.where(ok, jnp.exp(scores - row), 0.0)
            dp = nt(v, gmine)
            inner = col_sum(prob * dp)
            ds = (prob * (dp - inner)).astype(BF16)
            gv = gv + nn(prob.astype(BF16), gmine)
            gk = gk + nn(ds, qm)
            gq = gq + tn(ds, km)
        g_ref[0, :, pl.ds(at, 128)] = gq.astype(BF16)
        g_ref[0, :, pl.ds(width + at, 128)] = gk.astype(BF16)
        g_ref[0, :, pl.ds(2 * width + at, 128)] = gv.astype(BF16)

    for p in range(width // 128):
        pair(p)


def back(counts, ga, w, qkv, lse):
    n, pad, width = ga.shape
    grid_spec = pltpu.PrefetchScalarGridSpec(
        num_scalar_prefetch=1,
        grid=(n,),
        in_specs=[by_image((pad, width)), whole(w.shape), by_image((pad, 3 * width)), by_image((16, pad))],
        out_specs=[by_image((pad, 3 * width))],
        scratch_shapes=[pltpu.VMEM((pad, width), BF16)],
    )
    return pl.pallas_call(
        functools.partial(back_kernel, pad),
        out_shape=[jax.ShapeDtypeStruct((n, pad, 3 * width), BF16)],
        grid_spec=grid_spec,
        compiler_params=params(40),
        cost_estimate=pl.CostEstimate(
            flops=2 * n * pad * width * (width + 10 * pad), bytes_accessed=16 * MIB,
            transcendentals=n * 12 * pad * pad),
        name="back",
    )(counts, ga, w, qkv, lse)[0]


def outgrad_kernel(o_ref, ga_ref, d_ref):
    d_ref[...] = tn(o_ref[...], ga_ref[...]).astype(BF16)


def outgrad(o, ga):
    rows, width = o.shape
    return pl.pallas_call(
        outgrad_kernel,
        out_shape=jax.ShapeDtypeStruct((width, width), BF16),
        grid=(2,),
        in_specs=[pl.BlockSpec((rows, width // 2), lambda j: (0, j)), whole(ga.shape)],
        out_specs=pl.BlockSpec((width // 2, width), lambda j: (j, 0)),
        compiler_params=params(32),
        cost_estimate=pl.CostEstimate(
            flops=2 * rows * width * width, bytes_accessed=6 * MIB, transcendentals=0),
        name="outgrad",
    )(o, ga)


def last_kernel(seq, pad, g_ref, a1_ref, w_ref, x_ref, gx_ref, gain_ref,
                d_ref, cols_ref, gi_ref, vec_ref, ga1, xs):
    c = pl.program_id(0)
    n = x_ref.shape[0]
    g = g_ref[...]
    d_ref[...] = tn(g, a1_ref[...]).astype(BF16)
    cols_ref[...] = col_sum(g.astype(F32))
    part = nn(g, w_ref[...])

    @pl.when(c == 0)
    def _():
        ga1[...] = part

    @pl.when(c > 0)
    def _():
        ga1[...] += part

    @pl.when(c == pl.num_programs(0) - 1)
    def _():
        width = x_ref.shape[-1]
        xs[pad - 8:pad, :] = jnp.zeros((8, width), F32)
        ggain = jnp.zeros((1, width), F32)
        gshift = jnp.zeros((1, width), F32)
        for i in range(n):
            xs[0:seq, :] = x_ref[i].astype(F32)
            normed, rstd = normalize(xs[...])
            grad = ga1[i * pad:(i + 1) * pad, :]
            ggain = ggain + col_sum(grad * normed)
            gshift = gshift + col_sum(grad)
            e = grad * gain_ref[...]
            gi = gx_ref[i] + rstd * (e - mean_row(e) - normed * mean_row(e * normed))
            gi_ref[i] = gi[0:seq]
        vec_ref[0:1, :] = ggain
        vec_ref[1:2, :] = gshift
        vec_ref[2:8, :] = jnp.zeros((6, width), F32)


def last(g, a1, w, images, gx, gain, pad, block=384):
    n, seq, width = images.shape
    rows, total = g.shape
    return pl.pallas_call(
        functools.partial(last_kernel, seq, pad),
        out_shape=[
            jax.ShapeDtypeStruct((total, width), BF16),
            jax.ShapeDtypeStruct((1, total), F32),
            jax.ShapeDtypeStruct((n, seq, width), F32),
            jax.ShapeDtypeStruct((8, width), F32),
        ],
        grid=(total // block,),
        in_specs=[
            pl.BlockSpec((rows, block), lambda c: (0, c)), whole(a1.shape),
            pl.BlockSpec((block, width), lambda c: (c, 0)), whole(images.shape), whole(gx.shape),
            whole(gain.shape),
        ],
        out_specs=[
            pl.BlockSpec((block, width), lambda c: (c, 0)), pl.BlockSpec((1, block), lambda c: (0, c)),
            whole((n, seq, width)), whole((8, width)),
        ],
        scratch_shapes=[pltpu.VMEM((rows, width), F32), pltpu.VMEM((pad, width), F32)],
        compiler_params=params(50),
        cost_estimate=pl.CostEstimate(
            flops=4 * rows * width * total, bytes_accessed=30 * MIB, transcendentals=0),
        name="last",
    )(g, a1, w, images, gx, gain)


def shards(
    images, grid_sizes, keep_flags, attn_gain, attn_shift, attend_weight, query_bias, value_bias,
    output_weight, output_bias, mlp_gain, mlp_shift, up_weight, up_bias, down_weight, down_bias,
    cotangent,
):
    n, seq, width = images.shape
    pad = -(-seq // 32) * 32
    counts = grid_sizes[:, 0] * grid_sizes[:, 1] + 2
    depth = keep_flags.astype(F32) / KEEP_PROB
    owners = width // attn_gain.shape[0]

    small = jnp.concatenate([
        attn_gain, attn_shift, query_bias, value_bias, output_bias, mlp_gain, mlp_shift, down_bias, up_bias])
    small = lax.all_gather(small.reshape(1, -1), "fsdp", axis=0, tiled=True).astype(F32)
    share = attn_gain.shape[0]
    vec = [small[:, k * share:(k + 1) * share].reshape(1, width) for k in range(8)]
    bu = small[:, 8 * share:].reshape(1, -1)
    gain_one, shift_one, bias_q, bias_v, bias_o, gain_two, shift_two, bias_d = vec
    bias = jnp.concatenate([bias_q, jnp.zeros_like(bias_q), bias_v], 1)

    attend = lax.all_gather(attend_weight.T, "fsdp", axis=0, tiled=True)
    out_w = lax.all_gather(output_weight, "fsdp", axis=0, tiled=True)
    up = lax.all_gather(up_weight.T, "fsdp", axis=0, tiled=True)
    down = lax.all_gather(down_weight, "fsdp", axis=0, tiled=True)

    a1, gm, qkv, o, lse = front(counts, depth, images, cotangent, attend, gain_one, shift_one, bias, pad)
    x1, a2, sums_two = middle(counts, depth, o, images, out_w, bias_o, gain_two, shift_two, pad)
    flat = lambda array: array.reshape(n * pad, array.shape[-1])
    block = up_weight.shape[1] if up_weight.shape[1] % 128 == 0 else 384
    dup, ddown, gbu, y, gx, ga, vec_feed = feed(
        counts, depth, flat(a2), flat(gm), up, down, bu, x1, cotangent, bias_d, gain_two, seq, pad, block)
    dout = outgrad(flat(o), flat(ga))
    g = back(counts, ga, out_w, qkv, lse)
    dattend, cols, gi, vec_last = last(flat(g), flat(a1), attend, images, gx, gain_one, pad)

    sums = jnp.stack([jnp.sum(sums_two[:, 0]), jnp.sum(sums_two[:, 1]), jnp.sum(vec_feed[4]),
                      jnp.sum(counts).astype(F32)])

    def spread(array):
        return lax.psum(lax.psum_scatter(array, "fsdp", scatter_dimension=0, tiled=True), "dp")

    def columns(array):
        hidden = up.shape[0]
        array = jnp.swapaxes(array, 0, 1).reshape(width, owners, hidden // owners)
        return jnp.swapaxes(array, 0, 1)

    gup = spread(columns(dup))[0]
    gdown = spread(columns(ddown))[0].T
    gout = spread(dout)
    gattend = spread(dattend).T
    rows = jnp.concatenate([
        vec_last[0:2], cols[:, :width], cols[:, 2 * width:], vec_feed[3:4], vec_feed[0:3],
    ], 0)
    tiny = jnp.concatenate([
        jnp.swapaxes(rows.reshape(8, owners, share), 0, 1).reshape(owners, 8 * share),
        gbu.reshape(owners, -1)], 1)
    tiny = spread(tiny)[0]
    sums = lax.psum(sums, ("dp", "fsdp"))
    root_means = jnp.sqrt(sums[:3] / (sums[3] * width))
    tv = [tiny[k * share:(k + 1) * share] for k in range(8)]
    f = lambda array: array.astype(F32)
    return (y, gi, tv[0], tv[1], f(gattend), tv[2], tv[3], f(gout), tv[4], tv[5], tv[6],
            f(gup), tiny[8 * share:], f(gdown), tv[7], root_means)


def solution(mesh):
    images = P(("dp", "fsdp"), None, None)
    flags = P(("dp", "fsdp"), None)
    vec, rows, cols = P("fsdp"), P("fsdp", None), P(None, "fsdp")
    return jax.shard_map(
        shards,
        mesh=mesh,
        in_specs=(images, flags, flags, vec, vec, cols, vec, vec, rows, vec, vec, vec, cols, vec, rows,
                  vec, images),
        out_specs=(images, images, vec, vec, cols, vec, vec, rows, vec, vec, vec, cols, vec, rows, vec,
                   P()),
        check_vma=False,
    )
```

```python
import functools
import math

import jax
import jax.numpy as jnp
from jax import lax
from jax.experimental import pallas as pl
from jax.experimental.pallas import tpu as pltpu
from jax.sharding import PartitionSpec as P

HEAD_DIM = 64
EPS = 1e-06
KEEP_PROB = 0.9
MASKED = -1e30
INV_ROOT_TWO = 0.7071067811865476
INV_ROOT_TWO_PI = 0.3989422804014327
F32 = jnp.float32
BF16 = jnp.bfloat16
MIB = 1024 * 1024


def nn(left, right):
    return lax.dot_general(left, right, (((1,), (0,)), ((), ())), preferred_element_type=F32)


def nt(left, right):
    return lax.dot_general(left, right, (((1,), (1,)), ((), ())), preferred_element_type=F32)


def tn(left, right):
    return lax.dot_general(left, right, (((0,), (0,)), ((), ())), preferred_element_type=F32)


def mean_row(values):
    return jnp.sum(values, -1, keepdims=True) * (1.0 / values.shape[-1])


def normalize(values):
    center = values - mean_row(values)
    rstd = lax.rsqrt(mean_row(center * center) + EPS)
    return center * rstd, rstd


def col_sum(values):
    return jnp.sum(values, 0, keepdims=True)


def params(limit, steps=1):
    return pltpu.CompilerParams(
        dimension_semantics=("arbitrary",) * steps, vmem_limit_bytes=limit * MIB
    )


def whole(shape, buffers=1):
    zeros = (0,) * len(shape)
    return pl.BlockSpec(shape, lambda *_: zeros, pipeline_mode=pl.Buffered(buffers))


def by_image(shape):
    rest = (0,) * len(shape)
    return pl.BlockSpec((1,) + shape, lambda i, *_: (i,) + rest)


SMEM = pl.BlockSpec(memory_space=pltpu.SMEM)


def front_kernel(seq, pad, counts, depth, x_ref, cot_ref, w_ref, vec_ref,
                 a1_ref, gm_ref, qkv_ref, o_ref, lse_ref, xs, lse_s):
    i = pl.program_id(0)
    width = x_ref.shape[-1]
    pairs = width // 128
    count = counts[i]
    rows = lax.broadcasted_iota(jnp.int32, (pad, 1), 0)
    xs[pad - 8:pad, :] = jnp.zeros((8, width), F32)
    xs[0:seq, :] = cot_ref[0].astype(F32)
    gm_ref[0] = jnp.where(rows < count, xs[...] * depth[i, 1], 0.0).astype(BF16)
    xs[0:seq, :] = x_ref[0].astype(F32)
    normed, _ = normalize(xs[...])
    a1 = (normed * vec_ref[0:1, :] + vec_ref[1:2, :]).astype(BF16)
    a1_ref[0] = a1
    for c in range(0, 3 * width, 384):
        part = nt(a1, w_ref[c:c + 384, :])
        if c < width:
            part = part + vec_ref[2:3, c:c + 384]
        elif c >= 2 * width:
            part = part + vec_ref[3:4, c - 2 * width:c - 2 * width + 384]
        qkv_ref[0, :, c:c + 384] = part.astype(BF16)
    ok = lax.broadcasted_iota(jnp.int32, (pad, pad), 1) < count
    lane = lax.broadcasted_iota(jnp.int32, (pad, 128), 1)
    lse_s[...] = jnp.zeros((pad, 128), F32)

    def pair(p):
        at = pl.multiple_of(p * 128, 128)
        q = qkv_ref[0, :, pl.ds(at, 128)] * 0.125
        k = qkv_ref[0, :, pl.ds(width + at, 128)]
        v = qkv_ref[0, :, pl.ds(2 * width + at, 128)]
        total = jnp.zeros((pad, 128), F32)
        for half in range(2):
            mine = (lane >= 64) if half else (lane < 64)
            scores = jnp.where(ok, nt(jnp.where(mine, q, 0), k), MASKED)
            top = jnp.max(scores, -1, keepdims=True)
            e = jnp.exp(scores - top)
            s = jnp.sum(e, -1, keepdims=True)
            prob = (e * (1.0 / s)).astype(BF16)
            total = total + nn(prob, jnp.where(mine, v, 0))
            lse_s[...] = jnp.where(lane == 2 * p + half, top + jnp.log(s), lse_s[...])
        o_ref[0, :, pl.ds(at, 128)] = total.astype(BF16)

    for p in range(pairs):
        pair(p)
    lse_ref[0] = jnp.transpose(lse_s[...])[0:16, :]


def front(counts, depth, images, cot, w, vec, pad):
    n, seq, width = images.shape
    grid_spec = pltpu.PrefetchScalarGridSpec(
        num_scalar_prefetch=2,
        grid=(n,),
        in_specs=[
            by_image((seq, width)), by_image((seq, width)),
            whole(w.shape), whole(vec.shape),
        ],
        out_specs=[
            by_image((pad, width)), by_image((pad, width)), by_image((pad, 3 * width)),
            by_image((pad, width)), by_image((16, pad)),
        ],
        scratch_shapes=[pltpu.VMEM((pad, width), F32), pltpu.VMEM((pad, 128), F32)],
    )
    return pl.pallas_call(
        functools.partial(front_kernel, seq, pad),
        out_shape=[
            jax.ShapeDtypeStruct((n, pad, width), BF16),
            jax.ShapeDtypeStruct((n, pad, width), BF16),
            jax.ShapeDtypeStruct((n, pad, 3 * width), BF16),
            jax.ShapeDtypeStruct((n, pad, width), BF16),
            jax.ShapeDtypeStruct((n, 16, pad), F32),
        ],
        grid_spec=grid_spec,
        compiler_params=params(60),
        cost_estimate=pl.CostEstimate(
            flops=2 * n * pad * width * (3 * width + 4 * pad), bytes_accessed=20 * MIB,
            transcendentals=n * 12 * pad * pad),
        name="front",
    )(counts, depth, images, cot, w, vec)


def middle_kernel(seq, pad, counts, depth, o_ref, x_ref, w_ref, vec_ref,
                  x1_ref, a2_ref, sums_ref, xs):
    i = pl.program_id(0)
    width = x_ref.shape[-1]
    rows = lax.broadcasted_iota(jnp.int32, (pad, 1), 0)
    ok = rows < counts[i]
    xs[pad - 8:pad, :] = jnp.zeros((8, width), F32)
    xs[0:seq, :] = x_ref[0].astype(F32)
    attn = nn(o_ref[0], w_ref[...]) + vec_ref[4:5, :]
    x1 = xs[...] + depth[i, 0] * attn
    x1_ref[0] = x1
    sums_ref[0, 0:1, :] = col_sum(jnp.where(ok, x1 * x1, 0.0))
    sums_ref[0, 1:2, :] = col_sum(jnp.where(ok, attn * attn, 0.0))
    sums_ref[0, 2:8, :] = jnp.zeros((6, width), F32)
    normed, _ = normalize(x1)
    a2_ref[0] = (normed * vec_ref[5:6, :] + vec_ref[6:7, :]).astype(BF16)


def middle(counts, depth, o, images, w, vec, pad):
    n, seq, width = images.shape
    grid_spec = pltpu.PrefetchScalarGridSpec(
        num_scalar_prefetch=2,
        grid=(n,),
        in_specs=[
            by_image((pad, width)), by_image((seq, width)),
            whole(w.shape), whole(vec.shape),
        ],
        out_specs=[by_image((pad, width)), by_image((pad, width)), by_image((8, width))],
        scratch_shapes=[pltpu.VMEM((pad, width), F32)],
    )
    return pl.pallas_call(
        functools.partial(middle_kernel, seq, pad),
        out_shape=[
            jax.ShapeDtypeStruct((n, pad, width), F32),
            jax.ShapeDtypeStruct((n, pad, width), BF16),
            jax.ShapeDtypeStruct((n, 8, width), F32),
        ],
        grid_spec=grid_spec,
        compiler_params=params(60),
        cost_estimate=pl.CostEstimate(
            flops=2 * n * pad * width * width, bytes_accessed=10 * MIB, transcendentals=0),
        name="middle",
    )(counts, depth, o, images, w, vec)


def gelu_pair(u):
    size = jnp.abs(u)
    t = 1.0 / (1.0 + (0.3275911 * INV_ROOT_TWO) * size)
    bell = jnp.exp(-0.5 * (u * u))
    series = t * (0.5 * 0.254829592 + t * (0.5 * -0.284496736 + t * (
        0.5 * 1.421413741 + t * (0.5 * -1.453152027 + t * (0.5 * 1.061405429)))))
    tail = series * bell
    phi = jnp.where(u >= 0, 1.0 - tail, tail)
    return u * phi, phi + u * (bell * INV_ROOT_TWO_PI)


def feed_kernel(seq, pad, counts, depth, a2_ref, gm_ref, up_ref, down_ref, bu_ref, x1_ref, cot_ref,
                vecs,
                dup_ref, ddown_ref, gbu_ref, y_ref, gx_ref, ga_ref, vec_ref,
                a2t, gmt, mlp, ga2, hs, gus, cs):
    j = pl.program_id(0)
    n = x1_ref.shape[0]

    @pl.when(j == 0)
    def _():
        a2t[...] = jnp.transpose(a2_ref[...])
        gmt[...] = jnp.transpose(gm_ref[...])
        mlp[...] = jnp.zeros_like(mlp)
        ga2[...] = jnp.zeros_like(ga2)

    gbu = jnp.zeros(bu_ref.shape[1:], F32)
    for i in range(n):
        at = slice(i * pad, (i + 1) * pad)
        u = nt(a2_ref[at, :], up_ref[...]) + bu_ref[0]
        t = nt(gm_ref[at, :], down_ref[...])
        act, slope = gelu_pair(u)
        h = act.astype(BF16)
        gu = (t * slope).astype(BF16)
        hs[at, :] = h
        gus[at, :] = gu
        gbu = gbu + col_sum(gu.astype(F32))
        mlp[at, :] += nn(h, down_ref[...])
        ga2[at, :] += nn(gu, up_ref[...])
    gbu_ref[0] = gbu
    dup_ref[0] = nn(a2t[...], gus[...]).astype(BF16)
    ddown_ref[0] = nn(gmt[...], hs[...]).astype(BF16)

    @pl.when(j == pl.num_programs(0) - 1)
    def _():
        width = x1_ref.shape[-1]
        rows = lax.broadcasted_iota(jnp.int32, (pad, 1), 0)
        cs[pad - 8:pad, :] = jnp.zeros((8, width), F32)
        msum = jnp.zeros((1, width), F32)
        ggain = jnp.zeros((1, width), F32)
        gshift = jnp.zeros((1, width), F32)
        gdown = jnp.zeros((1, width), F32)
        gout = jnp.zeros((1, width), F32)
        for i in range(n):
            at = slice(i * pad, (i + 1) * pad)
            ok = rows < counts[i]
            x1 = x1_ref[i]
            out = mlp[at, :] + vecs[7:8, :]
            msum = msum + col_sum(jnp.where(ok, out * out, 0.0))
            y_ref[i] = jnp.where(ok, x1 + depth[i, 1] * out, 0.0).astype(BF16)[0:seq]
            cs[0:seq, :] = cot_ref[i].astype(F32)
            g = jnp.where(ok, cs[...], 0.0)
            gdown = gdown + col_sum(gm_ref[at, :].astype(F32))
            back = ga2[at, :]
            normed, rstd = normalize(x1)
            ggain = ggain + col_sum(back * normed)
            gshift = gshift + col_sum(back)
            e = back * vecs[5:6, :]
            gx = g + rstd * (e - mean_row(e) - normed * mean_row(e * normed))
            gx_ref[i] = gx
            ga = (depth[i, 0] * gx).astype(BF16)
            ga_ref[i] = ga
            gout = gout + col_sum(ga.astype(F32))
        vec_ref[0:1, :] = ggain
        vec_ref[1:2, :] = gshift
        vec_ref[2:3, :] = gdown
        vec_ref[3:4, :] = gout
        vec_ref[4:5, :] = msum
        vec_ref[5:8, :] = jnp.zeros((3, width), F32)


def feed(counts, depth, a2, gm, up, down, bu, x1, cot, vec, seq, pad, block):
    rows, width = a2.shape
    n = rows // pad
    hidden = up.shape[0]
    steps = hidden // block
    at = lambda j, *_: (j, 0)
    at3 = lambda j, *_: (j, 0, 0)
    grid_spec = pltpu.PrefetchScalarGridSpec(
        num_scalar_prefetch=2,
        grid=(steps,),
        in_specs=[
            whole(a2.shape), whole(gm.shape),
            pl.BlockSpec((block, width), at), pl.BlockSpec((block, width), at),
            pl.BlockSpec((1, 1, block), at3),
            whole(x1.shape), whole(cot.shape), whole(vec.shape),
        ],
        out_specs=[
            pl.BlockSpec((1, width, block), at3), pl.BlockSpec((1, width, block), at3),
            pl.BlockSpec((1, 1, block), at3),
            whole((n, seq, width)), whole((n, pad, width)), whole((n, pad, width)), whole((8, width)),
        ],
        scratch_shapes=[
            pltpu.VMEM((width, rows), BF16), pltpu.VMEM((width, rows), BF16),
            pltpu.VMEM((rows, width), F32), pltpu.VMEM((rows, width), F32),
            pltpu.VMEM((rows, block), BF16), pltpu.VMEM((rows, block), BF16),
            pltpu.VMEM((pad, width), F32),
        ],
    )
    return pl.pallas_call(
        functools.partial(feed_kernel, seq, pad),
        out_shape=[
            jax.ShapeDtypeStruct((steps, width, block), BF16),
            jax.ShapeDtypeStruct((steps, width, block), BF16),
            jax.ShapeDtypeStruct((steps, 1, block), F32),
            jax.ShapeDtypeStruct((n, seq, width), BF16),
            jax.ShapeDtypeStruct((n, pad, width), F32),
            jax.ShapeDtypeStruct((n, pad, width), BF16),
            jax.ShapeDtypeStruct((8, width), F32),
        ],
        grid_spec=grid_spec,
        compiler_params=params(60),
        cost_estimate=pl.CostEstimate(
            flops=12 * rows * width * hidden, bytes_accessed=40 * MIB, transcendentals=rows * hidden),
        name="feed",
    )(counts, depth, a2, gm, up, down, bu.reshape(steps, 1, block), x1, cot, vec)


def back_kernel(pad, counts, ga_ref, w_ref, qkv_ref, lse_ref, g_ref, go):
    i = pl.program_id(0)
    width = ga_ref.shape[-1]
    count = counts[i]
    go[...] = nt(ga_ref[0], w_ref[...]).astype(BF16)
    ok = lax.broadcasted_iota(jnp.int32, (pad, pad), 0) < count
    lane = lax.broadcasted_iota(jnp.int32, (pad, 128), 1)

    def pair(p):
        at = pl.multiple_of(p * 128, 128)
        q = qkv_ref[0, :, pl.ds(at, 128)] * 0.125
        k = qkv_ref[0, :, pl.ds(width + at, 128)]
        v = qkv_ref[0, :, pl.ds(2 * width + at, 128)]
        g = go[:, pl.ds(at, 128)]
        gq = jnp.zeros((pad, 128), F32)
        gk = jnp.zeros((pad, 128), F32)
        gv = jnp.zeros((pad, 128), F32)
        for half in range(2):
            mine = (lane >= 64) if half else (lane < 64)
            qm = jnp.where(mine, q, 0)
            km = jnp.where(mine, k, 0) * 0.125
            gmine = jnp.where(mine, g, 0)
            scores = nt(k, qm)
            row = lse_ref[0, 2 * p + half:2 * p + half + 1, :]
            prob = jnp.where(ok, jnp.exp(scores - row), 0.0)
            dp = nt(v, gmine)
            inner = col_sum(prob * dp)
            ds = (prob * (dp - inner)).astype(BF16)
            gv = gv + nn(prob.astype(BF16), gmine)
            gk = gk + nn(ds, qm)
            gq = gq + tn(ds, km)
        g_ref[0, :, pl.ds(at, 128)] = gq.astype(BF16)
        g_ref[0, :, pl.ds(width + at, 128)] = gk.astype(BF16)
        g_ref[0, :, pl.ds(2 * width + at, 128)] = gv.astype(BF16)

    for p in range(width // 128):
        pair(p)


def back(counts, ga, w, qkv, lse):
    n, pad, width = ga.shape
    grid_spec = pltpu.PrefetchScalarGridSpec(
        num_scalar_prefetch=1,
        grid=(n,),
        in_specs=[by_image((pad, width)), whole(w.shape), by_image((pad, 3 * width)), by_image((16, pad))],
        out_specs=[by_image((pad, 3 * width))],
        scratch_shapes=[pltpu.VMEM((pad, width), BF16)],
    )
    return pl.pallas_call(
        functools.partial(back_kernel, pad),
        out_shape=[jax.ShapeDtypeStruct((n, pad, 3 * width), BF16)],
        grid_spec=grid_spec,
        compiler_params=params(60),
        cost_estimate=pl.CostEstimate(
            flops=2 * n * pad * width * (width + 10 * pad), bytes_accessed=16 * MIB,
            transcendentals=n * 12 * pad * pad),
        name="back",
    )(counts, ga, w, qkv, lse)[0]


def outgrad_kernel(o_ref, ga_ref, d_ref):
    d_ref[...] = tn(o_ref[...], ga_ref[...]).astype(BF16)


def outgrad(o, ga):
    rows, width = o.shape
    return pl.pallas_call(
        outgrad_kernel,
        out_shape=jax.ShapeDtypeStruct((width, width), BF16),
        grid=(2,),
        in_specs=[pl.BlockSpec((rows, width // 2), lambda j: (0, j)), whole(ga.shape)],
        out_specs=pl.BlockSpec((width // 2, width), lambda j: (j, 0)),
        compiler_params=params(60),
        cost_estimate=pl.CostEstimate(
            flops=2 * rows * width * width, bytes_accessed=6 * MIB, transcendentals=0),
        name="outgrad",
    )(o, ga)


def last_kernel(seq, pad, g_ref, a1_ref, w_ref, x_ref, gx_ref, vecs,
                d_ref, cols_ref, gi_ref, vec_ref, ga1, xs):
    c = pl.program_id(0)
    n = x_ref.shape[0]
    g = g_ref[...]
    d_ref[...] = tn(g, a1_ref[...]).astype(BF16)
    cols_ref[...] = col_sum(g.astype(F32))
    part = nn(g, w_ref[...])

    @pl.when(c == 0)
    def _():
        ga1[...] = part

    @pl.when(c > 0)
    def _():
        ga1[...] += part

    @pl.when(c == pl.num_programs(0) - 1)
    def _():
        width = x_ref.shape[-1]
        xs[pad - 8:pad, :] = jnp.zeros((8, width), F32)
        ggain = jnp.zeros((1, width), F32)
        gshift = jnp.zeros((1, width), F32)
        for i in range(n):
            xs[0:seq, :] = x_ref[i].astype(F32)
            normed, rstd = normalize(xs[...])
            grad = ga1[i * pad:(i + 1) * pad, :]
            ggain = ggain + col_sum(grad * normed)
            gshift = gshift + col_sum(grad)
            e = grad * vecs[0:1, :]
            gi = gx_ref[i] + rstd * (e - mean_row(e) - normed * mean_row(e * normed))
            gi_ref[i] = gi[0:seq]
        vec_ref[0:1, :] = ggain
        vec_ref[1:2, :] = gshift
        vec_ref[2:8, :] = jnp.zeros((6, width), F32)


def last(g, a1, w, images, gx, vec, pad, block=384):
    n, seq, width = images.shape
    rows, total = g.shape
    return pl.pallas_call(
        functools.partial(last_kernel, seq, pad),
        out_shape=[
            jax.ShapeDtypeStruct((total, width), BF16),
            jax.ShapeDtypeStruct((1, total), F32),
            jax.ShapeDtypeStruct((n, seq, width), F32),
            jax.ShapeDtypeStruct((8, width), F32),
        ],
        grid=(total // block,),
        in_specs=[
            pl.BlockSpec((rows, block), lambda c: (0, c)), whole(a1.shape),
            pl.BlockSpec((block, width), lambda c: (c, 0)), whole(images.shape), whole(gx.shape),
            whole(vec.shape),
        ],
        out_specs=[
            pl.BlockSpec((block, width), lambda c: (c, 0)), pl.BlockSpec((1, block), lambda c: (0, c)),
            whole((n, seq, width)), whole((8, width)),
        ],
        scratch_shapes=[pltpu.VMEM((rows, width), F32), pltpu.VMEM((pad, width), F32)],
        compiler_params=params(60),
        cost_estimate=pl.CostEstimate(
            flops=4 * rows * width * total, bytes_accessed=30 * MIB, transcendentals=0),
        name="last",
    )(g, a1, w, images, gx, vec)


def shards_any(
    images, grid_sizes, keep_flags, attn_gain, attn_shift, attend_weight, query_bias, value_bias,
    output_weight, output_bias, mlp_gain, mlp_shift, up_weight, up_bias, down_weight, down_bias,
    cotangent,
):
    n, seq, width = images.shape
    pad = -(-seq // 32) * 32
    counts = grid_sizes[:, 0] * grid_sizes[:, 1] + 2
    depth = keep_flags.astype(F32) / KEEP_PROB
    owners = width // attn_gain.shape[0]

    small = jnp.concatenate([
        attn_gain, attn_shift, query_bias, value_bias, output_bias, mlp_gain, mlp_shift, down_bias, up_bias])
    small = lax.all_gather(small.reshape(1, -1), "fsdp", axis=0, tiled=True).astype(F32)
    share = attn_gain.shape[0]
    vec = jnp.stack([small[:, k * share:(k + 1) * share].reshape(width) for k in range(8)])
    bu = small[:, 8 * share:].reshape(1, -1)

    attend = lax.all_gather(attend_weight.T, "fsdp", axis=0, tiled=True)
    out_w = lax.all_gather(output_weight, "fsdp", axis=0, tiled=True)
    up = lax.all_gather(up_weight.T, "fsdp", axis=0, tiled=True)
    down = lax.all_gather(down_weight, "fsdp", axis=0, tiled=True)

    a1, gm, qkv, o, lse = front(counts, depth, images, cotangent, attend, vec, pad)
    x1, a2, sums_two = middle(counts, depth, o, images, out_w, vec, pad)
    flat = lambda array: array.reshape(n * pad, array.shape[-1])
    block = up_weight.shape[1] if up_weight.shape[1] % 128 == 0 else 384
    dup, ddown, gbu, y, gx, ga, vec_feed = feed(
        counts, depth, flat(a2), flat(gm), up, down, bu, x1, cotangent, vec, seq, pad, block)
    dout = outgrad(flat(o), flat(ga))
    g = back(counts, ga, out_w, qkv, lse)
    dattend, cols, gi, vec_last = last(flat(g), flat(a1), attend, images, gx, vec, pad)

    sums = jnp.stack([jnp.sum(sums_two[:, 0]), jnp.sum(sums_two[:, 1]), jnp.sum(vec_feed[4]),
                      jnp.sum(counts).astype(F32)])

    def spread(array):
        return lax.psum(lax.psum_scatter(array, "fsdp", scatter_dimension=0, tiled=True), "dp")

    def columns(array):
        hidden = up.shape[0]
        array = jnp.swapaxes(array, 0, 1).reshape(width, owners, hidden // owners)
        return jnp.swapaxes(array, 0, 1)

    gup = spread(columns(dup))[0]
    gdown = spread(columns(ddown))[0].T
    gout = spread(dout)
    gattend = spread(dattend).T
    rows = jnp.concatenate([
        vec_last[0:2], cols[:, :width], cols[:, 2 * width:], vec_feed[3:4], vec_feed[0:3],
    ], 0)
    tiny = jnp.concatenate([
        jnp.swapaxes(rows.reshape(8, owners, share), 0, 1).reshape(owners, 8 * share),
        gbu.reshape(owners, -1)], 1)
    tiny = spread(tiny)[0]
    sums = lax.psum(sums, ("dp", "fsdp"))
    root_means = jnp.sqrt(sums[:3] / (sums[3] * width))
    tv = [tiny[k * share:(k + 1) * share] for k in range(8)]
    f = lambda array: array.astype(F32)
    return (y, gi, tv[0], tv[1], f(gattend), tv[2], tv[3], f(gout), tv[4], tv[5], tv[6],
            f(gup), tiny[8 * share:], f(gdown), tv[7], root_means)


def over_dp(array, m):
    return lax.ppermute(array, "dp", [(i, i ^ m) for i in range(4)])


def over_z(array, a):
    return lax.ppermute(array, "fsdp", [(i, i ^ (2 * a)) for i in range(8)])


def over_core(array):
    return lax.ppermute(array, "fsdp", [(i, i ^ 1) for i in range(8)])


def staged(kernel, ids, arrays, out_shape, name):
    size = sum(math.prod(s.shape) * s.dtype.itemsize for s in [*arrays, *out_shape])
    return pl.pallas_call(
        kernel,
        out_shape=out_shape,
        grid_spec=pltpu.PrefetchScalarGridSpec(
            num_scalar_prefetch=1, grid=(1,),
            in_specs=[whole(s.shape) for s in arrays],
            out_specs=[whole(s.shape) for s in out_shape]),
        compiler_params=params(60),
        cost_estimate=pl.CostEstimate(flops=0, bytes_accessed=size, transcendentals=0),
        name=name,
    )(ids, *arrays)


def simple(kernel, ids, arrays, out_shape, name, scratch=()):
    size = sum(math.prod(s.shape) * s.dtype.itemsize for s in [*arrays, *out_shape])
    inside = pl.BlockSpec(memory_space=pltpu.VMEM)
    return pl.pallas_call(
        kernel,
        out_shape=out_shape,
        in_specs=[SMEM] + [inside] * len(arrays),
        out_specs=[inside] * len(out_shape),
        scratch_shapes=list(scratch),
        compiler_params=pltpu.CompilerParams(vmem_limit_bytes=16 * MIB),
        cost_estimate=pl.CostEstimate(flops=0, bytes_accessed=size, transcendentals=0),
        name=name,
    )(ids, *arrays)


def pack_kernel(ids, at_ref, ow_ref, up_ref, down_ref, *refs):
    vectors, (own1, first1, own, first) = refs[:9], refs[9:]
    q = ids[0]
    att = jnp.transpose(at_ref[...])
    up = jnp.transpose(up_ref[...])
    r = ow_ref.shape[0]
    for t in range(4):
        own1[t ^ q] = att[t * r:(t + 1) * r] if t < 3 else ow_ref[...]
        at, to = 0, 0
        for k in (2 * r // 3, r // 3):
            own[t ^ q, to:to + k] = up[at + t * k:at + (t + 1) * k]
            own[t ^ q, to + k:to + 2 * k] = down_ref[at + t * k:at + (t + 1) * k, :]
            at, to = at + 4 * k, to + 2 * k
    first1[0:r, :] = own1[0]
    pieces = [v[...].reshape(1, -1).astype(F32) for v in vectors]
    blank = jnp.zeros((1, first1.shape[1] - r), F32)
    rows = [jnp.concatenate([p, blank], 1) for p in pieces[:8]]
    rows += [jnp.concatenate([pieces[8][:, k * r:(k + 1) * r], blank], 1) for k in range(4)]
    rows.append(jnp.zeros((4, first1.shape[1]), F32))
    first1[r:r + 16, :] = jnp.concatenate(rows, 0).astype(BF16)
    first[...] = own[0]


def pack(ids, at, ow, up, down, vectors):
    r, width = ow.shape
    s = lambda *shape: jax.ShapeDtypeStruct(shape, BF16)
    return staged(pack_kernel, ids, [at, ow, up, down, *vectors],
                  [s(4, r, width), s(r + 16, width), s(4, 2 * r, width), s(2 * r, width)],
                  "pack")


def after(value, *before):
    return lax.optimization_barrier((value, before))[0]


def line(ids, own, first, zr, xr):
    r, width = own.shape[1:]

    def kernel(ids, own, first, z1, z2, z3, x1, x2, x3, mine):
        zs, xs = (z1, z2, z3), (x1, x2, x3)
        for m in range(4):
            mine[m * r:(m + 1) * r] = own[m]
        mine[16 * r:16 * r + 16] = first[r:r + 16]
        for a in range(1, 4):
            at = 4 * a * r
            mine[at:at + r] = zs[a - 1][0:r]
            mine[16 * r + 16 * a:16 * r + 16 * a + 16] = zs[a - 1][r:r + 16]
            for m in range(1, 4):
                mine[at + m * r:at + (m + 1) * r] = xs[m - 1][a - 1]

    return simple(kernel, ids, [own, first, *zr, *xr], [jax.ShapeDtypeStruct((16 * r + 64, width), BF16)], "line")[0]


def stack_rows(ids, arrays, spans):
    width = arrays[0].shape[1]

    def kernel(ids, *refs):
        for out, (low, high) in zip(refs[3:], spans):
            for a in range(3):
                out[a] = refs[a][low:high]

    return simple(kernel, ids, arrays,
                  [jax.ShapeDtypeStruct((3, high - low, width), BF16) for low, high in spans], "stack")


def head_kernel(seq, pad, ids, counts, depth, mine, sib, x_ref, cot_ref, at_out, ow_out, vec_ref, b2_ref, b3_ref,
                a1_ref, gm_ref, qkv_ref, o_ref, lse_ref, at_s, ow_s, xs, lse_s, sems):
    q, z, c = ids[0], ids[1], ids[2]
    copies = [pltpu.make_async_copy(at_s, at_out, sems.at[0]), pltpu.make_async_copy(ow_s, ow_out, sems.at[1])]
    step = pl.program_id(0)

    @pl.when(step == 0)
    def _():
        r = ow_s.shape[0] // 8
        cut = b2_ref.shape[2]
        for j in range(8):
            a = (j >> 1) ^ z
            own = ((j & 1) ^ c) == 0

            def place(ref_in):
                small = ref_in[pl.ds(pl.multiple_of(16 * r + 16 * a, 16), 16), 0:r].astype(F32)
                vec_ref[0:8, j * r:(j + 1) * r] = small[0:8]
                for k in range(4):
                    row = small[8 + k:9 + k]
                    at, to = k * r, (k + 1) * r
                    if at < cut:
                        b2_ref[j, :, at:min(to, cut)] = row[:, 0:min(to, cut) - at]
                    if to > cut:
                        b3_ref[j, :, max(at, cut) - cut:to - cut] = row[:, max(at, cut) - at:]
                for t in range(4):
                    ref, at = (ow_s, j * r) if t == 3 else (at_s, (3 * j + t) * r)
                    ref[at:at + r, :] = ref_in[pl.ds(pl.multiple_of((4 * a + (t ^ q)) * r, r), r), :]

            @pl.when(own)
            def _():
                place(mine)

            @pl.when(jnp.logical_not(own))
            def _():
                place(sib)

        for copy in copies:
            copy.start()

    front_kernel(seq, pad, counts, depth, x_ref, cot_ref, at_s, vec_ref, a1_ref, gm_ref, qkv_ref, o_ref, lse_ref, xs, lse_s)

    @pl.when(step == pl.num_programs(0) - 1)
    def _():
        for copy in copies:
            copy.wait()


def head(ids, counts, depth, mine, sib, images, cot, pad):
    n, seq, width = images.shape
    r = width // 8
    cut = 8 * r // 3
    sd = jax.ShapeDtypeStruct
    far = pl.BlockSpec(memory_space=pl.ANY)
    return pl.pallas_call(
        functools.partial(head_kernel, seq, pad),
        out_shape=[
            sd((24 * r, width), BF16), sd((8 * r, width), BF16), sd((8, width), F32), sd((8, 1, cut), F32),
            sd((8, 1, 4 * r - cut), F32),
            sd((n, pad, width), BF16), sd((n, pad, width), BF16), sd((n, pad, 3 * width), BF16),
            sd((n, pad, width), BF16), sd((n, 16, pad), F32),
        ],
        grid_spec=pltpu.PrefetchScalarGridSpec(
            num_scalar_prefetch=3, grid=(n,),
            in_specs=[whole(mine.shape), whole(sib.shape), by_image((seq, width)), by_image((seq, width))],
            out_specs=[
                far, far, whole((8, width)), whole((8, 1, cut)), whole((8, 1, 4 * r - cut)),
                by_image((pad, width)), by_image((pad, width)), by_image((pad, 3 * width)),
                by_image((pad, width)), by_image((16, pad)),
            ],
            scratch_shapes=[
                pltpu.VMEM((24 * r, width), BF16), pltpu.VMEM((8 * r, width), BF16),
                pltpu.VMEM((pad, width), F32), pltpu.VMEM((pad, 128), F32), pltpu.SemaphoreType.DMA((2,))]),
        compiler_params=params(60),
        cost_estimate=pl.CostEstimate(
            flops=2 * n * pad * width * (3 * width + 4 * pad), bytes_accessed=20 * MIB,
            transcendentals=n * 12 * pad * pad),
        name="head",
    )(ids, counts, depth, mine, sib, images, cot)


def part_kernel(pad, second, group, ids, a2_ref, gm_ref, *rest):
    sides, bu_ref, rest = (rest[0:5], rest[5:10]), rest[10], rest[11:]
    if second:
        mlp_in, ga2_in, a2t, gmt, both, gbu_ref, mlp, ga2, hs, gus = rest
    else:
        both, gbu_ref, mlp, ga2, a2t, gmt, hs, gus = rest
    step = pl.program_id(0)
    q, z, c = ids[0], ids[1], ids[2]
    rows, width = a2_ref.shape
    n = rows // pad
    block = bu_ref.shape[-1]

    @pl.when(step == 0)
    def _():
        if second:
            mlp[...] = mlp_in[...]
            ga2[...] = ga2_in[...]
        else:
            a2t[...] = jnp.transpose(a2_ref[...])
            gmt[...] = jnp.transpose(gm_ref[...])
            mlp[...] = jnp.zeros_like(mlp)
            ga2[...] = jnp.zeros_like(ga2)

    pairs = [(k, side) for k in range(group) for side in range(2)]
    owners = [(((step * group + k) ^ z) << 1) | (c ^ side) for k, side in pairs]
    r = sides[0][0].shape[1] // 2

    def piece(k, side, t, low):
        own, message, *crossed = sides[side]
        slot, m = step * group + k, t ^ q
        at = slice(low, low + r)
        index = jnp.maximum(slot - 1, 0) if group > 1 else 0
        value = message[index, at]
        for x, ref in enumerate(crossed):
            value = jnp.where(m == x + 1, ref[index, at], value)
        return jnp.where(slot == 0, own[m, at], value)

    up = jnp.concatenate([piece(k, side, t, 0) for k, side in pairs for t in range(4)], 0)
    down = jnp.concatenate([piece(k, side, t, r) for k, side in pairs for t in range(4)], 0)
    bu = jnp.concatenate([bu_ref[owner] for owner in owners], 1)
    gbu = jnp.zeros(bu.shape, F32)
    for i in range(n):
        at = slice(i * pad, (i + 1) * pad)
        u = nt(a2_ref[at, :], up) + bu
        t = nt(gm_ref[at, :], down)
        act, slope = gelu_pair(u)
        h = act.astype(BF16)
        gu = (t * slope).astype(BF16)
        hs[at, :] = h
        gus[at, :] = gu
        gbu = gbu + col_sum(gu.astype(F32))
        mlp[at, :] += nn(h, down)
        ga2[at, :] += nn(gu, up)
    for p, owner in enumerate(owners):
        gbu_ref[owner] = gbu[:, p * block:(p + 1) * block]
    part = width // 4
    span = 2 * group
    for t in range(4):
        at = slice(t * part, (t + 1) * part)
        for kind, (left, right) in enumerate(((a2t, gus), (gmt, hs))):
            d = nn(left[at, :], right[...]).astype(BF16)
            for p, owner in enumerate(owners):
                both[owner % span, t, kind] = d[:, p * block:(p + 1) * block]


def part(ids, a2, gm, mine, sib, bu, pad, group, offset, carry=()):
    rows, width = a2.shape
    block = bu.shape[-1]
    r = block // 4
    second = len(carry) > 0
    steps = 4 // group
    sd = jax.ShapeDtypeStruct
    own = pl.BlockSpec((4, 2 * r, width), lambda s, *_: (0, offset // (2 * r), 0), pipeline_mode=pl.Buffered(1))
    if group > 1:
        got = pl.BlockSpec((3, 2 * r, width), lambda s, *_: (0, offset // (2 * r), 0), pipeline_mode=pl.Buffered(1))
    else:
        got = pl.BlockSpec((1, 2 * r, width), lambda s, *_: (jnp.maximum(s - 1, 0), offset // (2 * r), 0))
    acc = sd((rows, width), F32)
    tr = sd((width, rows), BF16)
    outs = [sd((8, 1, block), F32), acc, acc] + ([] if second else [tr, tr])
    return pl.pallas_call(
        functools.partial(part_kernel, pad, second, group),
        out_shape=[sd((8, 4, 2, width // 4, block), BF16)] + outs,
        grid_spec=pltpu.PrefetchScalarGridSpec(
            num_scalar_prefetch=1, grid=(steps,),
            in_specs=[whole(a2.shape), whole(gm.shape)] + [own, got, got, got, got] * 2 + [whole(bu.shape)] + [whole(s.shape) for s in carry],
            out_specs=[pl.BlockSpec((2 * group, 4, 2, width // 4, block),
                                    lambda s, ids, *_: (s ^ (ids[1] // group), 0, 0, 0, 0))]
            + [whole(s.shape) for s in outs],
            scratch_shapes=[pltpu.VMEM((rows, 2 * group * block), BF16), pltpu.VMEM((rows, 2 * group * block), BF16)]),
        compiler_params=params(60),
        cost_estimate=pl.CostEstimate(
            flops=12 * rows * width * 8 * block, bytes_accessed=30 * MIB, transcendentals=0),
        name="feed_b" if second else "feed_a",
    )(ids, a2, gm, *mine, *sib, bu, *carry)


def turn_kernel(seq, pad, counts, depth, mlp, ga2, x1_ref, cot_ref, gm_ref, vecs,
                y_ref, gx_ref, ga_ref, vec_ref, cs):
    i = pl.program_id(0)
    width = x1_ref.shape[-1]
    ok = lax.broadcasted_iota(jnp.int32, (pad, 1), 0) < counts[i]
    x1 = x1_ref[0]
    out = mlp[0] + vecs[7:8, :]
    y_ref[0] = jnp.where(ok, x1 + depth[i, 1] * out, 0.0).astype(BF16)[0:seq]
    cs[pad - 8:pad, :] = jnp.zeros((8, width), F32)
    cs[0:seq, :] = cot_ref[0].astype(F32)
    g = jnp.where(ok, cs[...], 0.0)
    back = ga2[0]
    normed, rstd = normalize(x1)
    e = back * vecs[5:6, :]
    gx = g + rstd * (e - mean_row(e) - normed * mean_row(e * normed))
    gx_ref[0] = gx
    ga = (depth[i, 0] * gx).astype(BF16)
    ga_ref[0] = ga

    @pl.when(i == 0)
    def _():
        vec_ref[...] = jnp.zeros_like(vec_ref)

    vec_ref[0:1, :] += col_sum(back * normed)
    vec_ref[1:2, :] += col_sum(back)
    vec_ref[2:3, :] += col_sum(gm_ref[0].astype(F32))
    vec_ref[3:4, :] += col_sum(ga.astype(F32))
    vec_ref[4:5, :] += col_sum(jnp.where(ok, out * out, 0.0))


def turn(counts, depth, mlp, ga2, x1, cot, gm, vec):
    n, seq, width = cot.shape
    pad = x1.shape[1]
    sd = jax.ShapeDtypeStruct
    rows = lambda array: array.reshape(n, pad, width)
    return pl.pallas_call(
        functools.partial(turn_kernel, seq, pad),
        out_shape=[sd((n, seq, width), BF16), sd((n, pad, width), F32), sd((n, pad, width), BF16), sd((8, width), F32)],
        grid_spec=pltpu.PrefetchScalarGridSpec(
            num_scalar_prefetch=2, grid=(n,),
            in_specs=[by_image((pad, width))] * 3 + [by_image((seq, width)), by_image((pad, width)), whole(vec.shape)],
            out_specs=[by_image((seq, width)), by_image((pad, width)), by_image((pad, width)), whole((8, width))],
            scratch_shapes=[pltpu.VMEM((pad, width), F32)]),
        compiler_params=params(60),
        cost_estimate=pl.CostEstimate(flops=10 ** 8, bytes_accessed=20 * MIB, transcendentals=0),
        name="turn",
    )(counts, depth, rows(mlp), rows(ga2), x1, cot, rows(gm), vec)


def grads_kernel(far_z, ids, g_ref, o_ref, a1_ref, ga_ref, near, far, cols_ref):
    s = pl.program_id(0)
    q, z, c = ids[0], ids[1], ids[2]
    r = near.shape[2]
    side = (z >> 1) ^ int(far_z)

    def put(value, j, t):
        a, m = ((j >> 1) ^ z) & 1, t ^ q
        own = ((j & 1) ^ c) == 0

        @pl.when(own)
        def _():
            near[m, a] = value

        @pl.when(jnp.logical_not(own))
        def _():
            far[m, a] = value

    @pl.when(s < 3)
    def _():
        g = g_ref[...]
        d = tn(g, a1_ref[...]).astype(BF16)
        cols_ref[...] = col_sum(g.astype(F32))
        for k in range(4):
            chunk = 4 * s + k
            put(d[k * r:(k + 1) * r], 4 * side + chunk // 3, chunk % 3)

    @pl.when(s >= 3)
    def _():
        d = tn(o_ref[...], ga_ref[...]).astype(BF16)
        for k in range(4):
            put(d[k * r:(k + 1) * r], 4 * side + k, 3)


def grads(ids, g, o, a1, ga, far_z, cols):
    rows, width = a1.shape
    r = width // 8
    block = 4 * r
    sd = jax.ShapeDtypeStruct
    side = lambda ids: (ids[1] >> 1) ^ int(far_z)
    column = lambda s, ids: (0, 3 * side(ids) + jnp.minimum(s, 2))
    kernel = functools.partial(grads_kernel, far_z)
    more = []
    if cols is not None:
        more = [cols]
        kernel = lambda ids, g, o, a1, ga, cols_in, *outs: grads_kernel(far_z, ids, g, o, a1, ga, *outs)
    return pl.pallas_call(
        kernel,
        out_shape=[sd((4, 2, r, width), BF16), sd((4, 2, r, width), BF16), sd((1, 3 * width), F32)],
        grid_spec=pltpu.PrefetchScalarGridSpec(
            num_scalar_prefetch=1, grid=(4,),
            in_specs=[
                pl.BlockSpec((rows, block), column),
                pl.BlockSpec((rows, block), lambda s, ids: (0, side(ids))),
                whole(a1.shape), whole(ga.shape)] + [pl.BlockSpec(memory_space=pl.ANY)] * len(more),
            out_specs=[whole((4, 2, r, width)), whole((4, 2, r, width)), pl.BlockSpec((1, block), column)]),
        input_output_aliases={5: 2} if more else {},
        compiler_params=params(60),
        cost_estimate=pl.CostEstimate(
            flops=4 * rows * width * width, bytes_accessed=12 * MIB, transcendentals=0),
        name="grads",
    )(ids, g, o, a1, ga, *more)


def final_kernel(seq, pad, g_ref, w_ref, x_ref, gx_ref, vecs, gi_ref, vec_ref, xs):
    i = pl.program_id(0)
    width = x_ref.shape[-1]
    grad = nn(g_ref[0], w_ref[...])
    xs[pad - 8:pad, :] = jnp.zeros((8, width), F32)
    xs[0:seq, :] = x_ref[0].astype(F32)
    normed, rstd = normalize(xs[...])

    @pl.when(i == 0)
    def _():
        vec_ref[...] = jnp.zeros_like(vec_ref)

    vec_ref[0:1, :] += col_sum(grad * normed)
    vec_ref[1:2, :] += col_sum(grad)
    e = grad * vecs[0:1, :]
    gi = gx_ref[0] + rstd * (e - mean_row(e) - normed * mean_row(e * normed))
    gi_ref[0] = gi[0:seq]


def final(g, w, images, gx, vec, pad):
    n, seq, width = images.shape
    sd = jax.ShapeDtypeStruct
    return pl.pallas_call(
        functools.partial(final_kernel, seq, pad),
        out_shape=[sd((n, seq, width), F32), sd((8, width), F32)],
        grid=(n,),
        in_specs=[by_image((pad, 3 * width)), whole(w.shape), by_image((seq, width)), by_image((pad, width)),
                  whole(vec.shape)],
        out_specs=[by_image((seq, width)), whole((8, width))],
        scratch_shapes=[pltpu.VMEM((pad, width), F32)],
        compiler_params=params(60),
        cost_estimate=pl.CostEstimate(
            flops=6 * n * pad * width * width, bytes_accessed=18 * MIB, transcendentals=0),
        name="final",
    )(g, w, images, gx, vec)


def add_pair(ids, near, got):
    slots, parts = near.shape[:2]
    shape = near.shape[1:]
    block = pl.BlockSpec((slots, 1) + shape[1:], lambda a, *_: (0, a) + (0,) * (len(shape) - 1))

    def kernel(a_ref, b_ref, *outs):
        for m in range(4):
            outs[m][...] = (a_ref[m].astype(F32) + b_ref[m].astype(F32)).astype(BF16)

    return pl.pallas_call(
        kernel,
        out_shape=[jax.ShapeDtypeStruct(shape, BF16)] * slots,
        grid=(parts,),
        in_specs=[block, block],
        out_specs=[pl.BlockSpec((1,) + shape[1:], lambda a: (a,) + (0,) * (len(shape) - 1))] * slots,
        compiler_params=params(60),
        cost_estimate=pl.CostEstimate(flops=0, bytes_accessed=6 * near.size, transcendentals=0),
        name="add_pair",
    )(near, got)


def add_four(ids, parts, split):
    shape = parts[0].shape

    def kernel(ids, a, b, c, d, *outs):
        if split:
            for k in range(shape[0]):
                outs[k][...] = ((a[k].astype(F32) + b[k].astype(F32)) + (c[k].astype(F32) + d[k].astype(F32))).astype(BF16)
        else:
            outs[0][...] = ((a[...].astype(F32) + b[...].astype(F32)) + (c[...].astype(F32) + d[...].astype(F32))).astype(BF16)

    count = shape[0] if split else 1
    out = jax.ShapeDtypeStruct(shape[1:] if split else shape, BF16)
    return simple(kernel, ids, parts, [out] * count, "add_four")


def merge(ids, s2, s3):
    _, _, rows, k2 = s2.shape
    k3 = s3.shape[3]

    def kernel(ids, a, b, out):
        for ref, at, to in ((a, 0, k2), (b, k2, k2 + k3)):
            out[:, :, at:to] = ((ref[0].astype(F32) + ref[1].astype(F32)) + (ref[2].astype(F32) + ref[3].astype(F32))).astype(BF16)

    return simple(kernel, ids, [s2, s3], [jax.ShapeDtypeStruct((2, rows, k2 + k3), BF16)], "merge")[0]


def place_feed_kernel(ids, p0, p1, p2, p3, up_ref, down_ref, cs):
    q = ids[0]
    rows = p0.shape[1]
    for m, p in enumerate((p0, p1, p2, p3)):
        to = pl.ds(pl.multiple_of((q ^ m) * rows, rows), rows)
        up_ref[to, :] = p[0].astype(F32)
        cs[to, :] = p[1].astype(F32)
    down_ref[...] = jnp.transpose(cs[...])


def place_feed(ids, parts):
    _, rows, block = parts[0].shape
    sd = jax.ShapeDtypeStruct
    return simple(place_feed_kernel, ids, parts, [sd((4 * rows, block), F32), sd((block, 4 * rows), F32)],
                  "place_feed", scratch=[pltpu.VMEM((4 * rows, block), F32)])


def place_attend_kernel(ids, p0, p1, p2, p3, at_ref, ow_ref, cs):
    q = ids[0]
    r = p0.shape[0]
    for m, p in enumerate((p0, p1, p2, p3)):
        cs[pl.ds(pl.multiple_of((q ^ m) * r, r), r), :] = p[...].astype(F32)
    at_ref[...] = jnp.transpose(cs[...])[:, 0:3 * r]
    ow_ref[...] = cs[3 * r:4 * r, :]


def place_attend(ids, parts):
    r, width = parts[0].shape
    sd = jax.ShapeDtypeStruct
    return simple(place_attend_kernel, ids, parts, [sd((width, 3 * r), F32), sd((r, width), F32)],
                  "place_attend", scratch=[pltpu.VMEM((4 * r, width), F32)])


def shards_grid(
    images, grid_sizes, keep_flags, attn_gain, attn_shift, attend_weight, query_bias, value_bias,
    output_weight, output_bias, mlp_gain, mlp_shift, up_weight, up_bias, down_weight, down_bias,
    cotangent,
):
    n, seq, width = images.shape
    pad = -(-seq // 32) * 32
    counts = grid_sizes[:, 0] * grid_sizes[:, 1] + 2
    depth = keep_flags.astype(F32) / KEEP_PROB
    owners = 8
    share = attn_gain.shape[0]
    f = lax.axis_index("fsdp")
    ids = jnp.stack([lax.axis_index("dp"), f >> 1, f & 1]).astype(jnp.int32)

    z_all = lambda array: [over_z(array, a) for a in (1, 2, 3)]
    dp_all = lambda array: [over_dp(array, m) for m in (1, 2, 3)]
    dp_out = lambda s: [s[0]] + [over_dp(s[m], m) for m in (1, 2, 3)]
    z_out = lambda s: [s[0]] + [over_z(s[a], a) for a in (1, 2, 3)]
    tied = lax.optimization_barrier
    flat = lambda array: array.reshape(n * pad, array.shape[-1])

    own1, first1, own, first = pack(
        ids, attend_weight, output_weight, up_weight, down_weight,
        [attn_gain, attn_shift, query_bias, value_bias, output_bias, mlp_gain, mlp_shift, down_bias, up_bias])
    zr1 = z_all(first1)
    first = after(first, zr1)
    message1, = stack_rows(ids, zr1, [(0, share)])
    xr1 = dp_all(message1)
    zr = z_all(first)
    xr1, zr = tied((xr1, zr))
    mine1 = line(ids, own1, first1, zr1, xr1)
    sib1 = over_core(mine1)
    message, = stack_rows(ids, zr, [(0, 2 * share)])
    xr = dp_all(message)
    sib1, message = tied((sib1, message))
    other = [over_core(own), over_core(message)]
    attend, out_w, vec, bu2, bu3, a1, gm, qkv, o, lse = head(ids, counts, depth, mine1, sib1, images, cotangent, pad)
    o, xr, other = tied((o, xr, other))
    mine, sib = [own, message, *xr], [*other, *(over_core(x) for x in xr)]
    x1, a2, sums_two = middle(counts, depth, o, images, out_w, vec, pad)
    x1, a2, sib = tied((x1, a2, sib))
    a2, gm = flat(a2), flat(gm)
    both2, gbu2, *carry = part(ids, a2, gm, mine, sib, bu2, pad, 1, 0)

    own_sum = lambda both: lax.psum_scatter(
        both.reshape(-1, both.shape[-1]), "fsdp", scatter_dimension=0, tiled=True).reshape(both.shape[1:])
    quarter = lambda shard: lax.all_to_all(shard, "dp", 0, 0, tiled=True)
    shard2 = own_sum(both2)
    both3, gbu3, mlp, ga2 = part(ids, a2, gm, mine, sib, bu3, pad, 2, 4 * (share // 3), carry)
    shard3 = own_sum(both3)
    y, gx, ga, vec_feed = turn(counts, depth, mlp, ga2, x1, cotangent, gm, vec)
    g = back(counts, ga, out_w, qkv, lse)
    near_p, far_p, cols = grads(ids, flat(g), flat(o), flat(a1), flat(ga), True, None)
    near_p, far_p, shard2 = tied((near_p, far_p, shard2))
    got_p = over_core(far_p)
    quarter2 = quarter(shard2)
    near_q, far_q, cols = grads(ids, flat(after(g, near_p)), flat(o), flat(a1), flat(ga), False, cols)
    near_q, far_q, got_p, quarter2 = tied((near_q, far_q, got_p, quarter2))
    got_q = over_core(far_q)
    s_p = add_pair(ids, near_p, got_p)
    dr_p = dp_out(s_p)
    gi, vec_last = final(after(g, s_p), attend, images, gx, vec, pad)
    gi, vec_last, got_q, dr_p = tied((gi, vec_last, got_q, dr_p))
    s_q = add_pair(ids, near_q, got_q)
    dr_q = dp_out(s_q)
    e_p = add_four(ids, after(dr_p, s_q), True)
    er_p = [over_z(e_p[0], 2), over_z(e_p[1], 3)]
    rows = jnp.concatenate([
        vec_last[0:2], cols[:, :width], cols[:, 2 * width:], vec_feed[3:4], vec_feed[0:3],
        jnp.concatenate([gbu2[:, 0], gbu3[:, 0]], 1).reshape(4, width), sums_two[:, 0:2].sum(0), vec_feed[4:5],
        jnp.full((1, width), jnp.sum(counts).astype(F32)),
    ], 0)
    rows = rows + over_core(after(rows, e_p))
    er_p, dr_q, rows, shard3 = tied((er_p, dr_q, rows, shard3))
    e_q = add_four(ids, dr_q, True)
    er_q = over_z(e_q[1], 1)
    quarter3 = quarter(after(shard3, e_q))
    rows = rows + over_dp(rows, 1)
    rows = rows + over_dp(rows, 2)
    er_q, rows, quarter3 = tied((er_q, rows, quarter3))
    f1 = add_four(ids, [e_q[0], er_q, *er_p], False)[0]
    fr1 = [f1] + dp_all(f1)
    f3 = merge(ids, quarter2, after(quarter3, f1))
    fr3 = [f3] + dp_all(f3)
    rows = rows + over_z(rows, 1)
    rows = rows + over_z(rows, 2)
    root_means = jnp.sqrt(jnp.sum(rows[12:15], 1) / (rows[15, 0] * width))
    tv = [lax.dynamic_slice(rows[k], (f * share,), (share,)) for k in range(8)]
    gub = lax.dynamic_slice(rows[8:12].reshape(-1), (f * up_bias.shape[0],), up_bias.shape)
    gattend, gout = place_attend(ids, fr1)
    gup, gdown = place_feed(ids, fr3)
    return (y, gi, tv[0], tv[1], gattend, tv[2], tv[3], gout, tv[4], tv[5], tv[6],
            gup, gub, gdown, tv[7], root_means)


def shards(on_grid, *args):
    images, attn_gain, up_weight = args[0], args[3], args[12]
    share = attn_gain.shape[0]
    fits = on_grid and share % 48 == 0 and up_weight.shape[1] == 4 * share and images.shape[2] == 8 * share
    return (shards_grid if fits else shards_any)(*args)


def solution(mesh):
    images = P(("dp", "fsdp"), None, None)
    flags = P(("dp", "fsdp"), None)
    vec, rows, cols = P("fsdp"), P("fsdp", None), P(None, "fsdp")
    return jax.shard_map(
        functools.partial(shards, dict(mesh.shape) == {"dp": 4, "fsdp": 8}),
        mesh=mesh,
        in_specs=(images, flags, flags, vec, vec, cols, vec, vec, rows, vec, vec, vec, cols, vec, rows,
                  vec, images),
        out_specs=(images, images, vec, vec, cols, vec, vec, rows, vec, vec, vec, cols, vec, rows, vec,
                   P()),
        check_vma=False,
    )
```

```python
import functools
import math

import jax
import jax.numpy as jnp
from jax import lax
from jax.experimental import pallas as pl
from jax.experimental.pallas import tpu as pltpu
from jax.sharding import PartitionSpec as P

HEAD_DIM = 64
EPS = 1e-06
KEEP_PROB = 0.9
MASKED = -1e30
INV_ROOT_TWO = 0.7071067811865476
INV_ROOT_TWO_PI = 0.3989422804014327
F32 = jnp.float32
BF16 = jnp.bfloat16
MIB = 1024 * 1024


def nn(left, right):
    return lax.dot_general(left, right, (((1,), (0,)), ((), ())), preferred_element_type=F32)


def nt(left, right):
    return lax.dot_general(left, right, (((1,), (1,)), ((), ())), preferred_element_type=F32)


def tn(left, right):
    return lax.dot_general(left, right, (((0,), (0,)), ((), ())), preferred_element_type=F32)


def mean_row(values):
    return jnp.sum(values, -1, keepdims=True) * (1.0 / values.shape[-1])


def normalize(values):
    center = values - mean_row(values)
    rstd = lax.rsqrt(mean_row(center * center) + EPS)
    return center * rstd, rstd


def col_sum(values):
    return jnp.sum(values, 0, keepdims=True)


def params(limit, steps=1):
    return pltpu.CompilerParams(
        dimension_semantics=("arbitrary",) * steps, vmem_limit_bytes=limit * MIB
    )


def whole(shape, buffers=1):
    zeros = (0,) * len(shape)
    return pl.BlockSpec(shape, lambda *_: zeros, pipeline_mode=pl.Buffered(buffers))


def by_image(shape):
    rest = (0,) * len(shape)
    return pl.BlockSpec((1,) + shape, lambda i, *_: (i,) + rest)


SMEM = pl.BlockSpec(memory_space=pltpu.SMEM)


def front_kernel(seq, pad, counts, depth, x_ref, cot_ref, w_ref, vec_ref,
                 a1_ref, gm_ref, qkv_ref, o_ref, lse_ref, xs, lse_s):
    i = pl.program_id(0)
    width = x_ref.shape[-1]
    count = counts[i]
    rows = lax.broadcasted_iota(jnp.int32, (pad, 1), 0)
    xs[pad - 8:pad, :] = jnp.zeros((8, width), F32)
    xs[0:seq, :] = cot_ref[0].astype(F32)
    gm_ref[0] = jnp.where(rows < count, xs[...] * depth[i, 1], 0.0).astype(BF16)
    xs[0:seq, :] = x_ref[0].astype(F32)
    normed, _ = normalize(xs[...])
    attend_image(pad, count, normed, w_ref, vec_ref, a1_ref, qkv_ref, o_ref, lse_ref, lse_s)


def attend_image(pad, count, normed, w_ref, vec_ref, a1_ref, qkv_ref, o_ref, lse_ref, lse_s):
    width = normed.shape[-1]
    pairs = width // 128
    a1 = (normed * vec_ref[0:1, :] + vec_ref[1:2, :]).astype(BF16)
    a1_ref[0] = a1
    for c in range(0, 3 * width, 384):
        part = nt(a1, w_ref[c:c + 384, :])
        if c < width:
            part = part + vec_ref[2:3, c:c + 384]
        elif c >= 2 * width:
            part = part + vec_ref[3:4, c - 2 * width:c - 2 * width + 384]
        qkv_ref[0, :, c:c + 384] = part.astype(BF16)
    ok = lax.broadcasted_iota(jnp.int32, (pad, pad), 1) < count
    lane = lax.broadcasted_iota(jnp.int32, (pad, 128), 1)
    lse_s[...] = jnp.zeros((pad, 128), F32)

    def pair(p):
        at = pl.multiple_of(p * 128, 128)
        q = qkv_ref[0, :, pl.ds(at, 128)] * 0.125
        k = qkv_ref[0, :, pl.ds(width + at, 128)]
        v = qkv_ref[0, :, pl.ds(2 * width + at, 128)]
        total = jnp.zeros((pad, 128), F32)
        for half in range(2):
            mine = (lane >= 64) if half else (lane < 64)
            scores = jnp.where(ok, nt(jnp.where(mine, q, 0), k), MASKED)
            top = jnp.max(scores, -1, keepdims=True)
            e = jnp.exp(scores - top)
            s = jnp.sum(e, -1, keepdims=True)
            prob = (e * (1.0 / s)).astype(BF16)
            total = total + nn(prob, jnp.where(mine, v, 0))
            lse_s[...] = jnp.where(lane == 2 * p + half, top + jnp.log(s), lse_s[...])
        o_ref[0, :, pl.ds(at, 128)] = total.astype(BF16)

    for p in range(pairs):
        pair(p)
    lse_ref[0] = jnp.transpose(lse_s[...])[0:16, :]


def front(counts, depth, images, cot, w, vec, pad):
    n, seq, width = images.shape
    grid_spec = pltpu.PrefetchScalarGridSpec(
        num_scalar_prefetch=2,
        grid=(n,),
        in_specs=[
            by_image((seq, width)), by_image((seq, width)),
            whole(w.shape), whole(vec.shape),
        ],
        out_specs=[
            by_image((pad, width)), by_image((pad, width)), by_image((pad, 3 * width)),
            by_image((pad, width)), by_image((16, pad)),
        ],
        scratch_shapes=[pltpu.VMEM((pad, width), F32), pltpu.VMEM((pad, 128), F32)],
    )
    return pl.pallas_call(
        functools.partial(front_kernel, seq, pad),
        out_shape=[
            jax.ShapeDtypeStruct((n, pad, width), BF16),
            jax.ShapeDtypeStruct((n, pad, width), BF16),
            jax.ShapeDtypeStruct((n, pad, 3 * width), BF16),
            jax.ShapeDtypeStruct((n, pad, width), BF16),
            jax.ShapeDtypeStruct((n, 16, pad), F32),
        ],
        grid_spec=grid_spec,
        compiler_params=params(60),
        cost_estimate=pl.CostEstimate(
            flops=2 * n * pad * width * (3 * width + 4 * pad), bytes_accessed=20 * MIB,
            transcendentals=n * 12 * pad * pad),
        name="front",
    )(counts, depth, images, cot, w, vec)


def middle_kernel(seq, pad, counts, depth, o_ref, x_ref, w_ref, vec_ref,
                  x1_ref, a2_ref, sums_ref, xs):
    i = pl.program_id(0)
    width = x_ref.shape[-1]
    rows = lax.broadcasted_iota(jnp.int32, (pad, 1), 0)
    ok = rows < counts[i]
    xs[pad - 8:pad, :] = jnp.zeros((8, width), F32)
    xs[0:seq, :] = x_ref[0].astype(F32)
    attn = nn(o_ref[0], w_ref[...]) + vec_ref[4:5, :]
    x1 = xs[...] + depth[i, 0] * attn
    x1_ref[0] = x1
    sums_ref[0, 0:1, :] = col_sum(jnp.where(ok, x1 * x1, 0.0))
    sums_ref[0, 1:2, :] = col_sum(jnp.where(ok, attn * attn, 0.0))
    sums_ref[0, 2:8, :] = jnp.zeros((6, width), F32)
    normed, _ = normalize(x1)
    a2_ref[0] = (normed * vec_ref[5:6, :] + vec_ref[6:7, :]).astype(BF16)


def middle(counts, depth, o, images, w, vec, pad):
    n, seq, width = images.shape
    grid_spec = pltpu.PrefetchScalarGridSpec(
        num_scalar_prefetch=2,
        grid=(n,),
        in_specs=[
            by_image((pad, width)), by_image((seq, width)),
            whole(w.shape), whole(vec.shape),
        ],
        out_specs=[by_image((pad, width)), by_image((pad, width)), by_image((8, width))],
        scratch_shapes=[pltpu.VMEM((pad, width), F32)],
    )
    return pl.pallas_call(
        functools.partial(middle_kernel, seq, pad),
        out_shape=[
            jax.ShapeDtypeStruct((n, pad, width), F32),
            jax.ShapeDtypeStruct((n, pad, width), BF16),
            jax.ShapeDtypeStruct((n, 8, width), F32),
        ],
        grid_spec=grid_spec,
        compiler_params=params(60),
        cost_estimate=pl.CostEstimate(
            flops=2 * n * pad * width * width, bytes_accessed=10 * MIB, transcendentals=0),
        name="middle",
    )(counts, depth, o, images, w, vec)


def gelu_pair(u):
    size = jnp.abs(u)
    t = 1.0 / (1.0 + (0.3275911 * INV_ROOT_TWO) * size)
    bell = jnp.exp(-0.5 * (u * u))
    series = t * (0.5 * 0.254829592 + t * (0.5 * -0.284496736 + t * (
        0.5 * 1.421413741 + t * (0.5 * -1.453152027 + t * (0.5 * 1.061405429)))))
    tail = series * bell
    phi = jnp.where(u >= 0, 1.0 - tail, tail)
    return u * phi, phi + u * (bell * INV_ROOT_TWO_PI)


def feed_kernel(seq, pad, counts, depth, a2_ref, gm_ref, up_ref, down_ref, bu_ref, x1_ref, cot_ref,
                vecs,
                dup_ref, ddown_ref, gbu_ref, y_ref, gx_ref, ga_ref, vec_ref,
                a2t, gmt, mlp, ga2, hs, gus, cs):
    j = pl.program_id(0)
    n = x1_ref.shape[0]

    @pl.when(j == 0)
    def _():
        a2t[...] = jnp.transpose(a2_ref[...])
        gmt[...] = jnp.transpose(gm_ref[...])
        mlp[...] = jnp.zeros_like(mlp)
        ga2[...] = jnp.zeros_like(ga2)

    gbu = jnp.zeros(bu_ref.shape[1:], F32)
    for i in range(n):
        at = slice(i * pad, (i + 1) * pad)
        u = nt(a2_ref[at, :], up_ref[...]) + bu_ref[0]
        t = nt(gm_ref[at, :], down_ref[...])
        act, slope = gelu_pair(u)
        h = act.astype(BF16)
        gu = (t * slope).astype(BF16)
        hs[at, :] = h
        gus[at, :] = gu
        gbu = gbu + col_sum(gu.astype(F32))
        mlp[at, :] += nn(h, down_ref[...])
        ga2[at, :] += nn(gu, up_ref[...])
    gbu_ref[0] = gbu
    dup_ref[0] = nn(a2t[...], gus[...]).astype(BF16)
    ddown_ref[0] = nn(gmt[...], hs[...]).astype(BF16)

    @pl.when(j == pl.num_programs(0) - 1)
    def _():
        width = x1_ref.shape[-1]
        rows = lax.broadcasted_iota(jnp.int32, (pad, 1), 0)
        cs[pad - 8:pad, :] = jnp.zeros((8, width), F32)
        msum = jnp.zeros((1, width), F32)
        ggain = jnp.zeros((1, width), F32)
        gshift = jnp.zeros((1, width), F32)
        gdown = jnp.zeros((1, width), F32)
        gout = jnp.zeros((1, width), F32)
        for i in range(n):
            at = slice(i * pad, (i + 1) * pad)
            ok = rows < counts[i]
            x1 = x1_ref[i]
            out = mlp[at, :] + vecs[7:8, :]
            msum = msum + col_sum(jnp.where(ok, out * out, 0.0))
            y_ref[i] = jnp.where(ok, x1 + depth[i, 1] * out, 0.0).astype(BF16)[0:seq]
            cs[0:seq, :] = cot_ref[i].astype(F32)
            g = jnp.where(ok, cs[...], 0.0)
            gdown = gdown + col_sum(gm_ref[at, :].astype(F32))
            back = ga2[at, :]
            normed, rstd = normalize(x1)
            ggain = ggain + col_sum(back * normed)
            gshift = gshift + col_sum(back)
            e = back * vecs[5:6, :]
            gx = g + rstd * (e - mean_row(e) - normed * mean_row(e * normed))
            gx_ref[i] = gx
            ga = (depth[i, 0] * gx).astype(BF16)
            ga_ref[i] = ga
            gout = gout + col_sum(ga.astype(F32))
        vec_ref[0:1, :] = ggain
        vec_ref[1:2, :] = gshift
        vec_ref[2:3, :] = gdown
        vec_ref[3:4, :] = gout
        vec_ref[4:5, :] = msum
        vec_ref[5:8, :] = jnp.zeros((3, width), F32)


def feed(counts, depth, a2, gm, up, down, bu, x1, cot, vec, seq, pad, block):
    rows, width = a2.shape
    n = rows // pad
    hidden = up.shape[0]
    steps = hidden // block
    at = lambda j, *_: (j, 0)
    at3 = lambda j, *_: (j, 0, 0)
    grid_spec = pltpu.PrefetchScalarGridSpec(
        num_scalar_prefetch=2,
        grid=(steps,),
        in_specs=[
            whole(a2.shape), whole(gm.shape),
            pl.BlockSpec((block, width), at), pl.BlockSpec((block, width), at),
            pl.BlockSpec((1, 1, block), at3),
            whole(x1.shape), whole(cot.shape), whole(vec.shape),
        ],
        out_specs=[
            pl.BlockSpec((1, width, block), at3), pl.BlockSpec((1, width, block), at3),
            pl.BlockSpec((1, 1, block), at3),
            whole((n, seq, width)), whole((n, pad, width)), whole((n, pad, width)), whole((8, width)),
        ],
        scratch_shapes=[
            pltpu.VMEM((width, rows), BF16), pltpu.VMEM((width, rows), BF16),
            pltpu.VMEM((rows, width), F32), pltpu.VMEM((rows, width), F32),
            pltpu.VMEM((rows, block), BF16), pltpu.VMEM((rows, block), BF16),
            pltpu.VMEM((pad, width), F32),
        ],
    )
    return pl.pallas_call(
        functools.partial(feed_kernel, seq, pad),
        out_shape=[
            jax.ShapeDtypeStruct((steps, width, block), BF16),
            jax.ShapeDtypeStruct((steps, width, block), BF16),
            jax.ShapeDtypeStruct((steps, 1, block), F32),
            jax.ShapeDtypeStruct((n, seq, width), BF16),
            jax.ShapeDtypeStruct((n, pad, width), F32),
            jax.ShapeDtypeStruct((n, pad, width), BF16),
            jax.ShapeDtypeStruct((8, width), F32),
        ],
        grid_spec=grid_spec,
        compiler_params=params(60),
        cost_estimate=pl.CostEstimate(
            flops=12 * rows * width * hidden, bytes_accessed=40 * MIB, transcendentals=rows * hidden),
        name="feed",
    )(counts, depth, a2, gm, up, down, bu.reshape(steps, 1, block), x1, cot, vec)


def back_kernel(pad, counts, ga_ref, w_ref, qkv_ref, lse_ref, g_ref, go):
    i = pl.program_id(0)
    width = ga_ref.shape[-1]
    count = counts[i]
    go[...] = nt(ga_ref[0], w_ref[...]).astype(BF16)
    ok = lax.broadcasted_iota(jnp.int32, (pad, pad), 0) < count
    lane = lax.broadcasted_iota(jnp.int32, (pad, 128), 1)

    def pair(p):
        at = pl.multiple_of(p * 128, 128)
        q = qkv_ref[0, :, pl.ds(at, 128)] * 0.125
        k = qkv_ref[0, :, pl.ds(width + at, 128)]
        v = qkv_ref[0, :, pl.ds(2 * width + at, 128)]
        g = go[:, pl.ds(at, 128)]
        gq = jnp.zeros((pad, 128), F32)
        gk = jnp.zeros((pad, 128), F32)
        gv = jnp.zeros((pad, 128), F32)
        for half in range(2):
            mine = (lane >= 64) if half else (lane < 64)
            qm = jnp.where(mine, q, 0)
            km = jnp.where(mine, k, 0) * 0.125
            gmine = jnp.where(mine, g, 0)
            scores = nt(k, qm)
            row = lse_ref[0, 2 * p + half:2 * p + half + 1, :]
            prob = jnp.where(ok, jnp.exp(scores - row), 0.0)
            dp = nt(v, gmine)
            inner = col_sum(prob * dp)
            ds = (prob * (dp - inner)).astype(BF16)
            gv = gv + nn(prob.astype(BF16), gmine)
            gk = gk + nn(ds, qm)
            gq = gq + tn(ds, km)
        g_ref[0, :, pl.ds(at, 128)] = gq.astype(BF16)
        g_ref[0, :, pl.ds(width + at, 128)] = gk.astype(BF16)
        g_ref[0, :, pl.ds(2 * width + at, 128)] = gv.astype(BF16)

    for p in range(width // 128):
        pair(p)


def back(counts, ga, w, qkv, lse):
    n, pad, width = ga.shape
    grid_spec = pltpu.PrefetchScalarGridSpec(
        num_scalar_prefetch=1,
        grid=(n,),
        in_specs=[by_image((pad, width)), whole(w.shape), by_image((pad, 3 * width)), by_image((16, pad))],
        out_specs=[by_image((pad, 3 * width))],
        scratch_shapes=[pltpu.VMEM((pad, width), BF16)],
    )
    return pl.pallas_call(
        functools.partial(back_kernel, pad),
        out_shape=[jax.ShapeDtypeStruct((n, pad, 3 * width), BF16)],
        grid_spec=grid_spec,
        compiler_params=params(60),
        cost_estimate=pl.CostEstimate(
            flops=2 * n * pad * width * (width + 10 * pad), bytes_accessed=16 * MIB,
            transcendentals=n * 12 * pad * pad),
        name="back",
    )(counts, ga, w, qkv, lse)[0]


def outgrad_kernel(o_ref, ga_ref, d_ref):
    d_ref[...] = tn(o_ref[...], ga_ref[...]).astype(BF16)


def outgrad(o, ga):
    rows, width = o.shape
    return pl.pallas_call(
        outgrad_kernel,
        out_shape=jax.ShapeDtypeStruct((width, width), BF16),
        grid=(2,),
        in_specs=[pl.BlockSpec((rows, width // 2), lambda j: (0, j)), whole(ga.shape)],
        out_specs=pl.BlockSpec((width // 2, width), lambda j: (j, 0)),
        compiler_params=params(60),
        cost_estimate=pl.CostEstimate(
            flops=2 * rows * width * width, bytes_accessed=6 * MIB, transcendentals=0),
        name="outgrad",
    )(o, ga)


def last_kernel(seq, pad, g_ref, a1_ref, w_ref, x_ref, gx_ref, vecs,
                d_ref, cols_ref, gi_ref, vec_ref, ga1, xs):
    c = pl.program_id(0)
    n = x_ref.shape[0]
    g = g_ref[...]
    d_ref[...] = tn(g, a1_ref[...]).astype(BF16)
    cols_ref[...] = col_sum(g.astype(F32))
    part = nn(g, w_ref[...])

    @pl.when(c == 0)
    def _():
        ga1[...] = part

    @pl.when(c > 0)
    def _():
        ga1[...] += part

    @pl.when(c == pl.num_programs(0) - 1)
    def _():
        width = x_ref.shape[-1]
        xs[pad - 8:pad, :] = jnp.zeros((8, width), F32)
        ggain = jnp.zeros((1, width), F32)
        gshift = jnp.zeros((1, width), F32)
        for i in range(n):
            xs[0:seq, :] = x_ref[i].astype(F32)
            normed, rstd = normalize(xs[...])
            grad = ga1[i * pad:(i + 1) * pad, :]
            ggain = ggain + col_sum(grad * normed)
            gshift = gshift + col_sum(grad)
            e = grad * vecs[0:1, :]
            gi = gx_ref[i] + rstd * (e - mean_row(e) - normed * mean_row(e * normed))
            gi_ref[i] = gi[0:seq]
        vec_ref[0:1, :] = ggain
        vec_ref[1:2, :] = gshift
        vec_ref[2:8, :] = jnp.zeros((6, width), F32)


def last(g, a1, w, images, gx, vec, pad, block=384):
    n, seq, width = images.shape
    rows, total = g.shape
    return pl.pallas_call(
        functools.partial(last_kernel, seq, pad),
        out_shape=[
            jax.ShapeDtypeStruct((total, width), BF16),
            jax.ShapeDtypeStruct((1, total), F32),
            jax.ShapeDtypeStruct((n, seq, width), F32),
            jax.ShapeDtypeStruct((8, width), F32),
        ],
        grid=(total // block,),
        in_specs=[
            pl.BlockSpec((rows, block), lambda c: (0, c)), whole(a1.shape),
            pl.BlockSpec((block, width), lambda c: (c, 0)), whole(images.shape), whole(gx.shape),
            whole(vec.shape),
        ],
        out_specs=[
            pl.BlockSpec((block, width), lambda c: (c, 0)), pl.BlockSpec((1, block), lambda c: (0, c)),
            whole((n, seq, width)), whole((8, width)),
        ],
        scratch_shapes=[pltpu.VMEM((rows, width), F32), pltpu.VMEM((pad, width), F32)],
        compiler_params=params(60),
        cost_estimate=pl.CostEstimate(
            flops=4 * rows * width * total, bytes_accessed=30 * MIB, transcendentals=0),
        name="last",
    )(g, a1, w, images, gx, vec)


def shards_any(
    images, grid_sizes, keep_flags, attn_gain, attn_shift, attend_weight, query_bias, value_bias,
    output_weight, output_bias, mlp_gain, mlp_shift, up_weight, up_bias, down_weight, down_bias,
    cotangent,
):
    n, seq, width = images.shape
    pad = -(-seq // 32) * 32
    counts = grid_sizes[:, 0] * grid_sizes[:, 1] + 2
    depth = keep_flags.astype(F32) / KEEP_PROB
    owners = width // attn_gain.shape[0]

    small = jnp.concatenate([
        attn_gain, attn_shift, query_bias, value_bias, output_bias, mlp_gain, mlp_shift, down_bias, up_bias])
    small = lax.all_gather(small.reshape(1, -1), "fsdp", axis=0, tiled=True).astype(F32)
    share = attn_gain.shape[0]
    vec = jnp.stack([small[:, k * share:(k + 1) * share].reshape(width) for k in range(8)])
    bu = small[:, 8 * share:].reshape(1, -1)

    attend = lax.all_gather(attend_weight.T, "fsdp", axis=0, tiled=True)
    out_w = lax.all_gather(output_weight, "fsdp", axis=0, tiled=True)
    up = lax.all_gather(up_weight.T, "fsdp", axis=0, tiled=True)
    down = lax.all_gather(down_weight, "fsdp", axis=0, tiled=True)

    a1, gm, qkv, o, lse = front(counts, depth, images, cotangent, attend, vec, pad)
    x1, a2, sums_two = middle(counts, depth, o, images, out_w, vec, pad)
    flat = lambda array: array.reshape(n * pad, array.shape[-1])
    block = up_weight.shape[1] if up_weight.shape[1] % 128 == 0 else 384
    dup, ddown, gbu, y, gx, ga, vec_feed = feed(
        counts, depth, flat(a2), flat(gm), up, down, bu, x1, cotangent, vec, seq, pad, block)
    dout = outgrad(flat(o), flat(ga))
    g = back(counts, ga, out_w, qkv, lse)
    dattend, cols, gi, vec_last = last(flat(g), flat(a1), attend, images, gx, vec, pad)

    sums = jnp.stack([jnp.sum(sums_two[:, 0]), jnp.sum(sums_two[:, 1]), jnp.sum(vec_feed[4]),
                      jnp.sum(counts).astype(F32)])

    def spread(array):
        return lax.psum(lax.psum_scatter(array, "fsdp", scatter_dimension=0, tiled=True), "dp")

    def columns(array):
        hidden = up.shape[0]
        array = jnp.swapaxes(array, 0, 1).reshape(width, owners, hidden // owners)
        return jnp.swapaxes(array, 0, 1)

    gup = spread(columns(dup))[0]
    gdown = spread(columns(ddown))[0].T
    gout = spread(dout)
    gattend = spread(dattend).T
    rows = jnp.concatenate([
        vec_last[0:2], cols[:, :width], cols[:, 2 * width:], vec_feed[3:4], vec_feed[0:3],
    ], 0)
    tiny = jnp.concatenate([
        jnp.swapaxes(rows.reshape(8, owners, share), 0, 1).reshape(owners, 8 * share),
        gbu.reshape(owners, -1)], 1)
    tiny = spread(tiny)[0]
    sums = lax.psum(sums, ("dp", "fsdp"))
    root_means = jnp.sqrt(sums[:3] / (sums[3] * width))
    tv = [tiny[k * share:(k + 1) * share] for k in range(8)]
    f = lambda array: array.astype(F32)
    return (y, gi, tv[0], tv[1], f(gattend), tv[2], tv[3], f(gout), tv[4], tv[5], tv[6],
            f(gup), tiny[8 * share:], f(gdown), tv[7], root_means)


def over_dp(array, m):
    return lax.ppermute(array, "dp", [(i, i ^ m) for i in range(4)])


def over_z(array, a):
    return lax.ppermute(array, "fsdp", [(i, i ^ (2 * a)) for i in range(8)])


def over_core(array):
    return lax.ppermute(array, "fsdp", [(i, i ^ 1) for i in range(8)])


def staged(kernel, ids, arrays, out_shape, name):
    size = sum(math.prod(s.shape) * s.dtype.itemsize for s in [*arrays, *out_shape])
    return pl.pallas_call(
        kernel,
        out_shape=out_shape,
        grid_spec=pltpu.PrefetchScalarGridSpec(
            num_scalar_prefetch=1, grid=(1,),
            in_specs=[whole(s.shape) for s in arrays],
            out_specs=[whole(s.shape) for s in out_shape]),
        compiler_params=params(60),
        cost_estimate=pl.CostEstimate(flops=0, bytes_accessed=size, transcendentals=0),
        name=name,
    )(ids, *arrays)


def simple(kernel, ids, arrays, out_shape, name, scratch=()):
    size = sum(math.prod(s.shape) * s.dtype.itemsize for s in [*arrays, *out_shape])
    inside = pl.BlockSpec(memory_space=pltpu.VMEM)
    return pl.pallas_call(
        kernel,
        out_shape=out_shape,
        in_specs=[SMEM] + [inside] * len(arrays),
        out_specs=[inside] * len(out_shape),
        scratch_shapes=list(scratch),
        compiler_params=pltpu.CompilerParams(vmem_limit_bytes=16 * MIB),
        cost_estimate=pl.CostEstimate(flops=0, bytes_accessed=size, transcendentals=0),
        name=name,
    )(ids, *arrays)


def pack_kernel(ids, at_ref, ow_ref, up_ref, down_ref, *refs):
    vectors, (own1, first1, own, first, rest) = refs[:9], refs[9:]
    q = ids[0]
    att = at_ref[...]
    up = jnp.transpose(up_ref[...])
    r = ow_ref.shape[0]
    for t in range(4):
        own1[t ^ q] = att[t * r:(t + 1) * r] if t < 3 else ow_ref[...]
        k = r // 3
        own[t ^ q, 0:k] = up[t * k:(t + 1) * k]
        own[t ^ q, k:2 * k] = down_ref[t * k:(t + 1) * k, :]
    k = 4 * (r // 3)
    rest[0] = up[k:]
    rest[1] = down_ref[k:, :]
    first1[0:r, :] = own1[0]
    pieces = [v[...].reshape(1, -1).astype(F32) for v in vectors]
    blank = jnp.zeros((1, first1.shape[1] - r), F32)
    rows = [jnp.concatenate([p, blank], 1) for p in pieces[:8]]
    rows += [jnp.concatenate([pieces[8][:, k * r:(k + 1) * r], blank], 1) for k in range(4)]
    rows.append(jnp.zeros((4, first1.shape[1]), F32))
    first1[r:r + 16, :] = jnp.concatenate(rows, 0).astype(BF16)
    first[...] = own[0]


def pack(ids, at, ow, up, down, vectors):
    r, width = ow.shape
    s = lambda *shape: jax.ShapeDtypeStruct(shape, BF16)
    return staged(pack_kernel, ids, [at, ow, up, down, *vectors],
                  [s(4, r, width), s(r + 16, width), s(4, 2 * r // 3, width), s(2 * r // 3, width), s(2, 8 * r // 3, width)],
                  "pack")


def after(value, *before):
    return lax.optimization_barrier((value, before))[0]


def line(ids, own, first, zr, xr):
    r, width = own.shape[1:]

    def kernel(ids, own, first, z1, z2, z3, x1, x2, x3, mine):
        zs, xs = (z1, z2, z3), (x1, x2, x3)
        for m in range(4):
            mine[m * r:(m + 1) * r] = own[m]
        mine[16 * r:16 * r + 16] = first[r:r + 16]
        for a in range(1, 4):
            at = 4 * a * r
            mine[at:at + r] = zs[a - 1][0:r]
            mine[16 * r + 16 * a:16 * r + 16 * a + 16] = zs[a - 1][r:r + 16]
            for m in range(1, 4):
                mine[at + m * r:at + (m + 1) * r] = xs[m - 1][a - 1]

    return simple(kernel, ids, [own, first, *zr, *xr], [jax.ShapeDtypeStruct((16 * r + 64, width), BF16)], "line")[0]


def stack_rows(ids, arrays, spans):
    width = arrays[0].shape[1]

    def kernel(ids, *refs):
        for out, (low, high) in zip(refs[3:], spans):
            for a in range(3):
                out[a] = refs[a][low:high]

    return simple(kernel, ids, arrays,
                  [jax.ShapeDtypeStruct((3, high - low, width), BF16) for low, high in spans], "stack")


def early_kernel(seq, pad, counts, depth, x_ref, cot_ref, norm_ref, gm_ref, xs):
    i = pl.program_id(0)
    width = x_ref.shape[-1]
    ok = lax.broadcasted_iota(jnp.int32, (pad, 1), 0) < counts[i]
    xs[pad - 8:pad, :] = jnp.zeros((8, width), F32)
    xs[0:seq, :] = cot_ref[0].astype(F32)
    gm_ref[0] = jnp.where(ok, xs[...] * depth[i, 1], 0.0).astype(BF16)
    xs[0:seq, :] = x_ref[0].astype(F32)
    norm_ref[0], _ = normalize(xs[...])


def early(counts, depth, images, cot, pad):
    n, seq, width = images.shape
    sd = jax.ShapeDtypeStruct
    return pl.pallas_call(
        functools.partial(early_kernel, seq, pad),
        out_shape=[sd((n, pad, width), F32), sd((n, pad, width), BF16)],
        grid_spec=pltpu.PrefetchScalarGridSpec(
            num_scalar_prefetch=2, grid=(n,),
            in_specs=[by_image((seq, width)), by_image((seq, width))],
            out_specs=[by_image((pad, width)), by_image((pad, width))],
            scratch_shapes=[pltpu.VMEM((pad, width), F32)]),
        compiler_params=params(16),
        cost_estimate=pl.CostEstimate(flops=10 ** 7, bytes_accessed=9 * MIB, transcendentals=0),
        name="early",
    )(counts, depth, images, cot)


def head_kernel(pad, ids, counts, mine, sib, norm_ref, at_out, ow_out, vec_ref, b2_ref, b3_ref,
                a1_ref, qkv_ref, o_ref, lse_ref, at_s, ow_s, lse_s, sems):
    q, z, c = ids[0], ids[1], ids[2]
    copies = [pltpu.make_async_copy(at_s, at_out, sems.at[0]), pltpu.make_async_copy(ow_s, ow_out, sems.at[1])]
    step = pl.program_id(0)

    @pl.when(step == 0)
    def _():
        r = ow_s.shape[0] // 8
        cut = b2_ref.shape[2]
        for j in range(8):
            a = (j >> 1) ^ z
            own = ((j & 1) ^ c) == 0

            def place(ref_in):
                small = ref_in[pl.ds(pl.multiple_of(16 * r + 16 * a, 16), 16), 0:r].astype(F32)
                vec_ref[0:8, j * r:(j + 1) * r] = small[0:8]
                for k in range(4):
                    row = small[8 + k:9 + k]
                    at, to = k * r, (k + 1) * r
                    if at < cut:
                        b2_ref[j, :, at:min(to, cut)] = row[:, 0:min(to, cut) - at]
                    if to > cut:
                        b3_ref[j, :, max(at, cut) - cut:to - cut] = row[:, max(at, cut) - at:]
                for t in range(4):
                    ref, at = (ow_s, j * r) if t == 3 else (at_s, (3 * j + t) * r)
                    ref[at:at + r, :] = ref_in[pl.ds(pl.multiple_of((4 * a + (t ^ q)) * r, r), r), :]

            @pl.when(own)
            def _():
                place(mine)

            @pl.when(jnp.logical_not(own))
            def _():
                place(sib)

        for copy in copies:
            copy.start()

    attend_image(pad, counts[step], norm_ref[0], at_s, vec_ref, a1_ref, qkv_ref, o_ref, lse_ref, lse_s)

    @pl.when(step == pl.num_programs(0) - 1)
    def _():
        for copy in copies:
            copy.wait()


def head(ids, counts, mine, sib, norm):
    n, pad, width = norm.shape
    r = width // 8
    cut = 4 * r // 3
    sd = jax.ShapeDtypeStruct
    far = pl.BlockSpec(memory_space=pl.ANY)
    return pl.pallas_call(
        functools.partial(head_kernel, pad),
        out_shape=[
            sd((24 * r, width), BF16), sd((8 * r, width), BF16), sd((8, width), F32), sd((8, 1, cut), F32),
            sd((8, 1, 4 * r - cut), F32),
            sd((n, pad, width), BF16), sd((n, pad, 3 * width), BF16),
            sd((n, pad, width), BF16), sd((n, 16, pad), F32),
        ],
        grid_spec=pltpu.PrefetchScalarGridSpec(
            num_scalar_prefetch=2, grid=(n,),
            in_specs=[whole(mine.shape), whole(sib.shape), by_image((pad, width))],
            out_specs=[
                far, far, whole((8, width)), whole((8, 1, cut)), whole((8, 1, 4 * r - cut)),
                by_image((pad, width)), by_image((pad, 3 * width)),
                by_image((pad, width)), by_image((16, pad)),
            ],
            scratch_shapes=[
                pltpu.VMEM((24 * r, width), BF16), pltpu.VMEM((8 * r, width), BF16),
                pltpu.VMEM((pad, 128), F32), pltpu.SemaphoreType.DMA((2,))]),
        compiler_params=params(60),
        cost_estimate=pl.CostEstimate(
            flops=2 * n * pad * width * (3 * width + 4 * pad), bytes_accessed=20 * MIB,
            transcendentals=n * 12 * pad * pad),
        name="head",
    )(ids, counts, mine, sib, norm)


def part_kernel(seq, pad, second, group, ids, counts, depth, a2_ref, gm_ref, *rest):
    if second:
        weights, bu_ref, *rest = rest
    else:
        sides, bu_ref, rest = (rest[0:5], rest[5:10]), rest[10], rest[11:]
    if second:
        (mlp_in, ga2_in, a2t_in, gmt_in, x1_in, cot_ref, vecs,
         both, gbu_ref, y_ref, vec_ref, gx_out, ga_out,
         a2t, gmt, mlp, ga2, hs, gus, mlp_s, ga2_s, x1_s, ga_s, cs, sems, out_sems) = rest
        loads = [pltpu.make_async_copy(a, b, sems.at[k]) for k, (a, b) in enumerate(
            ((a2t_in, a2t), (gmt_in, gmt), (mlp_in, mlp_s), (ga2_in, ga2_s), (x1_in, x1_s)))]
    else:
        both, gbu_ref, mlp_out, ga2_out, a2t_out, gmt_out, a2t, gmt, mlp, ga2, hs, gus, sems = rest
        stores = [pltpu.make_async_copy(a, b, sems.at[k]) for k, (a, b) in enumerate(
            ((a2t, a2t_out), (gmt, gmt_out), (mlp, mlp_out), (ga2, ga2_out)))]
    step = pl.program_id(0)
    end = pl.num_programs(0) - 1
    q, z, c = ids[0], ids[1], ids[2]
    rows, width = a2_ref.shape
    n = rows // pad
    block = bu_ref.shape[-1]

    @pl.when(step == 0)
    def _():
        if second:
            for copy in loads:
                copy.start()
        else:
            a2t[...] = jnp.transpose(a2_ref[...])
            gmt[...] = jnp.transpose(gm_ref[...])
            stores[0].start()
            stores[1].start()
        mlp[...] = jnp.zeros_like(mlp)
        ga2[...] = jnp.zeros_like(ga2)

    pairs = [(k, side) for k in range(group) for side in range(2)]
    owners = [(((step * group + k) ^ z) << 1) | (c ^ side) for k, side in pairs]
    def piece(k, side, t, low):
        own, message, *crossed = sides[side]
        slot, m = step * group + k, t ^ q
        at = slice(low, low + r)
        index = jnp.maximum(slot - 1, 0) if group > 1 else 0
        value = message[index, at]
        for x, ref in enumerate(crossed):
            value = jnp.where(m == x + 1, ref[index, at], value)
        return jnp.where(slot == 0, own[m, at], value)

    if second:
        up, down = (jnp.concatenate([weights[c, kind], weights[c ^ 1, kind]], 0) for kind in range(2))
    else:
        r = sides[0][0].shape[1] // 2
        up = jnp.concatenate([piece(k, side, t, 0) for k, side in pairs for t in range(4)], 0)
        down = jnp.concatenate([piece(k, side, t, r) for k, side in pairs for t in range(4)], 0)
    bu = jnp.concatenate([bu_ref[owner] for owner in owners], 1)
    gbu = jnp.zeros(bu.shape, F32)
    for i in range(n):
        at = slice(i * pad, (i + 1) * pad)
        u = nt(a2_ref[at, :], up) + bu
        t = nt(gm_ref[at, :], down)
        act, slope = gelu_pair(u)
        h = act.astype(BF16)
        gu = (t * slope).astype(BF16)
        hs[at, :] = h
        gus[at, :] = gu
        gbu = gbu + col_sum(gu.astype(F32))
        mlp[at, :] += nn(h, down)
        ga2[at, :] += nn(gu, up)
    for p, owner in enumerate(owners):
        gbu_ref[owner] = gbu[:, p * block:(p + 1) * block]

    if second:
        @pl.when(step == 0)
        def _():
            loads[0].wait()
            loads[1].wait()
    else:
        @pl.when(step == end)
        def _():
            stores[2].start()
            stores[3].start()

    part = width // 4
    span = 2 * group
    for t in range(4):
        at = slice(t * part, (t + 1) * part)
        for kind, (left, right) in enumerate(((a2t, gus), (gmt, hs))):
            d = nn(left[at, :], right[...]).astype(BF16)
            for p, owner in enumerate(owners):
                both[owner % span, t, kind] = d[:, p * block:(p + 1) * block]

    if not second:
        @pl.when(step == end)
        def _():
            for copy in stores:
                copy.wait()
        return

    @pl.when(step == end)
    def _():
        for copy in loads[2:]:
            copy.wait()
        mask_rows = lax.broadcasted_iota(jnp.int32, (pad, 1), 0)
        cs[pad - 8:pad, :] = jnp.zeros((8, width), F32)
        sums = [jnp.zeros((1, width), F32)] * 5
        outs = []
        for i in range(n):
            at = slice(i * pad, (i + 1) * pad)
            ok = mask_rows < counts[i]
            x1 = x1_s[i]
            out = mlp[at, :] + mlp_s[at, :] + vecs[7:8, :]
            y_ref[i] = jnp.where(ok, x1 + depth[i, 1] * out, 0.0).astype(BF16)[0:seq]
            cs[0:seq, :] = cot_ref[i].astype(F32)
            g = jnp.where(ok, cs[...], 0.0)
            back = ga2[at, :] + ga2_s[at, :]
            normed, rstd = normalize(x1)
            e = back * vecs[5:6, :]
            gx = g + rstd * (e - mean_row(e) - normed * mean_row(e * normed))
            ga = (depth[i, 0] * gx).astype(BF16)
            x1_s[i] = gx
            ga_s[i] = ga
            for k, (ref, to) in enumerate(((x1_s, gx_out), (ga_s, ga_out))):
                copy = pltpu.make_async_copy(ref.at[i], to.at[i], out_sems.at[i, k])
                copy.start()
                outs.append(copy)
            terms = (back * normed, back, gm_ref[at, :].astype(F32), ga.astype(F32), jnp.where(ok, out * out, 0.0))
            sums = [total + col_sum(term) for total, term in zip(sums, terms)]
        for k, total in enumerate(sums):
            vec_ref[k:k + 1, :] = total
        vec_ref[5:8, :] = jnp.zeros((3, width), F32)
        for copy in outs:
            copy.wait()


def part(ids, counts, depth, a2, gm, weights, bu, pad, group, carry=(), x1=None, cot=None, vec=None):
    rows, width = a2.shape
    n = rows // pad
    block = bu.shape[-1]
    second = len(carry) > 0
    sd = jax.ShapeDtypeStruct
    if second:
        w_specs = [pl.BlockSpec((2, 2, block, width), lambda s, ids, *_: (s ^ ids[1], 0, 0, 0))]
    else:
        w_specs = [whole(w.shape) for w in weights]
    far = pl.BlockSpec(memory_space=pl.ANY)
    acc = sd((rows, width), F32)
    tr = sd((width, rows), BF16)
    in_specs = [whole(a2.shape), whole(gm.shape)] + w_specs + [whole(bu.shape)]
    args = [a2, gm, *weights, bu]
    outs = [sd((8, 4, 2, width // 4, block), BF16), sd((8, 1, block), F32)]
    out_specs = [
        pl.BlockSpec((2 * group, 4, 2, width // 4, block), lambda s, ids, *_: (s ^ (ids[1] // group), 0, 0, 0, 0)),
        whole((8, 1, block))]
    scratch = [pltpu.VMEM(tr.shape, BF16), pltpu.VMEM(tr.shape, BF16), pltpu.VMEM(acc.shape, F32),
               pltpu.VMEM(acc.shape, F32), pltpu.VMEM((rows, 2 * group * block), BF16),
               pltpu.VMEM((rows, 2 * group * block), BF16)]
    if second:
        seq = cot.shape[1]
        args += [*carry, x1, cot, vec]
        in_specs += [far] * 5 + [whole(cot.shape), whole(vec.shape)]
        outs += [sd((n, seq, width), BF16), sd((8, width), F32), sd((n, pad, width), F32), sd((n, pad, width), BF16)]
        out_specs += [whole((n, seq, width)), whole((8, width)), far, far]
        scratch += [pltpu.VMEM(acc.shape, F32), pltpu.VMEM(acc.shape, F32), pltpu.VMEM((n, pad, width), F32),
                    pltpu.VMEM((n, pad, width), BF16), pltpu.VMEM((pad, width), F32), pltpu.SemaphoreType.DMA((5,)),
                    pltpu.SemaphoreType.DMA((n, 2))]
    else:
        seq = 0
        outs += [acc, acc, tr, tr]
        out_specs += [far] * 4
        scratch += [pltpu.SemaphoreType.DMA((4,))]
    return pl.pallas_call(
        functools.partial(part_kernel, seq, pad, second, group),
        out_shape=outs,
        grid_spec=pltpu.PrefetchScalarGridSpec(
            num_scalar_prefetch=3, grid=(4 // group,), in_specs=in_specs, out_specs=out_specs,
            scratch_shapes=scratch),
        compiler_params=params(60),
        cost_estimate=pl.CostEstimate(
            flops=12 * rows * width * 8 * block, bytes_accessed=30 * MIB, transcendentals=0),
        name="feed_b" if second else "feed_a",
    )(ids, counts, depth, *args)


def grads_kernel(far_z, ids, g_ref, o_ref, a1_ref, ga_ref, near, far, cols_ref):
    s = pl.program_id(0)
    q, z, c = ids[0], ids[1], ids[2]
    r = near.shape[2]
    side = (z >> 1) ^ int(far_z)

    def put(value, j, t):
        a, m = ((j >> 1) ^ z) & 1, t ^ q
        own = ((j & 1) ^ c) == 0

        @pl.when(own)
        def _():
            near[m, a] = value

        @pl.when(jnp.logical_not(own))
        def _():
            far[m, a] = value

    @pl.when(s < 3)
    def _():
        g = g_ref[...]
        d = tn(g, a1_ref[...]).astype(BF16)
        cols_ref[...] = col_sum(g.astype(F32))
        for k in range(4):
            chunk = 4 * s + k
            put(d[k * r:(k + 1) * r], 4 * side + chunk // 3, chunk % 3)

    @pl.when(s >= 3)
    def _():
        d = tn(o_ref[...], ga_ref[...]).astype(BF16)
        for k in range(4):
            put(d[k * r:(k + 1) * r], 4 * side + k, 3)


def grads(ids, g, o, a1, ga, far_z, cols):
    rows, width = a1.shape
    r = width // 8
    block = 4 * r
    sd = jax.ShapeDtypeStruct
    side = lambda ids: (ids[1] >> 1) ^ int(far_z)
    column = lambda s, ids: (0, 3 * side(ids) + jnp.minimum(s, 2))
    kernel = functools.partial(grads_kernel, far_z)
    more = []
    if cols is not None:
        more = [cols]
        kernel = lambda ids, g, o, a1, ga, cols_in, *outs: grads_kernel(far_z, ids, g, o, a1, ga, *outs)
    return pl.pallas_call(
        kernel,
        out_shape=[sd((4, 2, r, width), BF16), sd((4, 2, r, width), BF16), sd((1, 3 * width), F32)],
        grid_spec=pltpu.PrefetchScalarGridSpec(
            num_scalar_prefetch=1, grid=(4,),
            in_specs=[
                pl.BlockSpec((rows, block), column),
                pl.BlockSpec((rows, block), lambda s, ids: (0, side(ids))),
                whole(a1.shape), whole(ga.shape)] + [pl.BlockSpec(memory_space=pl.ANY)] * len(more),
            out_specs=[whole((4, 2, r, width)), whole((4, 2, r, width)), pl.BlockSpec((1, block), column)]),
        input_output_aliases={5: 2} if more else {},
        compiler_params=params(60),
        cost_estimate=pl.CostEstimate(
            flops=4 * rows * width * width, bytes_accessed=12 * MIB, transcendentals=0),
        name="grads",
    )(ids, g, o, a1, ga, *more)


def final_kernel(seq, pad, g_ref, w_ref, x_ref, gx_ref, vecs, gi_ref, vec_ref, xs):
    i = pl.program_id(0)
    width = x_ref.shape[-1]
    grad = nn(g_ref[0], w_ref[...])
    xs[pad - 8:pad, :] = jnp.zeros((8, width), F32)
    xs[0:seq, :] = x_ref[0].astype(F32)
    normed, rstd = normalize(xs[...])

    @pl.when(i == 0)
    def _():
        vec_ref[...] = jnp.zeros_like(vec_ref)

    vec_ref[0:1, :] += col_sum(grad * normed)
    vec_ref[1:2, :] += col_sum(grad)
    e = grad * vecs[0:1, :]
    gi = gx_ref[0] + rstd * (e - mean_row(e) - normed * mean_row(e * normed))
    gi_ref[0] = gi[0:seq]


def final(g, w, images, gx, vec, pad):
    n, seq, width = images.shape
    sd = jax.ShapeDtypeStruct
    return pl.pallas_call(
        functools.partial(final_kernel, seq, pad),
        out_shape=[sd((n, seq, width), F32), sd((8, width), F32)],
        grid=(n,),
        in_specs=[by_image((pad, 3 * width)), whole(w.shape), by_image((seq, width)), by_image((pad, width)),
                  whole(vec.shape)],
        out_specs=[by_image((seq, width)), whole((8, width))],
        scratch_shapes=[pltpu.VMEM((pad, width), F32)],
        compiler_params=params(60),
        cost_estimate=pl.CostEstimate(
            flops=6 * n * pad * width * width, bytes_accessed=18 * MIB, transcendentals=0),
        name="final",
    )(g, w, images, gx, vec)


def add_pair(ids, near, got):
    slots, parts = near.shape[:2]
    shape = near.shape[1:]
    block = pl.BlockSpec((slots, 1) + shape[1:], lambda a, *_: (0, a) + (0,) * (len(shape) - 1))

    def kernel(a_ref, b_ref, *outs):
        for m in range(4):
            outs[m][...] = (a_ref[m].astype(F32) + b_ref[m].astype(F32)).astype(BF16)

    return pl.pallas_call(
        kernel,
        out_shape=[jax.ShapeDtypeStruct(shape, BF16)] * slots,
        grid=(parts,),
        in_specs=[block, block],
        out_specs=[pl.BlockSpec((1,) + shape[1:], lambda a: (a,) + (0,) * (len(shape) - 1))] * slots,
        compiler_params=params(60),
        cost_estimate=pl.CostEstimate(flops=0, bytes_accessed=6 * near.size, transcendentals=0),
        name="add_pair",
    )(near, got)


def add_four(ids, parts, split):
    shape = parts[0].shape

    def kernel(ids, a, b, c, d, *outs):
        if split:
            for k in range(shape[0]):
                outs[k][...] = ((a[k].astype(F32) + b[k].astype(F32)) + (c[k].astype(F32) + d[k].astype(F32))).astype(BF16)
        else:
            outs[0][...] = ((a[...].astype(F32) + b[...].astype(F32)) + (c[...].astype(F32) + d[...].astype(F32))).astype(BF16)

    count = shape[0] if split else 1
    out = jax.ShapeDtypeStruct(shape[1:] if split else shape, BF16)
    return simple(kernel, ids, parts, [out] * count, "add_four")


def merge(ids, s2, s3):
    _, _, rows, k2 = s2.shape
    k3 = s3.shape[3]

    def kernel(ids, a, b, out):
        for ref, at, to in ((a, 0, k2), (b, k2, k2 + k3)):
            out[:, :, at:to] = ((ref[0].astype(F32) + ref[1].astype(F32)) + (ref[2].astype(F32) + ref[3].astype(F32))).astype(BF16)

    return simple(kernel, ids, [s2, s3], [jax.ShapeDtypeStruct((2, rows, k2 + k3), BF16)], "merge")[0]


def place_feed_kernel(ids, p0, p1, p2, p3, up_ref, down_ref, cs):
    q = ids[0]
    rows = p0.shape[1]
    for m, p in enumerate((p0, p1, p2, p3)):
        to = pl.ds(pl.multiple_of((q ^ m) * rows, rows), rows)
        up_ref[to, :] = p[0].astype(F32)
        cs[to, :] = p[1].astype(F32)
    down_ref[...] = jnp.transpose(cs[...])


def place_feed(ids, parts):
    _, rows, block = parts[0].shape
    sd = jax.ShapeDtypeStruct
    return simple(place_feed_kernel, ids, parts, [sd((4 * rows, block), F32), sd((block, 4 * rows), F32)],
                  "place_feed", scratch=[pltpu.VMEM((4 * rows, block), F32)])


def place_attend_kernel(ids, p0, p1, p2, p3, at_ref, ow_ref, cs):
    q = ids[0]
    r = p0.shape[0]
    for m, p in enumerate((p0, p1, p2, p3)):
        cs[pl.ds(pl.multiple_of((q ^ m) * r, r), r), :] = p[...].astype(F32)
    at_ref[...] = cs[0:3 * r, :]
    ow_ref[...] = cs[3 * r:4 * r, :]


def place_attend(ids, parts):
    r, width = parts[0].shape
    sd = jax.ShapeDtypeStruct
    return simple(place_attend_kernel, ids, parts, [sd((3 * r, width), F32), sd((r, width), F32)],
                  "place_attend", scratch=[pltpu.VMEM((4 * r, width), F32)])


def cut_vectors(ids, rows, share):
    width = rows.shape[1]
    parts = width // share

    def kernel(ids, rows_ref, *outs):
        owner = 2 * ids[1] + ids[2]
        vectors, bias = outs[:8], outs[8]
        for j in range(parts):
            @pl.when(owner == j)
            def _():
                for k in range(8):
                    vectors[k][...] = rows_ref[k:k + 1, j * share:(j + 1) * share].reshape(share)
                at = j * 4 * share
                bias[...] = rows_ref[8 + at // width:9 + at // width, at % width:at % width + 4 * share].reshape(4 * share)

    sd = jax.ShapeDtypeStruct
    return simple(kernel, ids, [rows], [sd((share,), F32)] * 8 + [sd((4 * share,), F32)], "cut_vectors")


def shards_grid(
    images, grid_sizes, keep_flags, attn_gain, attn_shift, attend_weight, query_bias, value_bias,
    output_weight, output_bias, mlp_gain, mlp_shift, up_weight, up_bias, down_weight, down_bias,
    cotangent,
):
    n, seq, width = images.shape
    pad = -(-seq // 32) * 32
    counts = grid_sizes[:, 0] * grid_sizes[:, 1] + 2
    depth = keep_flags.astype(F32) / KEEP_PROB
    owners = 8
    share = attn_gain.shape[0]
    f = lax.axis_index("fsdp")
    ids = jnp.stack([lax.axis_index("dp"), f >> 1, f & 1]).astype(jnp.int32)

    z_all = lambda array: [over_z(array, a) for a in (1, 2, 3)]
    dp_all = lambda array: [over_dp(array, m) for m in (1, 2, 3)]
    dp_out = lambda s: [s[0]] + [over_dp(s[m], m) for m in (1, 2, 3)]
    z_out = lambda s: [s[0]] + [over_z(s[a], a) for a in (1, 2, 3)]
    tied = lax.optimization_barrier
    flat = lambda array: array.reshape(n * pad, array.shape[-1])

    own1, first1, own, first, rest = pack(
        ids, attend_weight.T, output_weight, up_weight, down_weight,
        [attn_gain, attn_shift, query_bias, value_bias, output_bias, mlp_gain, mlp_shift, down_bias, up_bias])
    zr1 = z_all(first1)
    own_other = over_core(own)
    first, rest, zr1, own_other = tied((first, rest, zr1, own_other))
    message1, = stack_rows(ids, zr1, [(0, share)])
    xr1 = dp_all(message1)
    zr = z_all(first)
    weights_b = lax.all_gather(rest[None], "fsdp", axis=0, tiled=True)
    norm, gm = early(counts, depth, images, cotangent, pad)
    xr1, zr, norm, gm = tied((xr1, zr, norm, gm))
    mine1 = line(ids, own1, first1, zr1, xr1)
    sib1 = over_core(mine1)
    message, = stack_rows(ids, zr, [(0, first.shape[0])])
    message_other = over_core(message)
    xr = dp_all(message)
    sib1, message_other = tied((sib1, message_other))
    attend, out_w, vec, bu2, bu3, a1, qkv, o, lse = head(ids, counts, mine1, sib1, norm)
    o, xr = tied((o, xr))
    sib = [own_other, message_other, *(over_core(x) for x in xr)]
    x1, a2, sums_two = middle(counts, depth, o, images, out_w, vec, pad)
    x1, a2, sib = tied((x1, a2, sib))
    a2, gm = flat(a2), flat(gm)
    both2, gbu2, mlp, ga2, a2t, gmt = part(
        ids, counts, depth, a2, gm, [own, message, *xr, *sib], bu2, pad, 2)
    mlp, weights_b = tied((mlp, weights_b))

    own_sum = lambda both: lax.psum_scatter(
        both.reshape(-1, both.shape[-1]), "fsdp", scatter_dimension=0, tiled=True).reshape(both.shape[1:])
    quarter = lambda shard: lax.all_to_all(shard, "dp", 0, 0, tiled=True)
    shard2 = own_sum(both2)
    both3, gbu3, y, vec_feed, gx, ga = part(
        ids, counts, depth, a2, gm, [weights_b], bu3, pad, 1, (mlp, ga2, a2t, gmt), x1, cotangent, vec)
    shard3 = own_sum(both3)
    quarter2 = quarter(after(shard2, ga))
    g = back(counts, ga, out_w, qkv, lse)
    g, quarter2 = tied((g, quarter2))
    near_p, far_p, cols = grads(ids, flat(g), flat(o), flat(a1), flat(ga), True, None)
    got_p = over_core(far_p)
    near_q, far_q, cols = grads(ids, flat(after(g, near_p)), flat(o), flat(a1), flat(ga), False, cols)
    near_q, far_q, got_p = tied((near_q, far_q, got_p))
    got_q = over_core(far_q)
    s_p = add_pair(ids, near_p, got_p)
    dr_p = dp_out(s_p)
    gi, vec_last = final(after(g, s_p), attend, images, gx, vec, pad)
    rows = jnp.concatenate([
        vec_last[0:2], cols[:, :width], cols[:, 2 * width:], vec_feed[3:4], vec_feed[0:3],
        jnp.concatenate([gbu2[:, 0], gbu3[:, 0]], 1).reshape(4, width), sums_two[:, 0:2].sum(0), vec_feed[4:5],
        jnp.full((1, width), jnp.sum(counts).astype(F32)),
    ], 0)
    s_q = add_pair(ids, near_q, after(got_q, gi))
    rows = rows + over_core(rows)
    s_q, rows, dr_p = tied((s_q, rows, dr_p))
    dr_q = dp_out(s_q)
    e_p = add_four(ids, dr_p, True)
    er_p = [over_z(e_p[0], 2), over_z(e_p[1], 3)]
    quarter3 = quarter(after(shard3, er_p[0]))
    er_p, dr_q, rows = tied((er_p, dr_q, rows))
    e_q = add_four(ids, dr_q, True)
    er_q = over_z(e_q[1], 1)
    got = dp_all(rows)
    rows = (rows + got[0]) + (got[1] + got[2])
    er_q, rows = tied((er_q, rows))
    f1 = add_four(ids, [e_q[0], er_q, *er_p], False)[0]
    fr1 = [f1] + dp_all(f1)
    got = z_all(after(rows, f1))
    rows = (rows + got[0]) + (got[1] + got[2])
    fr1, rows, y, gi = tied((fr1, rows, y, gi))
    f3 = merge(ids, quarter2, after(quarter3, f1))
    fr3 = [f3] + dp_all(f3)
    root_means = jnp.sqrt(jnp.sum(rows[12:15], 1) / (rows[15, 0] * width))
    *tv, gub = cut_vectors(ids, rows, share)
    gattend, gout = place_attend(ids, fr1)
    gattend = gattend.T
    gup, gdown = place_feed(ids, fr3)
    return (y, gi, tv[0], tv[1], gattend, tv[2], tv[3], gout, tv[4], tv[5], tv[6],
            gup, gub, gdown, tv[7], root_means)


def shards(on_grid, *args):
    images, attn_gain, up_weight = args[0], args[3], args[12]
    share = attn_gain.shape[0]
    fits = on_grid and share % 48 == 0 and up_weight.shape[1] == 4 * share and images.shape[2] == 8 * share
    return (shards_grid if fits else shards_any)(*args)


def solution(mesh):
    images = P(("dp", "fsdp"), None, None)
    flags = P(("dp", "fsdp"), None)
    vec, rows, cols = P("fsdp"), P("fsdp", None), P(None, "fsdp")
    return jax.shard_map(
        functools.partial(shards, dict(mesh.shape) == {"dp": 4, "fsdp": 8}),
        mesh=mesh,
        in_specs=(images, flags, flags, vec, vec, cols, vec, vec, rows, vec, vec, vec, cols, vec, rows,
                  vec, images),
        out_specs=(images, images, vec, vec, cols, vec, vec, rows, vec, vec, vec, cols, vec, rows, vec,
                   P()),
        check_vma=False,
    )
```

```python
import functools
import math

import jax
import jax.numpy as jnp
from jax import lax
from jax.experimental import pallas as pl
from jax.experimental.pallas import tpu as pltpu
from jax.sharding import PartitionSpec as P

HEAD_DIM = 64
EPS = 1e-06
KEEP_PROB = 0.9
MASKED = -1e30
INV_ROOT_TWO = 0.7071067811865476
INV_ROOT_TWO_PI = 0.3989422804014327
F32 = jnp.float32
BF16 = jnp.bfloat16
MIB = 1024 * 1024


def nn(left, right):
    return lax.dot_general(left, right, (((1,), (0,)), ((), ())), preferred_element_type=F32)


def nt(left, right):
    return lax.dot_general(left, right, (((1,), (1,)), ((), ())), preferred_element_type=F32)


def tn(left, right):
    return lax.dot_general(left, right, (((0,), (0,)), ((), ())), preferred_element_type=F32)


def mean_row(values):
    return jnp.sum(values, -1, keepdims=True) * (1.0 / values.shape[-1])


def normalize(values):
    center = values - mean_row(values)
    rstd = lax.rsqrt(mean_row(center * center) + EPS)
    return center * rstd, rstd


def col_sum(values):
    return jnp.sum(values, 0, keepdims=True)


def params(limit, steps=1):
    return pltpu.CompilerParams(
        dimension_semantics=("arbitrary",) * steps, vmem_limit_bytes=limit * MIB
    )


def whole(shape, buffers=1):
    zeros = (0,) * len(shape)
    return pl.BlockSpec(shape, lambda *_: zeros, pipeline_mode=pl.Buffered(buffers))


def by_image(shape):
    rest = (0,) * len(shape)
    return pl.BlockSpec((1,) + shape, lambda i, *_: (i,) + rest)


SMEM = pl.BlockSpec(memory_space=pltpu.SMEM)


def front_kernel(seq, pad, counts, depth, x_ref, cot_ref, w_ref, vec_ref,
                 a1_ref, gm_ref, qkv_ref, o_ref, lse_ref, xs, lse_s):
    i = pl.program_id(0)
    width = x_ref.shape[-1]
    count = counts[i]
    rows = lax.broadcasted_iota(jnp.int32, (pad, 1), 0)
    xs[pad - 8:pad, :] = jnp.zeros((8, width), F32)
    xs[0:seq, :] = cot_ref[0].astype(F32)
    gm_ref[0] = jnp.where(rows < count, xs[...] * depth[i, 1], 0.0).astype(BF16)
    xs[0:seq, :] = x_ref[0].astype(F32)
    normed, _ = normalize(xs[...])
    attend_image(pad, count, normed, w_ref, vec_ref, a1_ref, qkv_ref, o_ref, lse_ref, lse_s)


def attend_image(pad, count, normed, w_ref, vec_ref, a1_ref, qkv_ref, o_ref, lse_ref, lse_s):
    width = normed.shape[-1]
    pairs = width // 128
    a1 = (normed * vec_ref[0:1, :] + vec_ref[1:2, :]).astype(BF16)
    a1_ref[0] = a1
    for c in range(0, 3 * width, 384):
        part = nt(a1, w_ref[c:c + 384, :])
        if c < width:
            part = part + vec_ref[2:3, c:c + 384]
        elif c >= 2 * width:
            part = part + vec_ref[3:4, c - 2 * width:c - 2 * width + 384]
        qkv_ref[0, :, c:c + 384] = part.astype(BF16)
    ok = lax.broadcasted_iota(jnp.int32, (pad, pad), 1) < count
    lane = lax.broadcasted_iota(jnp.int32, (pad, 128), 1)
    lse_s[...] = jnp.zeros((pad, 128), F32)

    def pair(p):
        at = pl.multiple_of(p * 128, 128)
        q = qkv_ref[0, :, pl.ds(at, 128)] * 0.125
        k = qkv_ref[0, :, pl.ds(width + at, 128)]
        v = qkv_ref[0, :, pl.ds(2 * width + at, 128)]
        total = jnp.zeros((pad, 128), F32)
        for half in range(2):
            mine = (lane >= 64) if half else (lane < 64)
            scores = jnp.where(ok, nt(jnp.where(mine, q, 0), k), MASKED)
            top = jnp.max(scores, -1, keepdims=True)
            e = jnp.exp(scores - top)
            s = jnp.sum(e, -1, keepdims=True)
            prob = (e * (1.0 / s)).astype(BF16)
            total = total + nn(prob, jnp.where(mine, v, 0))
            lse_s[...] = jnp.where(lane == 2 * p + half, top + jnp.log(s), lse_s[...])
        o_ref[0, :, pl.ds(at, 128)] = total.astype(BF16)

    for p in range(pairs):
        pair(p)
    lse_ref[0] = jnp.transpose(lse_s[...])[0:16, :]


def front(counts, depth, images, cot, w, vec, pad):
    n, seq, width = images.shape
    grid_spec = pltpu.PrefetchScalarGridSpec(
        num_scalar_prefetch=2,
        grid=(n,),
        in_specs=[
            by_image((seq, width)), by_image((seq, width)),
            whole(w.shape), whole(vec.shape),
        ],
        out_specs=[
            by_image((pad, width)), by_image((pad, width)), by_image((pad, 3 * width)),
            by_image((pad, width)), by_image((16, pad)),
        ],
        scratch_shapes=[pltpu.VMEM((pad, width), F32), pltpu.VMEM((pad, 128), F32)],
    )
    return pl.pallas_call(
        functools.partial(front_kernel, seq, pad),
        out_shape=[
            jax.ShapeDtypeStruct((n, pad, width), BF16),
            jax.ShapeDtypeStruct((n, pad, width), BF16),
            jax.ShapeDtypeStruct((n, pad, 3 * width), BF16),
            jax.ShapeDtypeStruct((n, pad, width), BF16),
            jax.ShapeDtypeStruct((n, 16, pad), F32),
        ],
        grid_spec=grid_spec,
        compiler_params=params(60),
        cost_estimate=pl.CostEstimate(
            flops=2 * n * pad * width * (3 * width + 4 * pad), bytes_accessed=20 * MIB,
            transcendentals=n * 12 * pad * pad),
        name="front",
    )(counts, depth, images, cot, w, vec)


def middle_kernel(seq, pad, counts, depth, o_ref, x_ref, w_ref, vec_ref,
                  x1_ref, a2_ref, sums_ref, xs):
    i = pl.program_id(0)
    width = x_ref.shape[-1]
    rows = lax.broadcasted_iota(jnp.int32, (pad, 1), 0)
    ok = rows < counts[i]
    xs[pad - 8:pad, :] = jnp.zeros((8, width), F32)
    xs[0:seq, :] = x_ref[0].astype(F32)
    attn = nn(o_ref[0], w_ref[...]) + vec_ref[4:5, :]
    x1 = xs[...] + depth[i, 0] * attn
    x1_ref[0] = x1
    sums_ref[0, 0:1, :] = col_sum(jnp.where(ok, x1 * x1, 0.0))
    sums_ref[0, 1:2, :] = col_sum(jnp.where(ok, attn * attn, 0.0))
    sums_ref[0, 2:8, :] = jnp.zeros((6, width), F32)
    normed, _ = normalize(x1)
    a2_ref[0] = (normed * vec_ref[5:6, :] + vec_ref[6:7, :]).astype(BF16)


def middle(counts, depth, o, images, w, vec, pad):
    n, seq, width = images.shape
    grid_spec = pltpu.PrefetchScalarGridSpec(
        num_scalar_prefetch=2,
        grid=(n,),
        in_specs=[
            by_image((pad, width)), by_image((seq, width)),
            whole(w.shape), whole(vec.shape),
        ],
        out_specs=[by_image((pad, width)), by_image((pad, width)), by_image((8, width))],
        scratch_shapes=[pltpu.VMEM((pad, width), F32)],
    )
    return pl.pallas_call(
        functools.partial(middle_kernel, seq, pad),
        out_shape=[
            jax.ShapeDtypeStruct((n, pad, width), F32),
            jax.ShapeDtypeStruct((n, pad, width), BF16),
            jax.ShapeDtypeStruct((n, 8, width), F32),
        ],
        grid_spec=grid_spec,
        compiler_params=params(60),
        cost_estimate=pl.CostEstimate(
            flops=2 * n * pad * width * width, bytes_accessed=10 * MIB, transcendentals=0),
        name="middle",
    )(counts, depth, o, images, w, vec)


def gelu_pair(u):
    size = jnp.abs(u)
    t = 1.0 / (1.0 + (0.3275911 * INV_ROOT_TWO) * size)
    bell = jnp.exp(-0.5 * (u * u))
    series = t * (0.5 * 0.254829592 + t * (0.5 * -0.284496736 + t * (
        0.5 * 1.421413741 + t * (0.5 * -1.453152027 + t * (0.5 * 1.061405429)))))
    tail = series * bell
    phi = jnp.where(u >= 0, 1.0 - tail, tail)
    return u * phi, phi + u * (bell * INV_ROOT_TWO_PI)


def feed_kernel(seq, pad, counts, depth, a2_ref, gm_ref, up_ref, down_ref, bu_ref, x1_ref, cot_ref,
                vecs,
                dup_ref, ddown_ref, gbu_ref, y_ref, gx_ref, ga_ref, vec_ref,
                a2t, gmt, mlp, ga2, hs, gus, cs):
    j = pl.program_id(0)
    n = x1_ref.shape[0]

    @pl.when(j == 0)
    def _():
        a2t[...] = jnp.transpose(a2_ref[...])
        gmt[...] = jnp.transpose(gm_ref[...])
        mlp[...] = jnp.zeros_like(mlp)
        ga2[...] = jnp.zeros_like(ga2)

    gbu = jnp.zeros(bu_ref.shape[1:], F32)
    for i in range(n):
        at = slice(i * pad, (i + 1) * pad)
        u = nt(a2_ref[at, :], up_ref[...]) + bu_ref[0]
        t = nt(gm_ref[at, :], down_ref[...])
        act, slope = gelu_pair(u)
        h = act.astype(BF16)
        gu = (t * slope).astype(BF16)
        hs[at, :] = h
        gus[at, :] = gu
        gbu = gbu + col_sum(gu.astype(F32))
        mlp[at, :] += nn(h, down_ref[...])
        ga2[at, :] += nn(gu, up_ref[...])
    gbu_ref[0] = gbu
    dup_ref[0] = nn(a2t[...], gus[...]).astype(BF16)
    ddown_ref[0] = nn(gmt[...], hs[...]).astype(BF16)

    @pl.when(j == pl.num_programs(0) - 1)
    def _():
        width = x1_ref.shape[-1]
        rows = lax.broadcasted_iota(jnp.int32, (pad, 1), 0)
        cs[pad - 8:pad, :] = jnp.zeros((8, width), F32)
        msum = jnp.zeros((1, width), F32)
        ggain = jnp.zeros((1, width), F32)
        gshift = jnp.zeros((1, width), F32)
        gdown = jnp.zeros((1, width), F32)
        gout = jnp.zeros((1, width), F32)
        for i in range(n):
            at = slice(i * pad, (i + 1) * pad)
            ok = rows < counts[i]
            x1 = x1_ref[i]
            out = mlp[at, :] + vecs[7:8, :]
            msum = msum + col_sum(jnp.where(ok, out * out, 0.0))
            y_ref[i] = jnp.where(ok, x1 + depth[i, 1] * out, 0.0).astype(BF16)[0:seq]
            cs[0:seq, :] = cot_ref[i].astype(F32)
            g = jnp.where(ok, cs[...], 0.0)
            gdown = gdown + col_sum(gm_ref[at, :].astype(F32))
            back = ga2[at, :]
            normed, rstd = normalize(x1)
            ggain = ggain + col_sum(back * normed)
            gshift = gshift + col_sum(back)
            e = back * vecs[5:6, :]
            gx = g + rstd * (e - mean_row(e) - normed * mean_row(e * normed))
            gx_ref[i] = gx
            ga = (depth[i, 0] * gx).astype(BF16)
            ga_ref[i] = ga
            gout = gout + col_sum(ga.astype(F32))
        vec_ref[0:1, :] = ggain
        vec_ref[1:2, :] = gshift
        vec_ref[2:3, :] = gdown
        vec_ref[3:4, :] = gout
        vec_ref[4:5, :] = msum
        vec_ref[5:8, :] = jnp.zeros((3, width), F32)


def feed(counts, depth, a2, gm, up, down, bu, x1, cot, vec, seq, pad, block):
    rows, width = a2.shape
    n = rows // pad
    hidden = up.shape[0]
    steps = hidden // block
    at = lambda j, *_: (j, 0)
    at3 = lambda j, *_: (j, 0, 0)
    grid_spec = pltpu.PrefetchScalarGridSpec(
        num_scalar_prefetch=2,
        grid=(steps,),
        in_specs=[
            whole(a2.shape), whole(gm.shape),
            pl.BlockSpec((block, width), at), pl.BlockSpec((block, width), at),
            pl.BlockSpec((1, 1, block), at3),
            whole(x1.shape), whole(cot.shape), whole(vec.shape),
        ],
        out_specs=[
            pl.BlockSpec((1, width, block), at3), pl.BlockSpec((1, width, block), at3),
            pl.BlockSpec((1, 1, block), at3),
            whole((n, seq, width)), whole((n, pad, width)), whole((n, pad, width)), whole((8, width)),
        ],
        scratch_shapes=[
            pltpu.VMEM((width, rows), BF16), pltpu.VMEM((width, rows), BF16),
            pltpu.VMEM((rows, width), F32), pltpu.VMEM((rows, width), F32),
            pltpu.VMEM((rows, block), BF16), pltpu.VMEM((rows, block), BF16),
            pltpu.VMEM((pad, width), F32),
        ],
    )
    return pl.pallas_call(
        functools.partial(feed_kernel, seq, pad),
        out_shape=[
            jax.ShapeDtypeStruct((steps, width, block), BF16),
            jax.ShapeDtypeStruct((steps, width, block), BF16),
            jax.ShapeDtypeStruct((steps, 1, block), F32),
            jax.ShapeDtypeStruct((n, seq, width), BF16),
            jax.ShapeDtypeStruct((n, pad, width), F32),
            jax.ShapeDtypeStruct((n, pad, width), BF16),
            jax.ShapeDtypeStruct((8, width), F32),
        ],
        grid_spec=grid_spec,
        compiler_params=params(60),
        cost_estimate=pl.CostEstimate(
            flops=12 * rows * width * hidden, bytes_accessed=40 * MIB, transcendentals=rows * hidden),
        name="feed",
    )(counts, depth, a2, gm, up, down, bu.reshape(steps, 1, block), x1, cot, vec)


def back_kernel(pad, counts, ga_ref, w_ref, qkv_ref, lse_ref, g_ref, go):
    i = pl.program_id(0)
    width = ga_ref.shape[-1]
    count = counts[i]
    go[...] = nt(ga_ref[0], w_ref[...]).astype(BF16)
    ok = lax.broadcasted_iota(jnp.int32, (pad, pad), 0) < count
    lane = lax.broadcasted_iota(jnp.int32, (pad, 128), 1)

    def pair(p):
        at = pl.multiple_of(p * 128, 128)
        q = qkv_ref[0, :, pl.ds(at, 128)] * 0.125
        k = qkv_ref[0, :, pl.ds(width + at, 128)]
        v = qkv_ref[0, :, pl.ds(2 * width + at, 128)]
        g = go[:, pl.ds(at, 128)]
        gq = jnp.zeros((pad, 128), F32)
        gk = jnp.zeros((pad, 128), F32)
        gv = jnp.zeros((pad, 128), F32)
        for half in range(2):
            mine = (lane >= 64) if half else (lane < 64)
            qm = jnp.where(mine, q, 0)
            km = jnp.where(mine, k, 0) * 0.125
            gmine = jnp.where(mine, g, 0)
            scores = nt(k, qm)
            row = lse_ref[0, 2 * p + half:2 * p + half + 1, :]
            prob = jnp.where(ok, jnp.exp(scores - row), 0.0)
            dp = nt(v, gmine)
            inner = col_sum(prob * dp)
            ds = (prob * (dp - inner)).astype(BF16)
            gv = gv + nn(prob.astype(BF16), gmine)
            gk = gk + nn(ds, qm)
            gq = gq + tn(ds, km)
        g_ref[0, :, pl.ds(at, 128)] = gq.astype(BF16)
        g_ref[0, :, pl.ds(width + at, 128)] = gk.astype(BF16)
        g_ref[0, :, pl.ds(2 * width + at, 128)] = gv.astype(BF16)

    for p in range(width // 128):
        pair(p)


def back(counts, ga, w, qkv, lse):
    n, pad, width = ga.shape
    grid_spec = pltpu.PrefetchScalarGridSpec(
        num_scalar_prefetch=1,
        grid=(n,),
        in_specs=[by_image((pad, width)), whole(w.shape), by_image((pad, 3 * width)), by_image((16, pad))],
        out_specs=[by_image((pad, 3 * width))],
        scratch_shapes=[pltpu.VMEM((pad, width), BF16)],
    )
    return pl.pallas_call(
        functools.partial(back_kernel, pad),
        out_shape=[jax.ShapeDtypeStruct((n, pad, 3 * width), BF16)],
        grid_spec=grid_spec,
        compiler_params=params(60),
        cost_estimate=pl.CostEstimate(
            flops=2 * n * pad * width * (width + 10 * pad), bytes_accessed=16 * MIB,
            transcendentals=n * 12 * pad * pad),
        name="back",
    )(counts, ga, w, qkv, lse)[0]


def outgrad_kernel(o_ref, ga_ref, d_ref):
    d_ref[...] = tn(o_ref[...], ga_ref[...]).astype(BF16)


def outgrad(o, ga):
    rows, width = o.shape
    return pl.pallas_call(
        outgrad_kernel,
        out_shape=jax.ShapeDtypeStruct((width, width), BF16),
        grid=(2,),
        in_specs=[pl.BlockSpec((rows, width // 2), lambda j: (0, j)), whole(ga.shape)],
        out_specs=pl.BlockSpec((width // 2, width), lambda j: (j, 0)),
        compiler_params=params(60),
        cost_estimate=pl.CostEstimate(
            flops=2 * rows * width * width, bytes_accessed=6 * MIB, transcendentals=0),
        name="outgrad",
    )(o, ga)


def last_kernel(seq, pad, g_ref, a1_ref, w_ref, x_ref, gx_ref, vecs,
                d_ref, cols_ref, gi_ref, vec_ref, ga1, xs):
    c = pl.program_id(0)
    n = x_ref.shape[0]
    g = g_ref[...]
    d_ref[...] = tn(g, a1_ref[...]).astype(BF16)
    cols_ref[...] = col_sum(g.astype(F32))
    part = nn(g, w_ref[...])

    @pl.when(c == 0)
    def _():
        ga1[...] = part

    @pl.when(c > 0)
    def _():
        ga1[...] += part

    @pl.when(c == pl.num_programs(0) - 1)
    def _():
        width = x_ref.shape[-1]
        xs[pad - 8:pad, :] = jnp.zeros((8, width), F32)
        ggain = jnp.zeros((1, width), F32)
        gshift = jnp.zeros((1, width), F32)
        for i in range(n):
            xs[0:seq, :] = x_ref[i].astype(F32)
            normed, rstd = normalize(xs[...])
            grad = ga1[i * pad:(i + 1) * pad, :]
            ggain = ggain + col_sum(grad * normed)
            gshift = gshift + col_sum(grad)
            e = grad * vecs[0:1, :]
            gi = gx_ref[i] + rstd * (e - mean_row(e) - normed * mean_row(e * normed))
            gi_ref[i] = gi[0:seq]
        vec_ref[0:1, :] = ggain
        vec_ref[1:2, :] = gshift
        vec_ref[2:8, :] = jnp.zeros((6, width), F32)


def last(g, a1, w, images, gx, vec, pad, block=384):
    n, seq, width = images.shape
    rows, total = g.shape
    return pl.pallas_call(
        functools.partial(last_kernel, seq, pad),
        out_shape=[
            jax.ShapeDtypeStruct((total, width), BF16),
            jax.ShapeDtypeStruct((1, total), F32),
            jax.ShapeDtypeStruct((n, seq, width), F32),
            jax.ShapeDtypeStruct((8, width), F32),
        ],
        grid=(total // block,),
        in_specs=[
            pl.BlockSpec((rows, block), lambda c: (0, c)), whole(a1.shape),
            pl.BlockSpec((block, width), lambda c: (c, 0)), whole(images.shape), whole(gx.shape),
            whole(vec.shape),
        ],
        out_specs=[
            pl.BlockSpec((block, width), lambda c: (c, 0)), pl.BlockSpec((1, block), lambda c: (0, c)),
            whole((n, seq, width)), whole((8, width)),
        ],
        scratch_shapes=[pltpu.VMEM((rows, width), F32), pltpu.VMEM((pad, width), F32)],
        compiler_params=params(60),
        cost_estimate=pl.CostEstimate(
            flops=4 * rows * width * total, bytes_accessed=30 * MIB, transcendentals=0),
        name="last",
    )(g, a1, w, images, gx, vec)


def shards_any(
    images, grid_sizes, keep_flags, attn_gain, attn_shift, attend_weight, query_bias, value_bias,
    output_weight, output_bias, mlp_gain, mlp_shift, up_weight, up_bias, down_weight, down_bias,
    cotangent,
):
    n, seq, width = images.shape
    pad = -(-seq // 32) * 32
    counts = grid_sizes[:, 0] * grid_sizes[:, 1] + 2
    depth = keep_flags.astype(F32) / KEEP_PROB
    owners = width // attn_gain.shape[0]

    small = jnp.concatenate([
        attn_gain, attn_shift, query_bias, value_bias, output_bias, mlp_gain, mlp_shift, down_bias, up_bias])
    small = lax.all_gather(small.reshape(1, -1), "fsdp", axis=0, tiled=True).astype(F32)
    share = attn_gain.shape[0]
    vec = jnp.stack([small[:, k * share:(k + 1) * share].reshape(width) for k in range(8)])
    bu = small[:, 8 * share:].reshape(1, -1)

    attend = lax.all_gather(attend_weight.T, "fsdp", axis=0, tiled=True)
    out_w = lax.all_gather(output_weight, "fsdp", axis=0, tiled=True)
    up = lax.all_gather(up_weight.T, "fsdp", axis=0, tiled=True)
    down = lax.all_gather(down_weight, "fsdp", axis=0, tiled=True)

    a1, gm, qkv, o, lse = front(counts, depth, images, cotangent, attend, vec, pad)
    x1, a2, sums_two = middle(counts, depth, o, images, out_w, vec, pad)
    flat = lambda array: array.reshape(n * pad, array.shape[-1])
    block = up_weight.shape[1] if up_weight.shape[1] % 128 == 0 else 384
    dup, ddown, gbu, y, gx, ga, vec_feed = feed(
        counts, depth, flat(a2), flat(gm), up, down, bu, x1, cotangent, vec, seq, pad, block)
    dout = outgrad(flat(o), flat(ga))
    g = back(counts, ga, out_w, qkv, lse)
    dattend, cols, gi, vec_last = last(flat(g), flat(a1), attend, images, gx, vec, pad)

    sums = jnp.stack([jnp.sum(sums_two[:, 0]), jnp.sum(sums_two[:, 1]), jnp.sum(vec_feed[4]),
                      jnp.sum(counts).astype(F32)])

    def spread(array):
        return lax.psum(lax.psum_scatter(array, "fsdp", scatter_dimension=0, tiled=True), "dp")

    def columns(array):
        hidden = up.shape[0]
        array = jnp.swapaxes(array, 0, 1).reshape(width, owners, hidden // owners)
        return jnp.swapaxes(array, 0, 1)

    gup = spread(columns(dup))[0]
    gdown = spread(columns(ddown))[0].T
    gout = spread(dout)
    gattend = spread(dattend).T
    rows = jnp.concatenate([
        vec_last[0:2], cols[:, :width], cols[:, 2 * width:], vec_feed[3:4], vec_feed[0:3],
    ], 0)
    tiny = jnp.concatenate([
        jnp.swapaxes(rows.reshape(8, owners, share), 0, 1).reshape(owners, 8 * share),
        gbu.reshape(owners, -1)], 1)
    tiny = spread(tiny)[0]
    sums = lax.psum(sums, ("dp", "fsdp"))
    root_means = jnp.sqrt(sums[:3] / (sums[3] * width))
    tv = [tiny[k * share:(k + 1) * share] for k in range(8)]
    f = lambda array: array.astype(F32)
    return (y, gi, tv[0], tv[1], f(gattend), tv[2], tv[3], f(gout), tv[4], tv[5], tv[6],
            f(gup), tiny[8 * share:], f(gdown), tv[7], root_means)


def over_dp(array, m):
    return lax.ppermute(array, "dp", [(i, i ^ m) for i in range(4)])


def over_z(array, a):
    return lax.ppermute(array, "fsdp", [(i, i ^ (2 * a)) for i in range(8)])


def over_core(array):
    return lax.ppermute(array, "fsdp", [(i, i ^ 1) for i in range(8)])


def staged(kernel, ids, arrays, out_shape, name):
    size = sum(math.prod(s.shape) * s.dtype.itemsize for s in [*arrays, *out_shape])
    return pl.pallas_call(
        kernel,
        out_shape=out_shape,
        grid_spec=pltpu.PrefetchScalarGridSpec(
            num_scalar_prefetch=1, grid=(1,),
            in_specs=[whole(s.shape) for s in arrays],
            out_specs=[whole(s.shape) for s in out_shape]),
        compiler_params=params(60),
        cost_estimate=pl.CostEstimate(flops=0, bytes_accessed=size, transcendentals=0),
        name=name,
    )(ids, *arrays)


def simple(kernel, ids, arrays, out_shape, name, scratch=()):
    size = sum(math.prod(s.shape) * s.dtype.itemsize for s in [*arrays, *out_shape])
    inside = pl.BlockSpec(memory_space=pltpu.VMEM)
    return pl.pallas_call(
        kernel,
        out_shape=out_shape,
        in_specs=[SMEM] + [inside] * len(arrays),
        out_specs=[inside] * len(out_shape),
        scratch_shapes=list(scratch),
        compiler_params=pltpu.CompilerParams(vmem_limit_bytes=16 * MIB),
        cost_estimate=pl.CostEstimate(flops=0, bytes_accessed=size, transcendentals=0),
        name=name,
    )(ids, *arrays)


def pack_kernel(ids, at_ref, ow_ref, up_ref, down_ref, *refs):
    vectors, (own1, first1, own, first, rest) = refs[:9], refs[9:]
    q = ids[0]
    att = at_ref[...]
    up = jnp.transpose(up_ref[...])
    r = ow_ref.shape[0]
    for t in range(4):
        own1[t ^ q] = att[t * r:(t + 1) * r] if t < 3 else ow_ref[...]
        k = r // 3
        own[t ^ q, 0:k] = up[t * k:(t + 1) * k]
        own[t ^ q, k:2 * k] = down_ref[t * k:(t + 1) * k, :]
    k = 4 * (r // 3)
    rest[0] = up[k:]
    rest[1] = down_ref[k:, :]
    first1[0:r, :] = own1[0]
    pieces = [v[...].reshape(1, -1).astype(F32) for v in vectors]
    blank = jnp.zeros((1, first1.shape[1] - r), F32)
    rows = [jnp.concatenate([p, blank], 1) for p in pieces[:8]]
    rows += [jnp.concatenate([pieces[8][:, k * r:(k + 1) * r], blank], 1) for k in range(4)]
    rows.append(jnp.zeros((4, first1.shape[1]), F32))
    first1[r:r + 16, :] = jnp.concatenate(rows, 0).astype(BF16)
    first[...] = own[0]


def pack(ids, at, ow, up, down, vectors):
    r, width = ow.shape
    s = lambda *shape: jax.ShapeDtypeStruct(shape, BF16)
    return staged(pack_kernel, ids, [at, ow, up, down, *vectors],
                  [s(4, r, width), s(r + 16, width), s(4, 2 * r // 3, width), s(2 * r // 3, width), s(2, 8 * r // 3, width)],
                  "pack")


def after(value, *before):
    return lax.optimization_barrier((value, before))[0]


def line(ids, own, first, zr, xr):
    r, width = own.shape[1:]

    def kernel(ids, own, first, z1, z2, z3, x1, x2, x3, mine):
        zs, xs = (z1, z2, z3), (x1, x2, x3)
        for m in range(4):
            mine[m * r:(m + 1) * r] = own[m]
        mine[16 * r:16 * r + 16] = first[r:r + 16]
        for a in range(1, 4):
            at = 4 * a * r
            mine[at:at + r] = zs[a - 1][0:r]
            mine[16 * r + 16 * a:16 * r + 16 * a + 16] = zs[a - 1][r:r + 16]
            for m in range(1, 4):
                mine[at + m * r:at + (m + 1) * r] = xs[m - 1][a - 1]

    return simple(kernel, ids, [own, first, *zr, *xr], [jax.ShapeDtypeStruct((16 * r + 64, width), BF16)], "line")[0]


def stack_rows(ids, arrays, spans):
    width = arrays[0].shape[1]

    def kernel(ids, *refs):
        for out, (low, high) in zip(refs[3:], spans):
            for a in range(3):
                out[a] = refs[a][low:high]

    return simple(kernel, ids, arrays,
                  [jax.ShapeDtypeStruct((3, high - low, width), BF16) for low, high in spans], "stack")


def early_kernel(seq, pad, counts, depth, x_ref, cot_ref, norm_ref, gm_ref, xs):
    i = pl.program_id(0)
    width = x_ref.shape[-1]
    ok = lax.broadcasted_iota(jnp.int32, (pad, 1), 0) < counts[i]
    xs[pad - 8:pad, :] = jnp.zeros((8, width), F32)
    xs[0:seq, :] = cot_ref[0].astype(F32)
    gm_ref[0] = jnp.where(ok, xs[...] * depth[i, 1], 0.0).astype(BF16)
    xs[0:seq, :] = x_ref[0].astype(F32)
    norm_ref[0], _ = normalize(xs[...])


def early(counts, depth, images, cot, pad):
    n, seq, width = images.shape
    sd = jax.ShapeDtypeStruct
    return pl.pallas_call(
        functools.partial(early_kernel, seq, pad),
        out_shape=[sd((n, pad, width), F32), sd((n, pad, width), BF16)],
        grid_spec=pltpu.PrefetchScalarGridSpec(
            num_scalar_prefetch=2, grid=(n,),
            in_specs=[by_image((seq, width)), by_image((seq, width))],
            out_specs=[by_image((pad, width)), by_image((pad, width))],
            scratch_shapes=[pltpu.VMEM((pad, width), F32)]),
        compiler_params=params(16),
        cost_estimate=pl.CostEstimate(flops=10 ** 7, bytes_accessed=9 * MIB, transcendentals=0),
        name="early",
    )(counts, depth, images, cot)


def head_kernel(pad, ids, counts, mine, sib, norm_ref, at_out, ow_out, vec_ref, b2_ref, b3_ref,
                a1_ref, qkv_ref, o_ref, lse_ref, at_s, ow_s, lse_s, sems):
    q, z, c = ids[0], ids[1], ids[2]
    copies = [pltpu.make_async_copy(at_s, at_out, sems.at[0]), pltpu.make_async_copy(ow_s, ow_out, sems.at[1])]
    step = pl.program_id(0)

    @pl.when(step == 0)
    def _():
        r = ow_s.shape[0] // 8
        cut = b2_ref.shape[2]
        for j in range(8):
            a = (j >> 1) ^ z
            own = ((j & 1) ^ c) == 0

            def place(ref_in):
                small = ref_in[pl.ds(pl.multiple_of(16 * r + 16 * a, 16), 16), 0:r].astype(F32)
                vec_ref[0:8, j * r:(j + 1) * r] = small[0:8]
                for k in range(4):
                    row = small[8 + k:9 + k]
                    at, to = k * r, (k + 1) * r
                    if at < cut:
                        b2_ref[j, :, at:min(to, cut)] = row[:, 0:min(to, cut) - at]
                    if to > cut:
                        b3_ref[j, :, max(at, cut) - cut:to - cut] = row[:, max(at, cut) - at:]
                for t in range(4):
                    ref, at = (ow_s, j * r) if t == 3 else (at_s, (3 * j + t) * r)
                    ref[at:at + r, :] = ref_in[pl.ds(pl.multiple_of((4 * a + (t ^ q)) * r, r), r), :]

            @pl.when(own)
            def _():
                place(mine)

            @pl.when(jnp.logical_not(own))
            def _():
                place(sib)

        for copy in copies:
            copy.start()

    attend_image(pad, counts[step], norm_ref[0], at_s, vec_ref, a1_ref, qkv_ref, o_ref, lse_ref, lse_s)

    @pl.when(step == pl.num_programs(0) - 1)
    def _():
        for copy in copies:
            copy.wait()


def head(ids, counts, mine, sib, norm):
    n, pad, width = norm.shape
    r = width // 8
    cut = 4 * r // 3
    sd = jax.ShapeDtypeStruct
    far = pl.BlockSpec(memory_space=pl.ANY)
    return pl.pallas_call(
        functools.partial(head_kernel, pad),
        out_shape=[
            sd((24 * r, width), BF16), sd((8 * r, width), BF16), sd((8, width), F32), sd((8, 1, cut), F32),
            sd((8, 1, 4 * r - cut), F32),
            sd((n, pad, width), BF16), sd((n, pad, 3 * width), BF16),
            sd((n, pad, width), BF16), sd((n, 16, pad), F32),
        ],
        grid_spec=pltpu.PrefetchScalarGridSpec(
            num_scalar_prefetch=2, grid=(n,),
            in_specs=[whole(mine.shape), whole(sib.shape), by_image((pad, width))],
            out_specs=[
                far, far, whole((8, width)), whole((8, 1, cut)), whole((8, 1, 4 * r - cut)),
                by_image((pad, width)), by_image((pad, 3 * width)),
                by_image((pad, width)), by_image((16, pad)),
            ],
            scratch_shapes=[
                pltpu.VMEM((24 * r, width), BF16), pltpu.VMEM((8 * r, width), BF16),
                pltpu.VMEM((pad, 128), F32), pltpu.SemaphoreType.DMA((2,))]),
        compiler_params=params(60),
        cost_estimate=pl.CostEstimate(
            flops=2 * n * pad * width * (3 * width + 4 * pad), bytes_accessed=20 * MIB,
            transcendentals=n * 12 * pad * pad),
        name="head",
    )(ids, counts, mine, sib, norm)


def part_kernel(seq, pad, second, group, ids, counts, depth, a2_ref, gm_ref, *rest):
    if second:
        weights, bu_ref, *rest = rest
    else:
        sides, bu_ref, rest = (rest[0:5], rest[5:10]), rest[10], rest[11:]
    if second:
        (mlp_in, ga2_in, a2t_in, gmt_in, x1_in, cot_ref, vecs,
         both, gbu_ref, y_ref, vec_ref, gx_out, ga_out,
         a2t, gmt, mlp, ga2, hs, gus, mlp_s, ga2_s, x1_s, ga_s, cs, sems, out_sems) = rest
        loads = [pltpu.make_async_copy(a, b, sems.at[k]) for k, (a, b) in enumerate(
            ((a2t_in, a2t), (gmt_in, gmt), (mlp_in, mlp_s), (ga2_in, ga2_s), (x1_in, x1_s)))]
    else:
        both, gbu_ref, mlp_out, ga2_out, a2t_out, gmt_out, a2t, gmt, mlp, ga2, hs, gus, sems = rest
        stores = [pltpu.make_async_copy(a, b, sems.at[k]) for k, (a, b) in enumerate(
            ((a2t, a2t_out), (gmt, gmt_out), (mlp, mlp_out), (ga2, ga2_out)))]
    step = pl.program_id(0)
    end = pl.num_programs(0) - 1
    q, z, c = ids[0], ids[1], ids[2]
    rows, width = a2_ref.shape
    n = rows // pad
    block = bu_ref.shape[-1]

    @pl.when(step == 0)
    def _():
        if second:
            for copy in loads:
                copy.start()
        else:
            a2t[...] = jnp.transpose(a2_ref[...])
            gmt[...] = jnp.transpose(gm_ref[...])
            stores[0].start()
            stores[1].start()
        mlp[...] = jnp.zeros_like(mlp)
        ga2[...] = jnp.zeros_like(ga2)

    pairs = [(k, side) for k in range(group) for side in range(2)]
    owners = [(((step * group + k) ^ z) << 1) | (c ^ side) for k, side in pairs]
    def piece(k, side, t, low):
        own, message, *crossed = sides[side]
        slot, m = step * group + k, t ^ q
        at = slice(low, low + r)
        index = jnp.maximum(slot - 1, 0) if group > 1 else 0
        value = message[index, at]
        for x, ref in enumerate(crossed):
            value = jnp.where(m == x + 1, ref[index, at], value)
        return jnp.where(slot == 0, own[m, at], value)

    if second:
        up, down = (jnp.concatenate([weights[c, kind], weights[c ^ 1, kind]], 0) for kind in range(2))
    else:
        r = sides[0][0].shape[1] // 2
        up = jnp.concatenate([piece(k, side, t, 0) for k, side in pairs for t in range(4)], 0)
        down = jnp.concatenate([piece(k, side, t, r) for k, side in pairs for t in range(4)], 0)
    bu = jnp.concatenate([bu_ref[owner] for owner in owners], 1)
    gbu = jnp.zeros(bu.shape, F32)
    for i in range(n):
        at = slice(i * pad, (i + 1) * pad)
        u = nt(a2_ref[at, :], up) + bu
        t = nt(gm_ref[at, :], down)
        act, slope = gelu_pair(u)
        h = act.astype(BF16)
        gu = (t * slope).astype(BF16)
        hs[at, :] = h
        gus[at, :] = gu
        gbu = gbu + col_sum(gu.astype(F32))
        mlp[at, :] += nn(h, down)
        ga2[at, :] += nn(gu, up)
    for p, owner in enumerate(owners):
        gbu_ref[owner] = gbu[:, p * block:(p + 1) * block]

    if second:
        @pl.when(step == 0)
        def _():
            loads[0].wait()
            loads[1].wait()
    else:
        @pl.when(step == end)
        def _():
            stores[2].start()
            stores[3].start()

    part = width // 4
    span = 2 * group
    for t in range(4):
        at = slice(t * part, (t + 1) * part)
        for kind, (left, right) in enumerate(((a2t, gus), (gmt, hs))):
            d = nn(left[at, :], right[...]).astype(BF16)
            for p, owner in enumerate(owners):
                both[owner % span, t, kind] = d[:, p * block:(p + 1) * block]

    if not second:
        @pl.when(step == end)
        def _():
            for copy in stores:
                copy.wait()
        return

    @pl.when(step == end)
    def _():
        for copy in loads[2:]:
            copy.wait()
        mask_rows = lax.broadcasted_iota(jnp.int32, (pad, 1), 0)
        cs[pad - 8:pad, :] = jnp.zeros((8, width), F32)
        sums = [jnp.zeros((1, width), F32)] * 5
        outs = []
        for i in range(n):
            at = slice(i * pad, (i + 1) * pad)
            ok = mask_rows < counts[i]
            x1 = x1_s[i]
            out = mlp[at, :] + mlp_s[at, :] + vecs[7:8, :]
            y_ref[i] = jnp.where(ok, x1 + depth[i, 1] * out, 0.0).astype(BF16)[0:seq]
            cs[0:seq, :] = cot_ref[i].astype(F32)
            g = jnp.where(ok, cs[...], 0.0)
            back = ga2[at, :] + ga2_s[at, :]
            normed, rstd = normalize(x1)
            e = back * vecs[5:6, :]
            gx = g + rstd * (e - mean_row(e) - normed * mean_row(e * normed))
            ga = (depth[i, 0] * gx).astype(BF16)
            x1_s[i] = gx
            ga_s[i] = ga
            for k, (ref, to) in enumerate(((x1_s, gx_out), (ga_s, ga_out))):
                copy = pltpu.make_async_copy(ref.at[i], to.at[i], out_sems.at[i, k])
                copy.start()
                outs.append(copy)
            terms = (back * normed, back, gm_ref[at, :].astype(F32), ga.astype(F32), jnp.where(ok, out * out, 0.0))
            sums = [total + col_sum(term) for total, term in zip(sums, terms)]
        for k, total in enumerate(sums):
            vec_ref[k:k + 1, :] = total
        vec_ref[5:8, :] = jnp.zeros((3, width), F32)
        for copy in outs:
            copy.wait()


def part(ids, counts, depth, a2, gm, weights, bu, pad, group, carry=(), x1=None, cot=None, vec=None):
    rows, width = a2.shape
    n = rows // pad
    block = bu.shape[-1]
    second = len(carry) > 0
    sd = jax.ShapeDtypeStruct
    if second:
        w_specs = [pl.BlockSpec((2, 2, block, width), lambda s, ids, *_: (s ^ ids[1], 0, 0, 0))]
    else:
        w_specs = [whole(w.shape) for w in weights]
    far = pl.BlockSpec(memory_space=pl.ANY)
    acc = sd((rows, width), F32)
    tr = sd((width, rows), BF16)
    in_specs = [whole(a2.shape), whole(gm.shape)] + w_specs + [whole(bu.shape)]
    args = [a2, gm, *weights, bu]
    outs = [sd((8, 4, 2, width // 4, block), BF16), sd((8, 1, block), F32)]
    out_specs = [
        pl.BlockSpec((2 * group, 4, 2, width // 4, block), lambda s, ids, *_: (s ^ (ids[1] // group), 0, 0, 0, 0)),
        whole((8, 1, block))]
    scratch = [pltpu.VMEM(tr.shape, BF16), pltpu.VMEM(tr.shape, BF16), pltpu.VMEM(acc.shape, F32),
               pltpu.VMEM(acc.shape, F32), pltpu.VMEM((rows, 2 * group * block), BF16),
               pltpu.VMEM((rows, 2 * group * block), BF16)]
    if second:
        seq = cot.shape[1]
        args += [*carry, x1, cot, vec]
        in_specs += [far] * 5 + [whole(cot.shape), whole(vec.shape)]
        outs += [sd((n, seq, width), BF16), sd((8, width), F32), sd((n, pad, width), F32), sd((n, pad, width), BF16)]
        out_specs += [whole((n, seq, width)), whole((8, width)), far, far]
        scratch += [pltpu.VMEM(acc.shape, F32), pltpu.VMEM(acc.shape, F32), pltpu.VMEM((n, pad, width), F32),
                    pltpu.VMEM((n, pad, width), BF16), pltpu.VMEM((pad, width), F32), pltpu.SemaphoreType.DMA((5,)),
                    pltpu.SemaphoreType.DMA((n, 2))]
    else:
        seq = 0
        outs += [acc, acc, tr, tr]
        out_specs += [far] * 4
        scratch += [pltpu.SemaphoreType.DMA((4,))]
    return pl.pallas_call(
        functools.partial(part_kernel, seq, pad, second, group),
        out_shape=outs,
        grid_spec=pltpu.PrefetchScalarGridSpec(
            num_scalar_prefetch=3, grid=(4 // group,), in_specs=in_specs, out_specs=out_specs,
            scratch_shapes=scratch),
        compiler_params=params(60),
        cost_estimate=pl.CostEstimate(
            flops=12 * rows * width * 8 * block, bytes_accessed=30 * MIB, transcendentals=0),
        name="feed_b" if second else "feed_a",
    )(ids, counts, depth, *args)


def grads_kernel(far_z, ids, g_ref, o_ref, a1_ref, ga_ref, near, far):
    s = pl.program_id(0)
    q, z, c = ids[0], ids[1], ids[2]
    r = near.shape[2]
    side = (z >> 1) ^ int(far_z)

    def put(value, j, t):
        a, m = ((j >> 1) ^ z) & 1, t ^ q
        own = ((j & 1) ^ c) == 0

        @pl.when(own)
        def _():
            near[m, a] = value

        @pl.when(jnp.logical_not(own))
        def _():
            far[m, a] = value

    @pl.when(s < 3)
    def _():
        g = g_ref[...]
        d = tn(g, a1_ref[...]).astype(BF16)
        for k in range(4):
            chunk = 4 * s + k
            put(d[k * r:(k + 1) * r], 4 * side + chunk // 3, chunk % 3)

    @pl.when(s >= 3)
    def _():
        d = tn(o_ref[...], ga_ref[...]).astype(BF16)
        for k in range(4):
            put(d[k * r:(k + 1) * r], 4 * side + k, 3)


def grads(ids, g, o, a1, ga, far_z):
    rows, width = a1.shape
    r = width // 8
    block = 4 * r
    sd = jax.ShapeDtypeStruct
    side = lambda ids: (ids[1] >> 1) ^ int(far_z)
    return pl.pallas_call(
        functools.partial(grads_kernel, far_z),
        out_shape=[sd((4, 2, r, width), BF16), sd((4, 2, r, width), BF16)],
        grid_spec=pltpu.PrefetchScalarGridSpec(
            num_scalar_prefetch=1, grid=(4,),
            in_specs=[
                pl.BlockSpec((rows, block), lambda s, ids: (0, 3 * side(ids) + jnp.minimum(s, 2))),
                pl.BlockSpec((rows, block), lambda s, ids: (0, side(ids))),
                whole(a1.shape), whole(ga.shape)],
            out_specs=[whole((4, 2, r, width)), whole((4, 2, r, width))]),
        compiler_params=params(60),
        cost_estimate=pl.CostEstimate(
            flops=4 * rows * width * width, bytes_accessed=12 * MIB, transcendentals=0),
        name="grads",
    )(ids, g, o, a1, ga)


def final_kernel(seq, pad, g_ref, w_ref, x_ref, gx_ref, y_ref, vecs, gi_ref, y_out, vec_ref, cols_ref, xs):
    i = pl.program_id(0)
    width = x_ref.shape[-1]
    grad = nn(g_ref[0], w_ref[...])
    xs[pad - 8:pad, :] = jnp.zeros((8, width), F32)
    xs[0:seq, :] = x_ref[0].astype(F32)
    normed, rstd = normalize(xs[...])

    @pl.when(i == 0)
    def _():
        vec_ref[...] = jnp.zeros_like(vec_ref)
        cols_ref[...] = jnp.zeros_like(cols_ref)

    vec_ref[0:1, :] += col_sum(grad * normed)
    vec_ref[1:2, :] += col_sum(grad)
    cols_ref[...] += col_sum(g_ref[0].astype(F32))
    e = grad * vecs[0:1, :]
    gi = gx_ref[0] + rstd * (e - mean_row(e) - normed * mean_row(e * normed))
    for k in range(gi_ref.shape[1]):
        @pl.when(i == k)
        def _():
            gi_ref[:, k, :] = gi[0:seq]
            y_out[:, k, :] = y_ref[0]


def final(g, w, images, gx, y, vec, pad):
    n, seq, width = images.shape
    sd = jax.ShapeDtypeStruct
    return pl.pallas_call(
        functools.partial(final_kernel, seq, pad),
        out_shape=[sd((seq, n, width), F32), sd((seq, n, width), BF16), sd((8, width), F32), sd((1, 3 * width), F32)],
        grid=(n,),
        in_specs=[by_image((pad, 3 * width)), whole(w.shape), by_image((seq, width)), by_image((pad, width)),
                  by_image((seq, width)), whole(vec.shape)],
        out_specs=[whole((seq, n, width)), whole((seq, n, width)), whole((8, width)), whole((1, 3 * width))],
        scratch_shapes=[pltpu.VMEM((pad, width), F32)],
        compiler_params=params(60),
        cost_estimate=pl.CostEstimate(
            flops=6 * n * pad * width * width, bytes_accessed=18 * MIB, transcendentals=0),
        name="final",
    )(g, w, images, gx, y, vec)


def add_pair(ids, near, got):
    slots, parts = near.shape[:2]
    shape = near.shape[1:]
    block = pl.BlockSpec((slots, 1) + shape[1:], lambda a, *_: (0, a) + (0,) * (len(shape) - 1))

    def kernel(a_ref, b_ref, *outs):
        for m in range(4):
            outs[m][...] = (a_ref[m].astype(F32) + b_ref[m].astype(F32)).astype(BF16)

    return pl.pallas_call(
        kernel,
        out_shape=[jax.ShapeDtypeStruct(shape, BF16)] * slots,
        grid=(parts,),
        in_specs=[block, block],
        out_specs=[pl.BlockSpec((1,) + shape[1:], lambda a: (a,) + (0,) * (len(shape) - 1))] * slots,
        compiler_params=params(60),
        cost_estimate=pl.CostEstimate(flops=0, bytes_accessed=6 * near.size, transcendentals=0),
        name="add_pair",
    )(near, got)


def add_four(ids, parts, split):
    shape = parts[0].shape

    def kernel(ids, a, b, c, d, *outs):
        if split:
            for k in range(shape[0]):
                outs[k][...] = ((a[k].astype(F32) + b[k].astype(F32)) + (c[k].astype(F32) + d[k].astype(F32))).astype(BF16)
        else:
            outs[0][...] = ((a[...].astype(F32) + b[...].astype(F32)) + (c[...].astype(F32) + d[...].astype(F32))).astype(BF16)

    count = shape[0] if split else 1
    out = jax.ShapeDtypeStruct(shape[1:] if split else shape, BF16)
    return simple(kernel, ids, parts, [out] * count, "add_four")


def merge(ids, s2, s3):
    _, _, rows, k2 = s2.shape
    k3 = s3.shape[3]

    def kernel(ids, a, b, out):
        for ref, at, to in ((a, 0, k2), (b, k2, k2 + k3)):
            out[:, :, at:to] = ((ref[0].astype(F32) + ref[1].astype(F32)) + (ref[2].astype(F32) + ref[3].astype(F32))).astype(BF16)

    return simple(kernel, ids, [s2, s3], [jax.ShapeDtypeStruct((2, rows, k2 + k3), BF16)], "merge")[0]


def place_feed_kernel(ids, p0, p1, p2, p3, up_ref, down_ref, cs):
    q = ids[0]
    rows = p0.shape[1]
    for m, p in enumerate((p0, p1, p2, p3)):
        to = pl.ds(pl.multiple_of((q ^ m) * rows, rows), rows)
        up_ref[to, :] = p[0].astype(F32)
        cs[to, :] = p[1].astype(F32)
    down_ref[...] = jnp.transpose(cs[...])


def place_feed(ids, parts):
    _, rows, block = parts[0].shape
    sd = jax.ShapeDtypeStruct
    return simple(place_feed_kernel, ids, parts, [sd((4 * rows, block), F32), sd((block, 4 * rows), F32)],
                  "place_feed", scratch=[pltpu.VMEM((4 * rows, block), F32)])


def place_attend_kernel(ids, p0, p1, p2, p3, at_ref, ow_ref, cs):
    q = ids[0]
    r = p0.shape[0]
    for m, p in enumerate((p0, p1, p2, p3)):
        cs[pl.ds(pl.multiple_of((q ^ m) * r, r), r), :] = p[...].astype(F32)
    at_ref[...] = cs[0:3 * r, :]
    ow_ref[...] = cs[3 * r:4 * r, :]


def place_attend(ids, parts):
    r, width = parts[0].shape
    sd = jax.ShapeDtypeStruct
    return simple(place_attend_kernel, ids, parts, [sd((3 * r, width), F32), sd((r, width), F32)],
                  "place_attend", scratch=[pltpu.VMEM((4 * r, width), F32)])


def cut_vectors(ids, rows, share):
    width = rows.shape[1]
    parts = width // share

    def kernel(ids, rows_ref, *outs):
        owner = 2 * ids[1] + ids[2]
        vectors, bias = outs[:8], outs[8]
        for j in range(parts):
            @pl.when(owner == j)
            def _():
                for k in range(8):
                    vectors[k][...] = rows_ref[k:k + 1, j * share:(j + 1) * share].reshape(share)
                at = j * 4 * share
                bias[...] = rows_ref[8 + at // width:9 + at // width, at % width:at % width + 4 * share].reshape(4 * share)

    sd = jax.ShapeDtypeStruct
    return simple(kernel, ids, [rows], [sd((share,), F32)] * 8 + [sd((4 * share,), F32)], "cut_vectors")


def shards_grid(
    images, grid_sizes, keep_flags, attn_gain, attn_shift, attend_weight, query_bias, value_bias,
    output_weight, output_bias, mlp_gain, mlp_shift, up_weight, up_bias, down_weight, down_bias,
    cotangent,
):
    n, seq, width = images.shape
    pad = -(-seq // 32) * 32
    counts = grid_sizes[:, 0] * grid_sizes[:, 1] + 2
    depth = keep_flags.astype(F32) / KEEP_PROB
    owners = 8
    share = attn_gain.shape[0]
    f = lax.axis_index("fsdp")
    ids = jnp.stack([lax.axis_index("dp"), f >> 1, f & 1]).astype(jnp.int32)

    z_all = lambda array: [over_z(array, a) for a in (1, 2, 3)]
    dp_all = lambda array: [over_dp(array, m) for m in (1, 2, 3)]
    dp_out = lambda s: [s[0]] + [over_dp(s[m], m) for m in (1, 2, 3)]
    z_out = lambda s: [s[0]] + [over_z(s[a], a) for a in (1, 2, 3)]
    tied = lax.optimization_barrier
    flat = lambda array: array.reshape(n * pad, array.shape[-1])

    own1, first1, own, first, rest = pack(
        ids, attend_weight.T, output_weight, up_weight, down_weight,
        [attn_gain, attn_shift, query_bias, value_bias, output_bias, mlp_gain, mlp_shift, down_bias, up_bias])
    zr1 = z_all(first1)
    own_other = over_core(own)
    first, rest, zr1, own_other = tied((first, rest, zr1, own_other))
    message1, = stack_rows(ids, zr1, [(0, share)])
    xr1 = dp_all(message1)
    zr = z_all(first)
    weights_b = lax.all_gather(rest[None], "fsdp", axis=0, tiled=True)
    norm, gm = early(counts, depth, images, cotangent, pad)
    xr1, zr, norm, gm = tied((xr1, zr, norm, gm))
    mine1 = line(ids, own1, first1, zr1, xr1)
    sib1 = over_core(mine1)
    message, = stack_rows(ids, zr, [(0, first.shape[0])])
    message_other = over_core(message)
    xr = dp_all(message)
    sib1, message_other = tied((sib1, message_other))
    attend, out_w, vec, bu2, bu3, a1, qkv, o, lse = head(ids, counts, mine1, sib1, norm)
    o, xr = tied((o, xr))
    sib = [own_other, message_other, *(over_core(x) for x in xr)]
    x1, a2, sums_two = middle(counts, depth, o, images, out_w, vec, pad)
    x1, a2, sib = tied((x1, a2, sib))
    a2, gm = flat(a2), flat(gm)
    both2, gbu2, mlp, ga2, a2t, gmt = part(
        ids, counts, depth, a2, gm, [own, message, *xr, *sib], bu2, pad, 2)
    mlp, weights_b = tied((mlp, weights_b))

    own_sum = lambda both: lax.psum_scatter(
        both.reshape(-1, both.shape[-1]), "fsdp", scatter_dimension=0, tiled=True).reshape(both.shape[1:])
    quarter = lambda shard: lax.all_to_all(shard, "dp", 0, 0, tiled=True)
    shard2 = own_sum(both2)
    both3, gbu3, y, vec_feed, gx, ga = part(
        ids, counts, depth, a2, gm, [weights_b], bu3, pad, 1, (mlp, ga2, a2t, gmt), x1, cotangent, vec)
    shard3 = own_sum(both3)
    quarter2 = quarter(after(shard2, ga))
    g = back(counts, ga, out_w, qkv, lse)
    g, quarter2 = tied((g, quarter2))
    near_p, far_p = grads(ids, flat(g), flat(o), flat(a1), flat(ga), True)
    got_p = over_core(far_p)
    near_q, far_q = grads(ids, flat(after(g, near_p)), flat(o), flat(a1), flat(ga), False)
    near_q, far_q, got_p = tied((near_q, far_q, got_p))
    got_q = over_core(far_q)
    s_p = add_pair(ids, near_p, got_p)
    dr_p = dp_out(s_p)
    gi, y, vec_last, cols = final(after(g, s_p), attend, images, gx, y, vec, pad)
    y, gi = y.swapaxes(0, 1), gi.swapaxes(0, 1)
    rows = jnp.concatenate([
        vec_last[0:2], cols[:, :width], cols[:, 2 * width:], vec_feed[3:4], vec_feed[0:3],
        jnp.concatenate([gbu2[:, 0], gbu3[:, 0]], 1).reshape(4, width), sums_two[:, 0:2].sum(0), vec_feed[4:5],
        jnp.full((1, width), jnp.sum(counts).astype(F32)),
    ], 0)
    rows = rows + over_core(rows)
    rows, got_q, dr_p = tied((rows, got_q, dr_p))
    s_q = add_pair(ids, near_q, got_q)
    rows = rows + over_dp(rows, 1)
    s_q, rows = tied((s_q, rows))
    dr_q = dp_out(s_q)
    quarter3 = quarter(after(shard3, s_q))
    e_p = add_four(ids, after(dr_p, s_q), True)
    er_p = [over_z(x, a) for a, x in zip((2, 3), e_p)]
    er_p, dr_q, rows, quarter3 = tied((er_p, dr_q, rows, quarter3))
    e_q = add_four(ids, dr_q, True)
    er_q = over_z(e_q[1], 1)
    rows = after(rows, e_q)
    rows = rows + over_dp(rows, 2)
    f3 = merge(ids, quarter2, after(quarter3, e_q))
    fr3 = [f3] + dp_all(f3)
    er_q, fr3[1], fr3[2] = tied((er_q, fr3[1], fr3[2]))
    f1 = add_four(ids, [e_q[0], er_q, *er_p], False)[0]
    fr1 = [f1] + dp_all(f1)
    got = z_all(after(rows, f1))
    rows = (rows + got[0]) + (got[1] + got[2])
    root_means = jnp.sqrt(jnp.sum(rows[12:15], 1) / (rows[15, 0] * width))
    *tv, gub = cut_vectors(ids, rows, share)
    gup, gdown = place_feed(ids, fr3)
    gattend, gout = place_attend(ids, fr1)
    gattend = gattend.T
    return (y, gi, tv[0], tv[1], gattend, tv[2], tv[3], gout, tv[4], tv[5], tv[6],
            gup, gub, gdown, tv[7], root_means)


def shards(on_grid, *args):
    images, attn_gain, up_weight = args[0], args[3], args[12]
    share = attn_gain.shape[0]
    fits = on_grid and share % 48 == 0 and up_weight.shape[1] == 4 * share and images.shape[2] == 8 * share
    return (shards_grid if fits else shards_any)(*args)


def solution(mesh):
    images = P(("dp", "fsdp"), None, None)
    flags = P(("dp", "fsdp"), None)
    vec, rows, cols = P("fsdp"), P("fsdp", None), P(None, "fsdp")
    return jax.shard_map(
        functools.partial(shards, dict(mesh.shape) == {"dp": 4, "fsdp": 8}),
        mesh=mesh,
        in_specs=(images, flags, flags, vec, vec, cols, vec, vec, rows, vec, vec, vec, cols, vec, rows,
                  vec, images),
        out_specs=(images, images, vec, vec, cols, vec, vec, rows, vec, vec, vec, cols, vec, rows, vec,
                   P()),
        check_vma=False,
    )
```

```python
import functools
import math

import jax
import jax.numpy as jnp
from jax import lax
from jax.experimental import pallas as pl
from jax.experimental.pallas import tpu as pltpu
from jax.sharding import PartitionSpec as P

HEAD_DIM = 64
EPS = 1e-06
KEEP_PROB = 0.9
MASKED = -1e30
INV_ROOT_TWO = 0.7071067811865476
INV_ROOT_TWO_PI = 0.3989422804014327
F32 = jnp.float32
BF16 = jnp.bfloat16
MIB = 1024 * 1024


def nn(left, right):
    return lax.dot_general(left, right, (((1,), (0,)), ((), ())), preferred_element_type=F32)


def nt(left, right):
    return lax.dot_general(left, right, (((1,), (1,)), ((), ())), preferred_element_type=F32)


def tn(left, right):
    return lax.dot_general(left, right, (((0,), (0,)), ((), ())), preferred_element_type=F32)


def mean_row(values):
    return jnp.sum(values, -1, keepdims=True) * (1.0 / values.shape[-1])


def normalize(values):
    center = values - mean_row(values)
    rstd = lax.rsqrt(mean_row(center * center) + EPS)
    return center * rstd, rstd


def col_sum(values):
    return jnp.sum(values, 0, keepdims=True)


def params(limit, steps=1):
    return pltpu.CompilerParams(
        dimension_semantics=("arbitrary",) * steps, vmem_limit_bytes=limit * MIB
    )


def whole(shape, buffers=1):
    zeros = (0,) * len(shape)
    return pl.BlockSpec(shape, lambda *_: zeros, pipeline_mode=pl.Buffered(buffers))


def by_image(shape):
    rest = (0,) * len(shape)
    return pl.BlockSpec((1,) + shape, lambda i, *_: (i,) + rest)


SMEM = pl.BlockSpec(memory_space=pltpu.SMEM)


def front_kernel(seq, pad, counts, depth, x_ref, cot_ref, w_ref, vec_ref,
                 a1_ref, gm_ref, qkv_ref, o_ref, lse_ref, xs, lse_s):
    i = pl.program_id(0)
    width = x_ref.shape[-1]
    count = counts[i]
    rows = lax.broadcasted_iota(jnp.int32, (pad, 1), 0)
    xs[pad - 8:pad, :] = jnp.zeros((8, width), F32)
    xs[0:seq, :] = cot_ref[0].astype(F32)
    gm_ref[0] = jnp.where(rows < count, xs[...] * depth[i, 1], 0.0).astype(BF16)
    xs[0:seq, :] = x_ref[0].astype(F32)
    normed, _ = normalize(xs[...])
    attend_image(pad, count, normed, w_ref, vec_ref, a1_ref, qkv_ref, o_ref, lse_ref, lse_s)


def attend_image(pad, count, normed, w_ref, vec_ref, a1_ref, qkv_ref, o_ref, lse_ref, lse_s):
    width = normed.shape[-1]
    pairs = width // 128
    a1 = (normed * vec_ref[0:1, :] + vec_ref[1:2, :]).astype(BF16)
    a1_ref[0] = a1
    for c in range(0, 3 * width, 384):
        part = nt(a1, w_ref[c:c + 384, :])
        if c < width:
            part = part + vec_ref[2:3, c:c + 384]
        elif c >= 2 * width:
            part = part + vec_ref[3:4, c - 2 * width:c - 2 * width + 384]
        qkv_ref[0, :, c:c + 384] = part.astype(BF16)
    ok = lax.broadcasted_iota(jnp.int32, (pad, pad), 1) < count
    lane = lax.broadcasted_iota(jnp.int32, (pad, 128), 1)
    lse_s[...] = jnp.zeros((pad, 128), F32)

    def pair(p):
        at = pl.multiple_of(p * 128, 128)
        q = qkv_ref[0, :, pl.ds(at, 128)] * 0.125
        k = qkv_ref[0, :, pl.ds(width + at, 128)]
        v = qkv_ref[0, :, pl.ds(2 * width + at, 128)]
        total = jnp.zeros((pad, 128), F32)
        for half in range(2):
            mine = (lane >= 64) if half else (lane < 64)
            scores = jnp.where(ok, nt(jnp.where(mine, q, 0), k), MASKED)
            top = jnp.max(scores, -1, keepdims=True)
            e = jnp.exp(scores - top)
            s = jnp.sum(e, -1, keepdims=True)
            prob = (e * (1.0 / s)).astype(BF16)
            total = total + nn(prob, jnp.where(mine, v, 0))
            lse_s[...] = jnp.where(lane == 2 * p + half, top + jnp.log(s), lse_s[...])
        o_ref[0, :, pl.ds(at, 128)] = total.astype(BF16)

    for p in range(pairs):
        pair(p)
    lse_ref[0] = jnp.transpose(lse_s[...])[0:16, :]


def front(counts, depth, images, cot, w, vec, pad):
    n, seq, width = images.shape
    grid_spec = pltpu.PrefetchScalarGridSpec(
        num_scalar_prefetch=2,
        grid=(n,),
        in_specs=[
            by_image((seq, width)), by_image((seq, width)),
            whole(w.shape), whole(vec.shape),
        ],
        out_specs=[
            by_image((pad, width)), by_image((pad, width)), by_image((pad, 3 * width)),
            by_image((pad, width)), by_image((16, pad)),
        ],
        scratch_shapes=[pltpu.VMEM((pad, width), F32), pltpu.VMEM((pad, 128), F32)],
    )
    return pl.pallas_call(
        functools.partial(front_kernel, seq, pad),
        out_shape=[
            jax.ShapeDtypeStruct((n, pad, width), BF16),
            jax.ShapeDtypeStruct((n, pad, width), BF16),
            jax.ShapeDtypeStruct((n, pad, 3 * width), BF16),
            jax.ShapeDtypeStruct((n, pad, width), BF16),
            jax.ShapeDtypeStruct((n, 16, pad), F32),
        ],
        grid_spec=grid_spec,
        compiler_params=params(60),
        cost_estimate=pl.CostEstimate(
            flops=2 * n * pad * width * (3 * width + 4 * pad), bytes_accessed=20 * MIB,
            transcendentals=n * 12 * pad * pad),
        name="front",
    )(counts, depth, images, cot, w, vec)


def middle_kernel(seq, pad, counts, depth, o_ref, x_ref, w_ref, vec_ref,
                  x1_ref, a2_ref, sums_ref, xs):
    i = pl.program_id(0)
    width = x_ref.shape[-1]
    rows = lax.broadcasted_iota(jnp.int32, (pad, 1), 0)
    ok = rows < counts[i]
    xs[pad - 8:pad, :] = jnp.zeros((8, width), F32)
    xs[0:seq, :] = x_ref[0].astype(F32)
    attn = nn(o_ref[0], w_ref[...]) + vec_ref[4:5, :]
    x1 = xs[...] + depth[i, 0] * attn
    x1_ref[0] = x1
    sums_ref[0, 0:1, :] = col_sum(jnp.where(ok, x1 * x1, 0.0))
    sums_ref[0, 1:2, :] = col_sum(jnp.where(ok, attn * attn, 0.0))
    sums_ref[0, 2:8, :] = jnp.zeros((6, width), F32)
    normed, _ = normalize(x1)
    a2_ref[0] = (normed * vec_ref[5:6, :] + vec_ref[6:7, :]).astype(BF16)


def middle(counts, depth, o, images, w, vec, pad):
    n, seq, width = images.shape
    grid_spec = pltpu.PrefetchScalarGridSpec(
        num_scalar_prefetch=2,
        grid=(n,),
        in_specs=[
            by_image((pad, width)), by_image((seq, width)),
            whole(w.shape), whole(vec.shape),
        ],
        out_specs=[by_image((pad, width)), by_image((pad, width)), by_image((8, width))],
        scratch_shapes=[pltpu.VMEM((pad, width), F32)],
    )
    return pl.pallas_call(
        functools.partial(middle_kernel, seq, pad),
        out_shape=[
            jax.ShapeDtypeStruct((n, pad, width), F32),
            jax.ShapeDtypeStruct((n, pad, width), BF16),
            jax.ShapeDtypeStruct((n, 8, width), F32),
        ],
        grid_spec=grid_spec,
        compiler_params=params(60),
        cost_estimate=pl.CostEstimate(
            flops=2 * n * pad * width * width, bytes_accessed=10 * MIB, transcendentals=0),
        name="middle",
    )(counts, depth, o, images, w, vec)


def gelu_pair(u):
    size = jnp.abs(u)
    t = 1.0 / (1.0 + (0.3275911 * INV_ROOT_TWO) * size)
    bell = jnp.exp(-0.5 * (u * u))
    series = t * (0.5 * 0.254829592 + t * (0.5 * -0.284496736 + t * (
        0.5 * 1.421413741 + t * (0.5 * -1.453152027 + t * (0.5 * 1.061405429)))))
    tail = series * bell
    phi = jnp.where(u >= 0, 1.0 - tail, tail)
    return u * phi, phi + u * (bell * INV_ROOT_TWO_PI)


def feed_kernel(seq, pad, counts, depth, a2_ref, gm_ref, up_ref, down_ref, bu_ref, x1_ref, cot_ref,
                vecs,
                dup_ref, ddown_ref, gbu_ref, y_ref, gx_ref, ga_ref, vec_ref,
                a2t, gmt, mlp, ga2, hs, gus, cs):
    j = pl.program_id(0)
    n = x1_ref.shape[0]

    @pl.when(j == 0)
    def _():
        a2t[...] = jnp.transpose(a2_ref[...])
        gmt[...] = jnp.transpose(gm_ref[...])
        mlp[...] = jnp.zeros_like(mlp)
        ga2[...] = jnp.zeros_like(ga2)

    gbu = jnp.zeros(bu_ref.shape[1:], F32)
    for i in range(n):
        at = slice(i * pad, (i + 1) * pad)
        u = nt(a2_ref[at, :], up_ref[...]) + bu_ref[0]
        t = nt(gm_ref[at, :], down_ref[...])
        act, slope = gelu_pair(u)
        h = act.astype(BF16)
        gu = (t * slope).astype(BF16)
        hs[at, :] = h
        gus[at, :] = gu
        gbu = gbu + col_sum(gu.astype(F32))
        mlp[at, :] += nn(h, down_ref[...])
        ga2[at, :] += nn(gu, up_ref[...])
    gbu_ref[0] = gbu
    dup_ref[0] = nn(a2t[...], gus[...]).astype(BF16)
    ddown_ref[0] = nn(gmt[...], hs[...]).astype(BF16)

    @pl.when(j == pl.num_programs(0) - 1)
    def _():
        width = x1_ref.shape[-1]
        rows = lax.broadcasted_iota(jnp.int32, (pad, 1), 0)
        cs[pad - 8:pad, :] = jnp.zeros((8, width), F32)
        msum = jnp.zeros((1, width), F32)
        ggain = jnp.zeros((1, width), F32)
        gshift = jnp.zeros((1, width), F32)
        gdown = jnp.zeros((1, width), F32)
        gout = jnp.zeros((1, width), F32)
        for i in range(n):
            at = slice(i * pad, (i + 1) * pad)
            ok = rows < counts[i]
            x1 = x1_ref[i]
            out = mlp[at, :] + vecs[7:8, :]
            msum = msum + col_sum(jnp.where(ok, out * out, 0.0))
            y_ref[i] = jnp.where(ok, x1 + depth[i, 1] * out, 0.0).astype(BF16)[0:seq]
            cs[0:seq, :] = cot_ref[i].astype(F32)
            g = jnp.where(ok, cs[...], 0.0)
            gdown = gdown + col_sum(gm_ref[at, :].astype(F32))
            back = ga2[at, :]
            normed, rstd = normalize(x1)
            ggain = ggain + col_sum(back * normed)
            gshift = gshift + col_sum(back)
            e = back * vecs[5:6, :]
            gx = g + rstd * (e - mean_row(e) - normed * mean_row(e * normed))
            gx_ref[i] = gx
            ga = (depth[i, 0] * gx).astype(BF16)
            ga_ref[i] = ga
            gout = gout + col_sum(ga.astype(F32))
        vec_ref[0:1, :] = ggain
        vec_ref[1:2, :] = gshift
        vec_ref[2:3, :] = gdown
        vec_ref[3:4, :] = gout
        vec_ref[4:5, :] = msum
        vec_ref[5:8, :] = jnp.zeros((3, width), F32)


def feed(counts, depth, a2, gm, up, down, bu, x1, cot, vec, seq, pad, block):
    rows, width = a2.shape
    n = rows // pad
    hidden = up.shape[0]
    steps = hidden // block
    at = lambda j, *_: (j, 0)
    at3 = lambda j, *_: (j, 0, 0)
    grid_spec = pltpu.PrefetchScalarGridSpec(
        num_scalar_prefetch=2,
        grid=(steps,),
        in_specs=[
            whole(a2.shape), whole(gm.shape),
            pl.BlockSpec((block, width), at), pl.BlockSpec((block, width), at),
            pl.BlockSpec((1, 1, block), at3),
            whole(x1.shape), whole(cot.shape), whole(vec.shape),
        ],
        out_specs=[
            pl.BlockSpec((1, width, block), at3), pl.BlockSpec((1, width, block), at3),
            pl.BlockSpec((1, 1, block), at3),
            whole((n, seq, width)), whole((n, pad, width)), whole((n, pad, width)), whole((8, width)),
        ],
        scratch_shapes=[
            pltpu.VMEM((width, rows), BF16), pltpu.VMEM((width, rows), BF16),
            pltpu.VMEM((rows, width), F32), pltpu.VMEM((rows, width), F32),
            pltpu.VMEM((rows, block), BF16), pltpu.VMEM((rows, block), BF16),
            pltpu.VMEM((pad, width), F32),
        ],
    )
    return pl.pallas_call(
        functools.partial(feed_kernel, seq, pad),
        out_shape=[
            jax.ShapeDtypeStruct((steps, width, block), BF16),
            jax.ShapeDtypeStruct((steps, width, block), BF16),
            jax.ShapeDtypeStruct((steps, 1, block), F32),
            jax.ShapeDtypeStruct((n, seq, width), BF16),
            jax.ShapeDtypeStruct((n, pad, width), F32),
            jax.ShapeDtypeStruct((n, pad, width), BF16),
            jax.ShapeDtypeStruct((8, width), F32),
        ],
        grid_spec=grid_spec,
        compiler_params=params(60),
        cost_estimate=pl.CostEstimate(
            flops=12 * rows * width * hidden, bytes_accessed=40 * MIB, transcendentals=rows * hidden),
        name="feed",
    )(counts, depth, a2, gm, up, down, bu.reshape(steps, 1, block), x1, cot, vec)


def back_kernel(pad, counts, ga_ref, w_ref, qkv_ref, lse_ref, g_ref, go):
    back_image(pad, counts[pl.program_id(0)], ga_ref.at[0], w_ref, qkv_ref, lse_ref, g_ref.at[0], go)


def back_image(pad, count, ga_ref, w_ref, qkv_ref, lse_ref, g_ref, go):
    width = ga_ref.shape[-1]
    go[...] = nt(ga_ref[...], w_ref[...]).astype(BF16)
    ok = lax.broadcasted_iota(jnp.int32, (pad, pad), 0) < count
    lane = lax.broadcasted_iota(jnp.int32, (pad, 128), 1)

    def pair(p):
        at = pl.multiple_of(p * 128, 128)
        q = qkv_ref[0, :, pl.ds(at, 128)] * 0.125
        k = qkv_ref[0, :, pl.ds(width + at, 128)]
        v = qkv_ref[0, :, pl.ds(2 * width + at, 128)]
        g = go[:, pl.ds(at, 128)]
        gq = jnp.zeros((pad, 128), F32)
        gk = jnp.zeros((pad, 128), F32)
        gv = jnp.zeros((pad, 128), F32)
        for half in range(2):
            mine = (lane >= 64) if half else (lane < 64)
            qm = jnp.where(mine, q, 0)
            km = jnp.where(mine, k, 0) * 0.125
            gmine = jnp.where(mine, g, 0)
            scores = nt(k, qm)
            row = lse_ref[0, 2 * p + half:2 * p + half + 1, :]
            prob = jnp.where(ok, jnp.exp(scores - row), 0.0)
            dp = nt(v, gmine)
            inner = col_sum(prob * dp)
            ds = (prob * (dp - inner)).astype(BF16)
            gv = gv + nn(prob.astype(BF16), gmine)
            gk = gk + nn(ds, qm)
            gq = gq + tn(ds, km)
        g_ref[:, pl.ds(at, 128)] = gq.astype(BF16)
        g_ref[:, pl.ds(width + at, 128)] = gk.astype(BF16)
        g_ref[:, pl.ds(2 * width + at, 128)] = gv.astype(BF16)

    for p in range(width // 128):
        pair(p)


def back(counts, ga, w, qkv, lse):
    n, pad, width = ga.shape
    grid_spec = pltpu.PrefetchScalarGridSpec(
        num_scalar_prefetch=1,
        grid=(n,),
        in_specs=[by_image((pad, width)), whole(w.shape), by_image((pad, 3 * width)), by_image((16, pad))],
        out_specs=[by_image((pad, 3 * width))],
        scratch_shapes=[pltpu.VMEM((pad, width), BF16)],
    )
    return pl.pallas_call(
        functools.partial(back_kernel, pad),
        out_shape=[jax.ShapeDtypeStruct((n, pad, 3 * width), BF16)],
        grid_spec=grid_spec,
        compiler_params=params(60),
        cost_estimate=pl.CostEstimate(
            flops=2 * n * pad * width * (width + 10 * pad), bytes_accessed=16 * MIB,
            transcendentals=n * 12 * pad * pad),
        name="back",
    )(counts, ga, w, qkv, lse)[0]


def outgrad_kernel(o_ref, ga_ref, d_ref):
    d_ref[...] = tn(o_ref[...], ga_ref[...]).astype(BF16)


def outgrad(o, ga):
    rows, width = o.shape
    return pl.pallas_call(
        outgrad_kernel,
        out_shape=jax.ShapeDtypeStruct((width, width), BF16),
        grid=(2,),
        in_specs=[pl.BlockSpec((rows, width // 2), lambda j: (0, j)), whole(ga.shape)],
        out_specs=pl.BlockSpec((width // 2, width), lambda j: (j, 0)),
        compiler_params=params(60),
        cost_estimate=pl.CostEstimate(
            flops=2 * rows * width * width, bytes_accessed=6 * MIB, transcendentals=0),
        name="outgrad",
    )(o, ga)


def last_kernel(seq, pad, g_ref, a1_ref, w_ref, x_ref, gx_ref, vecs,
                d_ref, cols_ref, gi_ref, vec_ref, ga1, xs):
    c = pl.program_id(0)
    n = x_ref.shape[0]
    g = g_ref[...]
    d_ref[...] = tn(g, a1_ref[...]).astype(BF16)
    cols_ref[...] = col_sum(g.astype(F32))
    part = nn(g, w_ref[...])

    @pl.when(c == 0)
    def _():
        ga1[...] = part

    @pl.when(c > 0)
    def _():
        ga1[...] += part

    @pl.when(c == pl.num_programs(0) - 1)
    def _():
        width = x_ref.shape[-1]
        xs[pad - 8:pad, :] = jnp.zeros((8, width), F32)
        ggain = jnp.zeros((1, width), F32)
        gshift = jnp.zeros((1, width), F32)
        for i in range(n):
            xs[0:seq, :] = x_ref[i].astype(F32)
            normed, rstd = normalize(xs[...])
            grad = ga1[i * pad:(i + 1) * pad, :]
            ggain = ggain + col_sum(grad * normed)
            gshift = gshift + col_sum(grad)
            e = grad * vecs[0:1, :]
            gi = gx_ref[i] + rstd * (e - mean_row(e) - normed * mean_row(e * normed))
            gi_ref[i] = gi[0:seq]
        vec_ref[0:1, :] = ggain
        vec_ref[1:2, :] = gshift
        vec_ref[2:8, :] = jnp.zeros((6, width), F32)


def last(g, a1, w, images, gx, vec, pad, block=384):
    n, seq, width = images.shape
    rows, total = g.shape
    return pl.pallas_call(
        functools.partial(last_kernel, seq, pad),
        out_shape=[
            jax.ShapeDtypeStruct((total, width), BF16),
            jax.ShapeDtypeStruct((1, total), F32),
            jax.ShapeDtypeStruct((n, seq, width), F32),
            jax.ShapeDtypeStruct((8, width), F32),
        ],
        grid=(total // block,),
        in_specs=[
            pl.BlockSpec((rows, block), lambda c: (0, c)), whole(a1.shape),
            pl.BlockSpec((block, width), lambda c: (c, 0)), whole(images.shape), whole(gx.shape),
            whole(vec.shape),
        ],
        out_specs=[
            pl.BlockSpec((block, width), lambda c: (c, 0)), pl.BlockSpec((1, block), lambda c: (0, c)),
            whole((n, seq, width)), whole((8, width)),
        ],
        scratch_shapes=[pltpu.VMEM((rows, width), F32), pltpu.VMEM((pad, width), F32)],
        compiler_params=params(60),
        cost_estimate=pl.CostEstimate(
            flops=4 * rows * width * total, bytes_accessed=30 * MIB, transcendentals=0),
        name="last",
    )(g, a1, w, images, gx, vec)


def shards_any(
    images, grid_sizes, keep_flags, attn_gain, attn_shift, attend_weight, query_bias, value_bias,
    output_weight, output_bias, mlp_gain, mlp_shift, up_weight, up_bias, down_weight, down_bias,
    cotangent,
):
    n, seq, width = images.shape
    pad = -(-seq // 32) * 32
    counts = grid_sizes[:, 0] * grid_sizes[:, 1] + 2
    depth = keep_flags.astype(F32) / KEEP_PROB
    owners = width // attn_gain.shape[0]

    small = jnp.concatenate([
        attn_gain, attn_shift, query_bias, value_bias, output_bias, mlp_gain, mlp_shift, down_bias, up_bias])
    small = lax.all_gather(small.reshape(1, -1), "fsdp", axis=0, tiled=True).astype(F32)
    share = attn_gain.shape[0]
    vec = jnp.stack([small[:, k * share:(k + 1) * share].reshape(width) for k in range(8)])
    bu = small[:, 8 * share:].reshape(1, -1)

    attend = lax.all_gather(attend_weight.T, "fsdp", axis=0, tiled=True)
    out_w = lax.all_gather(output_weight, "fsdp", axis=0, tiled=True)
    up = lax.all_gather(up_weight.T, "fsdp", axis=0, tiled=True)
    down = lax.all_gather(down_weight, "fsdp", axis=0, tiled=True)

    a1, gm, qkv, o, lse = front(counts, depth, images, cotangent, attend, vec, pad)
    x1, a2, sums_two = middle(counts, depth, o, images, out_w, vec, pad)
    flat = lambda array: array.reshape(n * pad, array.shape[-1])
    block = up_weight.shape[1] if up_weight.shape[1] % 128 == 0 else 384
    dup, ddown, gbu, y, gx, ga, vec_feed = feed(
        counts, depth, flat(a2), flat(gm), up, down, bu, x1, cotangent, vec, seq, pad, block)
    dout = outgrad(flat(o), flat(ga))
    g = back(counts, ga, out_w, qkv, lse)
    dattend, cols, gi, vec_last = last(flat(g), flat(a1), attend, images, gx, vec, pad)

    sums = jnp.stack([jnp.sum(sums_two[:, 0]), jnp.sum(sums_two[:, 1]), jnp.sum(vec_feed[4]),
                      jnp.sum(counts).astype(F32)])

    def spread(array):
        return lax.psum(lax.psum_scatter(array, "fsdp", scatter_dimension=0, tiled=True), "dp")

    def columns(array):
        hidden = up.shape[0]
        array = jnp.swapaxes(array, 0, 1).reshape(width, owners, hidden // owners)
        return jnp.swapaxes(array, 0, 1)

    gup = spread(columns(dup))[0]
    gdown = spread(columns(ddown))[0].T
    gout = spread(dout)
    gattend = spread(dattend).T
    rows = jnp.concatenate([
        vec_last[0:2], cols[:, :width], cols[:, 2 * width:], vec_feed[3:4], vec_feed[0:3],
    ], 0)
    tiny = jnp.concatenate([
        jnp.swapaxes(rows.reshape(8, owners, share), 0, 1).reshape(owners, 8 * share),
        gbu.reshape(owners, -1)], 1)
    tiny = spread(tiny)[0]
    sums = lax.psum(sums, ("dp", "fsdp"))
    root_means = jnp.sqrt(sums[:3] / (sums[3] * width))
    tv = [tiny[k * share:(k + 1) * share] for k in range(8)]
    f = lambda array: array.astype(F32)
    return (y, gi, tv[0], tv[1], f(gattend), tv[2], tv[3], f(gout), tv[4], tv[5], tv[6],
            f(gup), tiny[8 * share:], f(gdown), tv[7], root_means)


def over_dp(array, m):
    return lax.ppermute(array, "dp", [(i, i ^ m) for i in range(4)])


def over_z(array, a):
    return lax.ppermute(array, "fsdp", [(i, i ^ (2 * a)) for i in range(8)])


def over_core(array):
    return lax.ppermute(array, "fsdp", [(i, i ^ 1) for i in range(8)])


def staged(kernel, ids, arrays, out_shape, name):
    size = sum(math.prod(s.shape) * s.dtype.itemsize for s in [*arrays, *out_shape])
    return pl.pallas_call(
        kernel,
        out_shape=out_shape,
        grid_spec=pltpu.PrefetchScalarGridSpec(
            num_scalar_prefetch=1, grid=(1,),
            in_specs=[whole(s.shape) for s in arrays],
            out_specs=[whole(s.shape) for s in out_shape]),
        compiler_params=params(60),
        cost_estimate=pl.CostEstimate(flops=0, bytes_accessed=size, transcendentals=0),
        name=name,
    )(ids, *arrays)


def simple(kernel, ids, arrays, out_shape, name, scratch=()):
    size = sum(math.prod(s.shape) * s.dtype.itemsize for s in [*arrays, *out_shape])
    inside = pl.BlockSpec(memory_space=pltpu.VMEM)
    return pl.pallas_call(
        kernel,
        out_shape=out_shape,
        in_specs=[SMEM] + [inside] * len(arrays),
        out_specs=[inside] * len(out_shape),
        scratch_shapes=list(scratch),
        compiler_params=pltpu.CompilerParams(vmem_limit_bytes=16 * MIB),
        cost_estimate=pl.CostEstimate(flops=0, bytes_accessed=size, transcendentals=0),
        name=name,
    )(ids, *arrays)


def pack_kernel(ids, at_ref, ow_ref, up_ref, down_ref, *refs):
    vectors, (own1, first1, own, first, rest) = refs[:9], refs[9:]
    q = ids[0]
    att = at_ref[...]
    up = jnp.transpose(up_ref[...])
    r = ow_ref.shape[0]
    for t in range(4):
        own1[t ^ q] = att[t * r:(t + 1) * r] if t < 3 else ow_ref[...]
        k = r // 3
        own[t ^ q, 0:k] = up[t * k:(t + 1) * k]
        own[t ^ q, k:2 * k] = down_ref[t * k:(t + 1) * k, :]
    k = 4 * (r // 3)
    rest[0] = up[k:]
    rest[1] = down_ref[k:, :]
    first1[0:r, :] = own1[0]
    pieces = [v[...].reshape(1, -1).astype(F32) for v in vectors]
    blank = jnp.zeros((1, first1.shape[1] - r), F32)
    rows = [jnp.concatenate([p, blank], 1) for p in pieces[:8]]
    rows += [jnp.concatenate([pieces[8][:, k * r:(k + 1) * r], blank], 1) for k in range(4)]
    rows.append(jnp.zeros((4, first1.shape[1]), F32))
    first1[r:r + 16, :] = jnp.concatenate(rows, 0).astype(BF16)
    first[...] = own[0]


def pack(ids, at, ow, up, down, vectors):
    r, width = ow.shape
    s = lambda *shape: jax.ShapeDtypeStruct(shape, BF16)
    return staged(pack_kernel, ids, [at, ow, up, down, *vectors],
                  [s(4, r, width), s(r + 16, width), s(4, 2 * r // 3, width), s(2 * r // 3, width), s(2, 8 * r // 3, width)],
                  "pack")


def after(value, *before):
    return lax.optimization_barrier((value, before))[0]


def line(ids, own, first, zr, xr):
    r, width = own.shape[1:]

    def kernel(ids, own, first, z1, z2, z3, x1, x2, x3, mine):
        zs, xs = (z1, z2, z3), (x1, x2, x3)
        for m in range(4):
            mine[m * r:(m + 1) * r] = own[m]
        mine[16 * r:16 * r + 16] = first[r:r + 16]
        for a in range(1, 4):
            at = 4 * a * r
            mine[at:at + r] = zs[a - 1][0:r]
            mine[16 * r + 16 * a:16 * r + 16 * a + 16] = zs[a - 1][r:r + 16]
            for m in range(1, 4):
                mine[at + m * r:at + (m + 1) * r] = xs[m - 1][a - 1]

    return simple(kernel, ids, [own, first, *zr, *xr], [jax.ShapeDtypeStruct((16 * r + 64, width), BF16)], "line")[0]


def stack_rows(ids, arrays, spans):
    width = arrays[0].shape[1]

    def kernel(ids, *refs):
        for out, (low, high) in zip(refs[3:], spans):
            for a in range(3):
                out[a] = refs[a][low:high]

    return simple(kernel, ids, arrays,
                  [jax.ShapeDtypeStruct((3, high - low, width), BF16) for low, high in spans], "stack")


def early_kernel(seq, pad, counts, depth, x_ref, cot_ref, norm_ref, gm_ref, xs):
    i = pl.program_id(0)
    width = x_ref.shape[-1]
    ok = lax.broadcasted_iota(jnp.int32, (pad, 1), 0) < counts[i]
    xs[pad - 8:pad, :] = jnp.zeros((8, width), F32)
    xs[0:seq, :] = cot_ref[0].astype(F32)
    gm_ref[0] = jnp.where(ok, xs[...] * depth[i, 1], 0.0).astype(BF16)
    xs[0:seq, :] = x_ref[0].astype(F32)
    norm_ref[0], _ = normalize(xs[...])


def early(counts, depth, images, cot, pad):
    n, seq, width = images.shape
    sd = jax.ShapeDtypeStruct
    return pl.pallas_call(
        functools.partial(early_kernel, seq, pad),
        out_shape=[sd((n, pad, width), F32), sd((n, pad, width), BF16)],
        grid_spec=pltpu.PrefetchScalarGridSpec(
            num_scalar_prefetch=2, grid=(n,),
            in_specs=[by_image((seq, width)), by_image((seq, width))],
            out_specs=[by_image((pad, width)), by_image((pad, width))],
            scratch_shapes=[pltpu.VMEM((pad, width), F32)]),
        compiler_params=params(16),
        cost_estimate=pl.CostEstimate(flops=10 ** 7, bytes_accessed=9 * MIB, transcendentals=0),
        name="early",
    )(counts, depth, images, cot)


def head_kernel(pad, ids, counts, mine, sib, norm_ref, at_out, ow_out, vec_ref, b2_ref, b3_ref,
                a1_ref, qkv_ref, o_ref, lse_ref, at_s, ow_s, lse_s, sems):
    q, z, c = ids[0], ids[1], ids[2]
    copies = [pltpu.make_async_copy(at_s, at_out, sems.at[0]), pltpu.make_async_copy(ow_s, ow_out, sems.at[1])]
    step = pl.program_id(0)

    @pl.when(step == 0)
    def _():
        r = ow_s.shape[0] // 8
        cut = b2_ref.shape[2]
        for j in range(8):
            a = (j >> 1) ^ z
            own = ((j & 1) ^ c) == 0

            def place(ref_in):
                small = ref_in[pl.ds(pl.multiple_of(16 * r + 16 * a, 16), 16), 0:r].astype(F32)
                vec_ref[0:8, j * r:(j + 1) * r] = small[0:8]
                for k in range(4):
                    row = small[8 + k:9 + k]
                    at, to = k * r, (k + 1) * r
                    if at < cut:
                        b2_ref[j, :, at:min(to, cut)] = row[:, 0:min(to, cut) - at]
                    if to > cut:
                        b3_ref[j, :, max(at, cut) - cut:to - cut] = row[:, max(at, cut) - at:]
                for t in range(4):
                    ref, at = (ow_s, j * r) if t == 3 else (at_s, (3 * j + t) * r)
                    ref[at:at + r, :] = ref_in[pl.ds(pl.multiple_of((4 * a + (t ^ q)) * r, r), r), :]

            @pl.when(own)
            def _():
                place(mine)

            @pl.when(jnp.logical_not(own))
            def _():
                place(sib)

        for copy in copies:
            copy.start()

    attend_image(pad, counts[step], norm_ref[0], at_s, vec_ref, a1_ref, qkv_ref, o_ref, lse_ref, lse_s)

    @pl.when(step == pl.num_programs(0) - 1)
    def _():
        for copy in copies:
            copy.wait()


def head(ids, counts, mine, sib, norm):
    n, pad, width = norm.shape
    r = width // 8
    cut = 4 * r // 3
    sd = jax.ShapeDtypeStruct
    far = pl.BlockSpec(memory_space=pl.ANY)
    return pl.pallas_call(
        functools.partial(head_kernel, pad),
        out_shape=[
            sd((24 * r, width), BF16), sd((8 * r, width), BF16), sd((8, width), F32), sd((8, 1, cut), F32),
            sd((8, 1, 4 * r - cut), F32),
            sd((n, pad, width), BF16), sd((n, pad, 3 * width), BF16),
            sd((n, pad, width), BF16), sd((n, 16, pad), F32),
        ],
        grid_spec=pltpu.PrefetchScalarGridSpec(
            num_scalar_prefetch=2, grid=(n,),
            in_specs=[whole(mine.shape), whole(sib.shape), by_image((pad, width))],
            out_specs=[
                far, far, whole((8, width)), whole((8, 1, cut)), whole((8, 1, 4 * r - cut)),
                by_image((pad, width)), by_image((pad, 3 * width)),
                by_image((pad, width)), by_image((16, pad)),
            ],
            scratch_shapes=[
                pltpu.VMEM((24 * r, width), BF16), pltpu.VMEM((8 * r, width), BF16),
                pltpu.VMEM((pad, 128), F32), pltpu.SemaphoreType.DMA((2,))]),
        compiler_params=params(60),
        cost_estimate=pl.CostEstimate(
            flops=2 * n * pad * width * (3 * width + 4 * pad), bytes_accessed=20 * MIB,
            transcendentals=n * 12 * pad * pad),
        name="head",
    )(ids, counts, mine, sib, norm)


def part_kernel(seq, pad, second, group, ids, counts, depth, a2_ref, gm_ref, *rest):
    if second:
        weights, bu_ref, *rest = rest
    else:
        sides, bu_ref, rest = (rest[0:5], rest[5:10]), rest[10], rest[11:]
    if second:
        (mlp_in, ga2_in, a2t_in, gmt_in, x1_in, cot_ref, vecs,
         both, gbu_ref, y_ref, vec_ref, gx_out, ga_out,
         a2t, gmt, mlp, ga2, hs, gus, mlp_s, ga2_s, x1_s, ga_s, cs, sems, out_sems) = rest
        loads = [pltpu.make_async_copy(a, b, sems.at[k]) for k, (a, b) in enumerate(
            ((a2t_in, a2t), (gmt_in, gmt), (mlp_in, mlp_s), (ga2_in, ga2_s), (x1_in, x1_s)))]
    else:
        both, gbu_ref, mlp_out, ga2_out, a2t_out, gmt_out, a2t, gmt, mlp, ga2, hs, gus, sems = rest
        stores = [pltpu.make_async_copy(a, b, sems.at[k]) for k, (a, b) in enumerate(
            ((a2t, a2t_out), (gmt, gmt_out), (mlp, mlp_out), (ga2, ga2_out)))]
    step = pl.program_id(0)
    end = pl.num_programs(0) - 1
    q, z, c = ids[0], ids[1], ids[2]
    rows, width = a2_ref.shape
    n = rows // pad
    block = bu_ref.shape[-1]

    @pl.when(step == 0)
    def _():
        if second:
            for copy in loads:
                copy.start()
        else:
            a2t[...] = jnp.transpose(a2_ref[...])
            gmt[...] = jnp.transpose(gm_ref[...])
            stores[0].start()
            stores[1].start()
        mlp[...] = jnp.zeros_like(mlp)
        ga2[...] = jnp.zeros_like(ga2)

    pairs = [(k, side) for k in range(group) for side in range(2)]
    owners = [(((step * group + k) ^ z) << 1) | (c ^ side) for k, side in pairs]
    def piece(k, side, t, low):
        own, message, *crossed = sides[side]
        slot, m = step * group + k, t ^ q
        at = slice(low, low + r)
        index = jnp.maximum(slot - 1, 0) if group > 1 else 0
        value = message[index, at]
        for x, ref in enumerate(crossed):
            value = jnp.where(m == x + 1, ref[index, at], value)
        return jnp.where(slot == 0, own[m, at], value)

    if second:
        up, down = (jnp.concatenate([weights[c, kind], weights[c ^ 1, kind]], 0) for kind in range(2))
    else:
        r = sides[0][0].shape[1] // 2
        up = jnp.concatenate([piece(k, side, t, 0) for k, side in pairs for t in range(4)], 0)
        down = jnp.concatenate([piece(k, side, t, r) for k, side in pairs for t in range(4)], 0)
    bu = jnp.concatenate([bu_ref[owner] for owner in owners], 1)
    gbu = jnp.zeros(bu.shape, F32)
    ready = None
    for i in range(n + 1):
        if i < n:
            at = slice(i * pad, (i + 1) * pad)
            fresh = nt(a2_ref[at, :], up) + bu, nt(gm_ref[at, :], down)
        if ready is not None:
            at = slice((i - 1) * pad, i * pad)
            u, t = ready
            act, slope = gelu_pair(u)
            h = act.astype(BF16)
            gu = (t * slope).astype(BF16)
            hs[at, :] = h
            gus[at, :] = gu
            gbu = gbu + col_sum(gu.astype(F32))
            mlp[at, :] += nn(h, down)
            ga2[at, :] += nn(gu, up)
        ready = fresh
    for p, owner in enumerate(owners):
        gbu_ref[owner] = gbu[:, p * block:(p + 1) * block]

    if second:
        @pl.when(step == 0)
        def _():
            loads[0].wait()
            loads[1].wait()
    else:
        @pl.when(step == end)
        def _():
            stores[2].start()
            stores[3].start()

    part = width // 4
    span = 2 * group
    for t in range(4):
        at = slice(t * part, (t + 1) * part)
        for kind, (left, right) in enumerate(((a2t, gus), (gmt, hs))):
            d = nn(left[at, :], right[...]).astype(BF16)
            for p, owner in enumerate(owners):
                both[owner % span, t, kind] = d[:, p * block:(p + 1) * block]

    if not second:
        @pl.when(step == end)
        def _():
            for copy in stores:
                copy.wait()
        return

    @pl.when(step == end)
    def _():
        for copy in loads[2:]:
            copy.wait()
        mask_rows = lax.broadcasted_iota(jnp.int32, (pad, 1), 0)
        cs[pad - 8:pad, :] = jnp.zeros((8, width), F32)
        sums = [jnp.zeros((1, width), F32)] * 5
        outs = []
        for i in range(n):
            at = slice(i * pad, (i + 1) * pad)
            ok = mask_rows < counts[i]
            x1 = x1_s[i]
            out = mlp[at, :] + mlp_s[at, :] + vecs[7:8, :]
            y_ref[i] = jnp.where(ok, x1 + depth[i, 1] * out, 0.0).astype(BF16)[0:seq]
            cs[0:seq, :] = cot_ref[i].astype(F32)
            g = jnp.where(ok, cs[...], 0.0)
            back = ga2[at, :] + ga2_s[at, :]
            normed, rstd = normalize(x1)
            e = back * vecs[5:6, :]
            gx = g + rstd * (e - mean_row(e) - normed * mean_row(e * normed))
            ga = (depth[i, 0] * gx).astype(BF16)
            x1_s[i] = gx
            ga_s[i] = ga
            for k, (ref, to) in enumerate(((x1_s, gx_out), (ga_s, ga_out))):
                copy = pltpu.make_async_copy(ref.at[i], to.at[i], out_sems.at[i, k])
                copy.start()
                outs.append(copy)
            terms = (back * normed, back, gm_ref[at, :].astype(F32), ga.astype(F32), jnp.where(ok, out * out, 0.0))
            sums = [total + col_sum(term) for total, term in zip(sums, terms)]
        for k, total in enumerate(sums):
            vec_ref[k:k + 1, :] = total
        vec_ref[5:8, :] = jnp.zeros((3, width), F32)
        for copy in outs:
            copy.wait()


def part(ids, counts, depth, a2, gm, weights, bu, pad, group, carry=(), x1=None, cot=None, vec=None):
    rows, width = a2.shape
    n = rows // pad
    block = bu.shape[-1]
    second = len(carry) > 0
    sd = jax.ShapeDtypeStruct
    if second:
        w_specs = [pl.BlockSpec((2, 2, block, width), lambda s, ids, *_: (s ^ ids[1], 0, 0, 0))]
    else:
        w_specs = [whole(w.shape) for w in weights]
    far = pl.BlockSpec(memory_space=pl.ANY)
    acc = sd((rows, width), F32)
    tr = sd((width, rows), BF16)
    in_specs = [whole(a2.shape), whole(gm.shape)] + w_specs + [whole(bu.shape)]
    args = [a2, gm, *weights, bu]
    outs = [sd((8, 4, 2, width // 4, block), BF16), sd((8, 1, block), F32)]
    out_specs = [
        pl.BlockSpec((2 * group, 4, 2, width // 4, block), lambda s, ids, *_: (s ^ (ids[1] // group), 0, 0, 0, 0)),
        whole((8, 1, block))]
    scratch = [pltpu.VMEM(tr.shape, BF16), pltpu.VMEM(tr.shape, BF16), pltpu.VMEM(acc.shape, F32),
               pltpu.VMEM(acc.shape, F32), pltpu.VMEM((rows, 2 * group * block), BF16),
               pltpu.VMEM((rows, 2 * group * block), BF16)]
    if second:
        seq = cot.shape[1]
        args += [*carry, x1, cot, vec]
        in_specs += [far] * 5 + [whole(cot.shape), whole(vec.shape)]
        outs += [sd((n, seq, width), BF16), sd((8, width), F32), sd((n, pad, width), F32), sd((n, pad, width), BF16)]
        out_specs += [whole((n, seq, width)), whole((8, width)), far, far]
        scratch += [pltpu.VMEM(acc.shape, F32), pltpu.VMEM(acc.shape, F32), pltpu.VMEM((n, pad, width), F32),
                    pltpu.VMEM((n, pad, width), BF16), pltpu.VMEM((pad, width), F32), pltpu.SemaphoreType.DMA((5,)),
                    pltpu.SemaphoreType.DMA((n, 2))]
    else:
        seq = 0
        outs += [acc, acc, tr, tr]
        out_specs += [far] * 4
        scratch += [pltpu.SemaphoreType.DMA((4,))]
    return pl.pallas_call(
        functools.partial(part_kernel, seq, pad, second, group),
        out_shape=outs,
        grid_spec=pltpu.PrefetchScalarGridSpec(
            num_scalar_prefetch=3, grid=(4 // group,), in_specs=in_specs, out_specs=out_specs,
            scratch_shapes=scratch),
        compiler_params=params(60),
        cost_estimate=pl.CostEstimate(
            flops=12 * rows * width * 8 * block, bytes_accessed=30 * MIB, transcendentals=0),
        name="feed_b" if second else "feed_a",
    )(ids, counts, depth, *args)


def back_first_kernel(pad, ids, counts, ga_ref, w_ref, qkv_ref, lse_ref, o_in, a1_in, g_out, near_p, far_p, near_q, far_q,
                      go, g_s, o_s, a1_s, sems, out_sems):
    i = pl.program_id(0)
    n, _, width = ga_ref.shape
    loads = [pltpu.make_async_copy(o_in, o_s, sems.at[0]), pltpu.make_async_copy(a1_in, a1_s, sems.at[1])]

    @pl.when(i == 0)
    def _():
        for copy in loads:
            copy.start()

    back_image(pad, counts[i], ga_ref.at[i], w_ref, qkv_ref, lse_ref, g_s.at[i], go)
    pltpu.make_async_copy(g_s.at[i], g_out.at[i], out_sems.at[i]).start()

    @pl.when(i == n - 1)
    def _():
        for copy in loads:
            copy.wait()
        q, z, c = ids[0], ids[1], ids[2]
        r = near_p.shape[2]

        def put(value, group, j, t):
            a, m = ((j >> 1) ^ z) & 1, t ^ q
            own = ((j & 1) ^ c) == 0

            @pl.when(own)
            def _():
                group[0][m, a] = value

            @pl.when(jnp.logical_not(own))
            def _():
                group[1][m, a] = value

        for group, side in (((near_p, far_p), 1 - (z >> 1)), ((near_q, far_q), z >> 1)):
            for s in range(4):
                if s < 3:
                    cols = pl.ds(pl.multiple_of(side * (12 * r) + s * (4 * r), 128), 4 * r)
                    left = g_s[:, :, cols].reshape(n * pad, 4 * r)
                    d = tn(left, a1_s[...].reshape(n * pad, width)).astype(BF16)
                else:
                    cols = pl.ds(pl.multiple_of(side * (4 * r), 128), 4 * r)
                    left = o_s[:, :, cols].reshape(n * pad, 4 * r)
                    d = tn(left, ga_ref[...].reshape(n * pad, width)).astype(BF16)
                for k in range(4):
                    chunk = 4 * s + k
                    value = d[k * r:(k + 1) * r]
                    if s < 3:
                        put(value, group, 4 * side + chunk // 3, chunk % 3)
                    else:
                        put(value, group, 4 * side + k, 3)
        for k in range(n):
            pltpu.make_async_copy(g_s.at[k], g_out.at[k], out_sems.at[k]).wait()


def back_first(ids, counts, ga, w, qkv, lse, o, a1):
    n, pad, width = ga.shape
    r = width // 8
    sd = jax.ShapeDtypeStruct
    far = pl.BlockSpec(memory_space=pl.ANY)
    group = sd((4, 2, r, width), BF16)
    return pl.pallas_call(
        functools.partial(back_first_kernel, pad),
        out_shape=[sd((n, pad, 3 * width), BF16)] + [group] * 4,
        grid_spec=pltpu.PrefetchScalarGridSpec(
            num_scalar_prefetch=2, grid=(n,),
            in_specs=[whole(ga.shape), whole(w.shape), by_image((pad, 3 * width)), by_image((16, pad)), far, far],
            out_specs=[far] + [whole(group.shape)] * 4,
            scratch_shapes=[
                pltpu.VMEM((pad, width), BF16), pltpu.VMEM((n, pad, 3 * width), BF16), pltpu.VMEM((n, pad, width), BF16),
                pltpu.VMEM((n, pad, width), BF16), pltpu.SemaphoreType.DMA((2,)), pltpu.SemaphoreType.DMA((n,))]),
        compiler_params=params(60),
        cost_estimate=pl.CostEstimate(
            flops=2 * n * pad * width * (3 * width + 10 * pad), bytes_accessed=16 * MIB,
            transcendentals=n * 12 * pad * pad),
        name="back",
    )(ids, counts, ga, w, qkv, lse, o, a1)


def final_kernel(seq, pad, g_ref, w_ref, x_ref, gx_ref, y_ref, vecs, gi_ref, y_out, vec_ref, cols_ref, xs):
    i = pl.program_id(0)
    width = x_ref.shape[-1]
    grad = nn(g_ref[0], w_ref[...])
    xs[pad - 8:pad, :] = jnp.zeros((8, width), F32)
    xs[0:seq, :] = x_ref[0].astype(F32)
    normed, rstd = normalize(xs[...])

    @pl.when(i == 0)
    def _():
        vec_ref[...] = jnp.zeros_like(vec_ref)
        cols_ref[...] = jnp.zeros_like(cols_ref)

    vec_ref[0:1, :] += col_sum(grad * normed)
    vec_ref[1:2, :] += col_sum(grad)
    cols_ref[...] += col_sum(g_ref[0].astype(F32))
    e = grad * vecs[0:1, :]
    gi = gx_ref[0] + rstd * (e - mean_row(e) - normed * mean_row(e * normed))
    for k in range(gi_ref.shape[1]):
        @pl.when(i == k)
        def _():
            gi_ref[:, k, :] = gi[0:seq]
            y_out[:, k, :] = y_ref[0]


def final(g, w, images, gx, y, vec, pad):
    n, seq, width = images.shape
    sd = jax.ShapeDtypeStruct
    return pl.pallas_call(
        functools.partial(final_kernel, seq, pad),
        out_shape=[sd((seq, n, width), F32), sd((seq, n, width), BF16), sd((8, width), F32), sd((1, 3 * width), F32)],
        grid=(n,),
        in_specs=[by_image((pad, 3 * width)), whole(w.shape), by_image((seq, width)), by_image((pad, width)),
                  by_image((seq, width)), whole(vec.shape)],
        out_specs=[whole((seq, n, width)), whole((seq, n, width)), whole((8, width)), whole((1, 3 * width))],
        scratch_shapes=[pltpu.VMEM((pad, width), F32)],
        compiler_params=params(60),
        cost_estimate=pl.CostEstimate(
            flops=6 * n * pad * width * width, bytes_accessed=18 * MIB, transcendentals=0),
        name="final",
    )(g, w, images, gx, y, vec)


def add_pair(ids, near, got):
    slots, parts = near.shape[:2]
    shape = near.shape[1:]
    block = pl.BlockSpec((slots, 1) + shape[1:], lambda a, *_: (0, a) + (0,) * (len(shape) - 1))

    def kernel(a_ref, b_ref, *outs):
        for m in range(4):
            outs[m][...] = (a_ref[m].astype(F32) + b_ref[m].astype(F32)).astype(BF16)

    return pl.pallas_call(
        kernel,
        out_shape=[jax.ShapeDtypeStruct(shape, BF16)] * slots,
        grid=(parts,),
        in_specs=[block, block],
        out_specs=[pl.BlockSpec((1,) + shape[1:], lambda a: (a,) + (0,) * (len(shape) - 1))] * slots,
        compiler_params=params(60),
        cost_estimate=pl.CostEstimate(flops=0, bytes_accessed=6 * near.size, transcendentals=0),
        name="add_pair",
    )(near, got)


def add_four(ids, parts, split):
    shape = parts[0].shape

    def kernel(ids, a, b, c, d, *outs):
        if split:
            for k in range(shape[0]):
                outs[k][...] = ((a[k].astype(F32) + b[k].astype(F32)) + (c[k].astype(F32) + d[k].astype(F32))).astype(BF16)
        else:
            outs[0][...] = ((a[...].astype(F32) + b[...].astype(F32)) + (c[...].astype(F32) + d[...].astype(F32))).astype(BF16)

    count = shape[0] if split else 1
    out = jax.ShapeDtypeStruct(shape[1:] if split else shape, BF16)
    return simple(kernel, ids, parts, [out] * count, "add_four")


def merge(ids, s2, s3):
    _, _, rows, k2 = s2.shape
    k3 = s3.shape[3]

    def kernel(ids, a, b, out):
        for ref, at, to in ((a, 0, k2), (b, k2, k2 + k3)):
            out[:, :, at:to] = ((ref[0].astype(F32) + ref[1].astype(F32)) + (ref[2].astype(F32) + ref[3].astype(F32))).astype(BF16)

    return simple(kernel, ids, [s2, s3], [jax.ShapeDtypeStruct((2, rows, k2 + k3), BF16)], "merge")[0]


def place_feed_kernel(ids, p0, p1, p2, p3, up_ref, down_ref, cs):
    q = ids[0]
    rows = p0.shape[1]
    for m, p in enumerate((p0, p1, p2, p3)):
        to = pl.ds(pl.multiple_of((q ^ m) * rows, rows), rows)
        up_ref[to, :] = p[0].astype(F32)
        cs[to, :] = p[1].astype(F32)
    down_ref[...] = jnp.transpose(cs[...])


def place_feed(ids, parts):
    _, rows, block = parts[0].shape
    sd = jax.ShapeDtypeStruct
    return simple(place_feed_kernel, ids, parts, [sd((4 * rows, block), F32), sd((block, 4 * rows), F32)],
                  "place_feed", scratch=[pltpu.VMEM((4 * rows, block), F32)])


def place_attend_kernel(ids, p0, p1, p2, p3, at_ref, ow_ref, cs):
    q = ids[0]
    r = p0.shape[0]
    for m, p in enumerate((p0, p1, p2, p3)):
        cs[pl.ds(pl.multiple_of((q ^ m) * r, r), r), :] = p[...].astype(F32)
    at_ref[...] = cs[0:3 * r, :]
    ow_ref[...] = cs[3 * r:4 * r, :]


def place_attend(ids, parts):
    r, width = parts[0].shape
    sd = jax.ShapeDtypeStruct
    return simple(place_attend_kernel, ids, parts, [sd((3 * r, width), F32), sd((r, width), F32)],
                  "place_attend", scratch=[pltpu.VMEM((4 * r, width), F32)])


def cut_vectors(ids, rows, share):
    width = rows.shape[1]
    parts = width // share

    def kernel(ids, rows_ref, *outs):
        owner = 2 * ids[1] + ids[2]
        vectors, bias = outs[:8], outs[8]
        for j in range(parts):
            @pl.when(owner == j)
            def _():
                for k in range(8):
                    vectors[k][...] = rows_ref[k:k + 1, j * share:(j + 1) * share].reshape(share)
                at = j * 4 * share
                bias[...] = rows_ref[8 + at // width:9 + at // width, at % width:at % width + 4 * share].reshape(4 * share)

    sd = jax.ShapeDtypeStruct
    return simple(kernel, ids, [rows], [sd((share,), F32)] * 8 + [sd((4 * share,), F32)], "cut_vectors")


def shards_grid(
    images, grid_sizes, keep_flags, attn_gain, attn_shift, attend_weight, query_bias, value_bias,
    output_weight, output_bias, mlp_gain, mlp_shift, up_weight, up_bias, down_weight, down_bias,
    cotangent,
):
    n, seq, width = images.shape
    pad = -(-seq // 32) * 32
    counts = grid_sizes[:, 0] * grid_sizes[:, 1] + 2
    depth = keep_flags.astype(F32) / KEEP_PROB
    owners = 8
    share = attn_gain.shape[0]
    f = lax.axis_index("fsdp")
    ids = jnp.stack([lax.axis_index("dp"), f >> 1, f & 1]).astype(jnp.int32)

    z_all = lambda array: [over_z(array, a) for a in (1, 2, 3)]
    dp_all = lambda array: [over_dp(array, m) for m in (1, 2, 3)]
    dp_out = lambda s: [s[0]] + [over_dp(s[m], m) for m in (1, 2, 3)]
    z_out = lambda s: [s[0]] + [over_z(s[a], a) for a in (1, 2, 3)]
    tied = lax.optimization_barrier
    flat = lambda array: array.reshape(n * pad, array.shape[-1])

    own1, first1, own, first, rest = pack(
        ids, attend_weight.T, output_weight, up_weight, down_weight,
        [attn_gain, attn_shift, query_bias, value_bias, output_bias, mlp_gain, mlp_shift, down_bias, up_bias])
    zr1 = z_all(first1)
    own_other = over_core(own)
    first, rest, zr1, own_other = tied((first, rest, zr1, own_other))
    message1, = stack_rows(ids, zr1, [(0, share)])
    xr1 = dp_all(message1)
    zr = z_all(first)
    weights_b = lax.all_gather(rest[None], "fsdp", axis=0, tiled=True)
    norm, gm = early(counts, depth, images, cotangent, pad)
    xr1, zr, norm, gm = tied((xr1, zr, norm, gm))
    mine1 = line(ids, own1, first1, zr1, xr1)
    sib1 = over_core(mine1)
    message, = stack_rows(ids, zr, [(0, first.shape[0])])
    message_other = over_core(message)
    xr = dp_all(message)
    sib1, message_other = tied((sib1, message_other))
    attend, out_w, vec, bu2, bu3, a1, qkv, o, lse = head(ids, counts, mine1, sib1, norm)
    o, xr = tied((o, xr))
    sib = [own_other, message_other, *(over_core(x) for x in xr)]
    x1, a2, sums_two = middle(counts, depth, o, images, out_w, vec, pad)
    x1, a2, sib = tied((x1, a2, sib))
    a2, gm = flat(a2), flat(gm)
    both2, gbu2, mlp, ga2, a2t, gmt = part(
        ids, counts, depth, a2, gm, [own, message, *xr, *sib], bu2, pad, 2)
    mlp, weights_b = tied((mlp, weights_b))

    own_sum = lambda both: lax.psum_scatter(
        both.reshape(-1, both.shape[-1]), "fsdp", scatter_dimension=0, tiled=True).reshape(both.shape[1:])
    quarter = lambda shard: lax.all_to_all(shard, "dp", 0, 0, tiled=True)
    shard2 = own_sum(both2)
    both3, gbu3, y, vec_feed, gx, ga = part(
        ids, counts, depth, a2, gm, [weights_b], bu3, pad, 1, (mlp, ga2, a2t, gmt), x1, cotangent, vec)
    shard3 = own_sum(both3)
    quarter2 = quarter(after(shard2, ga))
    g, near_p, far_p, near_q, far_q = back_first(ids, counts, ga, out_w, qkv, lse, o, a1)
    g, near_p, far_p, near_q, far_q, quarter2 = tied((g, near_p, far_p, near_q, far_q, quarter2))
    got_p = over_core(far_p)
    got_q = over_core(far_q)
    s_p = add_pair(ids, near_p, got_p)
    dr_p = dp_out(s_p)
    gi, y, vec_last, cols = final(after(g, s_p), attend, images, gx, y, vec, pad)
    y, gi = y.swapaxes(0, 1), gi.swapaxes(0, 1)
    rows = jnp.concatenate([
        vec_last[0:2], cols[:, :width], cols[:, 2 * width:], vec_feed[3:4], vec_feed[0:3],
        jnp.concatenate([gbu2[:, 0], gbu3[:, 0]], 1).reshape(4, width), sums_two[:, 0:2].sum(0), vec_feed[4:5],
        jnp.full((1, width), jnp.sum(counts).astype(F32)),
    ], 0)
    rows = rows + over_core(rows)
    rows, got_q, dr_p = tied((rows, got_q, dr_p))
    s_q = add_pair(ids, near_q, got_q)
    rows = rows + over_dp(rows, 1)
    s_q, rows = tied((s_q, rows))
    dr_q = dp_out(s_q)
    quarter3 = quarter(after(shard3, s_q))
    e_p = add_four(ids, after(dr_p, s_q), True)
    er_p = [over_z(x, a) for a, x in zip((2, 3), e_p)]
    er_p, dr_q, rows, quarter3 = tied((er_p, dr_q, rows, quarter3))
    e_q = add_four(ids, dr_q, True)
    er_q = over_z(e_q[1], 1)
    rows = after(rows, e_q)
    rows = rows + over_dp(rows, 2)
    f3 = merge(ids, quarter2, after(quarter3, e_q))
    fr3 = [f3] + dp_all(f3)
    er_q, fr3[1], fr3[2] = tied((er_q, fr3[1], fr3[2]))
    f1 = add_four(ids, [e_q[0], er_q, *er_p], False)[0]
    fr1 = [f1] + dp_all(f1)
    got = z_all(after(rows, f1))
    rows = (rows + got[0]) + (got[1] + got[2])
    root_means = jnp.sqrt(jnp.sum(rows[12:15], 1) / (rows[15, 0] * width))
    *tv, gub = cut_vectors(ids, rows, share)
    gup, gdown = place_feed(ids, fr3)
    gattend, gout = place_attend(ids, fr1)
    gattend = gattend.T
    return (y, gi, tv[0], tv[1], gattend, tv[2], tv[3], gout, tv[4], tv[5], tv[6],
            gup, gub, gdown, tv[7], root_means)


def shards(on_grid, *args):
    images, attn_gain, up_weight = args[0], args[3], args[12]
    share = attn_gain.shape[0]
    fits = on_grid and share % 48 == 0 and up_weight.shape[1] == 4 * share and images.shape[2] == 8 * share
    return (shards_grid if fits else shards_any)(*args)


def solution(mesh):
    images = P(("dp", "fsdp"), None, None)
    flags = P(("dp", "fsdp"), None)
    vec, rows, cols = P("fsdp"), P("fsdp", None), P(None, "fsdp")
    return jax.shard_map(
        functools.partial(shards, dict(mesh.shape) == {"dp": 4, "fsdp": 8}),
        mesh=mesh,
        in_specs=(images, flags, flags, vec, vec, cols, vec, vec, rows, vec, vec, vec, cols, vec, rows,
                  vec, images),
        out_specs=(images, images, vec, vec, cols, vec, vec, rows, vec, vec, vec, cols, vec, rows, vec,
                   P()),
        check_vma=False,
    )
```

```python
import functools
import math

import jax
import jax.numpy as jnp
from jax import lax
from jax.experimental import pallas as pl
from jax.experimental.pallas import tpu as pltpu
from jax.sharding import PartitionSpec as P

HEAD_DIM = 64
EPS = 1e-06
KEEP_PROB = 0.9
MASKED = -1e30
INV_ROOT_TWO = 0.7071067811865476
INV_ROOT_TWO_PI = 0.3989422804014327
F32 = jnp.float32
BF16 = jnp.bfloat16
MIB = 1024 * 1024


def nn(left, right):
    return lax.dot_general(left, right, (((1,), (0,)), ((), ())), preferred_element_type=F32)


def nt(left, right):
    return lax.dot_general(left, right, (((1,), (1,)), ((), ())), preferred_element_type=F32)


def tn(left, right):
    return lax.dot_general(left, right, (((0,), (0,)), ((), ())), preferred_element_type=F32)


def mean_row(values):
    return jnp.sum(values, -1, keepdims=True) * (1.0 / values.shape[-1])


def normalize(values):
    center = values - mean_row(values)
    rstd = lax.rsqrt(mean_row(center * center) + EPS)
    return center * rstd, rstd


def col_sum(values):
    return jnp.sum(values, 0, keepdims=True)


def params(limit, steps=1):
    return pltpu.CompilerParams(
        dimension_semantics=("arbitrary",) * steps, vmem_limit_bytes=limit * MIB
    )


def whole(shape, buffers=1):
    zeros = (0,) * len(shape)
    return pl.BlockSpec(shape, lambda *_: zeros, pipeline_mode=pl.Buffered(buffers))


def by_image(shape):
    rest = (0,) * len(shape)
    return pl.BlockSpec((1,) + shape, lambda i, *_: (i,) + rest)


SMEM = pl.BlockSpec(memory_space=pltpu.SMEM)


def front_kernel(seq, pad, counts, depth, x_ref, cot_ref, w_ref, vec_ref,
                 a1_ref, gm_ref, qkv_ref, o_ref, lse_ref, xs, lse_s):
    i = pl.program_id(0)
    width = x_ref.shape[-1]
    count = counts[i]
    rows = lax.broadcasted_iota(jnp.int32, (pad, 1), 0)
    xs[pad - 8:pad, :] = jnp.zeros((8, width), F32)
    xs[0:seq, :] = cot_ref[0].astype(F32)
    gm_ref[0] = jnp.where(rows < count, xs[...] * depth[i, 1], 0.0).astype(BF16)
    xs[0:seq, :] = x_ref[0].astype(F32)
    normed, _ = normalize(xs[...])
    attend_image(pad, count, normed, w_ref, vec_ref, a1_ref, qkv_ref, o_ref, lse_ref, lse_s)


def attend_image(pad, count, normed, w_ref, vec_ref, a1_ref, qkv_ref, o_ref, lse_ref, lse_s):
    width = normed.shape[-1]
    pairs = width // 128
    a1 = (normed * vec_ref[0:1, :] + vec_ref[1:2, :]).astype(BF16)
    a1_ref[0] = a1
    for c in range(0, 3 * width, 384):
        part = nt(a1, w_ref[c:c + 384, :])
        if c < width:
            part = part + vec_ref[2:3, c:c + 384]
        elif c >= 2 * width:
            part = part + vec_ref[3:4, c - 2 * width:c - 2 * width + 384]
        qkv_ref[0, :, c:c + 384] = part.astype(BF16)
    ok = lax.broadcasted_iota(jnp.int32, (pad, pad), 1) < count
    lane = lax.broadcasted_iota(jnp.int32, (pad, 128), 1)
    lse_s[...] = jnp.zeros((pad, 128), F32)

    def mine(half):
        return (lane >= 64) if half else (lane < 64)

    def products(p):
        at = p * 128
        q = qkv_ref[0, :, at:at + 128] * 0.125
        k = qkv_ref[0, :, width + at:width + at + 128]
        return [nt(jnp.where(mine(half), q, 0), k) for half in range(2)]

    ready = None
    for p in range(pairs + 1):
        fresh = products(p) if p < pairs else None
        if ready is not None:
            at = (p - 1) * 128
            values = qkv_ref[0, :, 2 * width + at:2 * width + at + 128]
            total = jnp.zeros((pad, 128), F32)
            for half in range(2):
                scores = jnp.where(ok, ready[half], MASKED)
                top = jnp.max(scores, -1, keepdims=True)
                e = jnp.exp(scores - top)
                s = jnp.sum(e, -1, keepdims=True)
                prob = (e * (1.0 / s)).astype(BF16)
                total = total + nn(prob, jnp.where(mine(half), values, 0))
                lse_s[...] = jnp.where(lane == 2 * (p - 1) + half, top + jnp.log(s), lse_s[...])
            o_ref[0, :, at:at + 128] = total.astype(BF16)
        ready = fresh
    lse_ref[0] = jnp.transpose(lse_s[...])[0:16, :]


def front(counts, depth, images, cot, w, vec, pad):
    n, seq, width = images.shape
    grid_spec = pltpu.PrefetchScalarGridSpec(
        num_scalar_prefetch=2,
        grid=(n,),
        in_specs=[
            by_image((seq, width)), by_image((seq, width)),
            whole(w.shape), whole(vec.shape),
        ],
        out_specs=[
            by_image((pad, width)), by_image((pad, width)), by_image((pad, 3 * width)),
            by_image((pad, width)), by_image((16, pad)),
        ],
        scratch_shapes=[pltpu.VMEM((pad, width), F32), pltpu.VMEM((pad, 128), F32)],
    )
    return pl.pallas_call(
        functools.partial(front_kernel, seq, pad),
        out_shape=[
            jax.ShapeDtypeStruct((n, pad, width), BF16),
            jax.ShapeDtypeStruct((n, pad, width), BF16),
            jax.ShapeDtypeStruct((n, pad, 3 * width), BF16),
            jax.ShapeDtypeStruct((n, pad, width), BF16),
            jax.ShapeDtypeStruct((n, 16, pad), F32),
        ],
        grid_spec=grid_spec,
        compiler_params=params(60),
        cost_estimate=pl.CostEstimate(
            flops=2 * n * pad * width * (3 * width + 4 * pad), bytes_accessed=20 * MIB,
            transcendentals=n * 12 * pad * pad),
        name="front",
    )(counts, depth, images, cot, w, vec)


def middle_kernel(seq, pad, counts, depth, o_ref, x_ref, w_ref, vec_ref,
                  x1_ref, a2_ref, sums_ref, xs):
    i = pl.program_id(0)
    width = x_ref.shape[-1]
    rows = lax.broadcasted_iota(jnp.int32, (pad, 1), 0)
    ok = rows < counts[i]
    xs[pad - 8:pad, :] = jnp.zeros((8, width), F32)
    xs[0:seq, :] = x_ref[0].astype(F32)
    attn = nn(o_ref[0], w_ref[...]) + vec_ref[4:5, :]
    x1 = xs[...] + depth[i, 0] * attn
    x1_ref[0] = x1
    sums_ref[0, 0:1, :] = col_sum(jnp.where(ok, x1 * x1, 0.0))
    sums_ref[0, 1:2, :] = col_sum(jnp.where(ok, attn * attn, 0.0))
    sums_ref[0, 2:8, :] = jnp.zeros((6, width), F32)
    normed, _ = normalize(x1)
    a2_ref[0] = (normed * vec_ref[5:6, :] + vec_ref[6:7, :]).astype(BF16)


def middle(counts, depth, o, images, w, vec, pad):
    n, seq, width = images.shape
    grid_spec = pltpu.PrefetchScalarGridSpec(
        num_scalar_prefetch=2,
        grid=(n,),
        in_specs=[
            by_image((pad, width)), by_image((seq, width)),
            whole(w.shape), whole(vec.shape),
        ],
        out_specs=[by_image((pad, width)), by_image((pad, width)), by_image((8, width))],
        scratch_shapes=[pltpu.VMEM((pad, width), F32)],
    )
    return pl.pallas_call(
        functools.partial(middle_kernel, seq, pad),
        out_shape=[
            jax.ShapeDtypeStruct((n, pad, width), F32),
            jax.ShapeDtypeStruct((n, pad, width), BF16),
            jax.ShapeDtypeStruct((n, 8, width), F32),
        ],
        grid_spec=grid_spec,
        compiler_params=params(60),
        cost_estimate=pl.CostEstimate(
            flops=2 * n * pad * width * width, bytes_accessed=10 * MIB, transcendentals=0),
        name="middle",
    )(counts, depth, o, images, w, vec)


def gelu_pair(u):
    size = jnp.abs(u)
    t = 1.0 / (1.0 + (0.3275911 * INV_ROOT_TWO) * size)
    bell = jnp.exp(-0.5 * (u * u))
    series = t * (0.5 * 0.254829592 + t * (0.5 * -0.284496736 + t * (
        0.5 * 1.421413741 + t * (0.5 * -1.453152027 + t * (0.5 * 1.061405429)))))
    tail = series * bell
    phi = jnp.where(u >= 0, 1.0 - tail, tail)
    return u * phi, phi + u * (bell * INV_ROOT_TWO_PI)


def feed_kernel(seq, pad, counts, depth, a2_ref, gm_ref, up_ref, down_ref, bu_ref, x1_ref, cot_ref,
                vecs,
                dup_ref, ddown_ref, gbu_ref, y_ref, gx_ref, ga_ref, vec_ref,
                a2t, gmt, mlp, ga2, hs, gus, cs):
    j = pl.program_id(0)
    n = x1_ref.shape[0]

    @pl.when(j == 0)
    def _():
        a2t[...] = jnp.transpose(a2_ref[...])
        gmt[...] = jnp.transpose(gm_ref[...])
        mlp[...] = jnp.zeros_like(mlp)
        ga2[...] = jnp.zeros_like(ga2)

    gbu = jnp.zeros(bu_ref.shape[1:], F32)
    for i in range(n):
        at = slice(i * pad, (i + 1) * pad)
        u = nt(a2_ref[at, :], up_ref[...]) + bu_ref[0]
        t = nt(gm_ref[at, :], down_ref[...])
        act, slope = gelu_pair(u)
        h = act.astype(BF16)
        gu = (t * slope).astype(BF16)
        hs[at, :] = h
        gus[at, :] = gu
        gbu = gbu + col_sum(gu.astype(F32))
        mlp[at, :] += nn(h, down_ref[...])
        ga2[at, :] += nn(gu, up_ref[...])
    gbu_ref[0] = gbu
    dup_ref[0] = nn(a2t[...], gus[...]).astype(BF16)
    ddown_ref[0] = nn(gmt[...], hs[...]).astype(BF16)

    @pl.when(j == pl.num_programs(0) - 1)
    def _():
        width = x1_ref.shape[-1]
        rows = lax.broadcasted_iota(jnp.int32, (pad, 1), 0)
        cs[pad - 8:pad, :] = jnp.zeros((8, width), F32)
        msum = jnp.zeros((1, width), F32)
        ggain = jnp.zeros((1, width), F32)
        gshift = jnp.zeros((1, width), F32)
        gdown = jnp.zeros((1, width), F32)
        gout = jnp.zeros((1, width), F32)
        for i in range(n):
            at = slice(i * pad, (i + 1) * pad)
            ok = rows < counts[i]
            x1 = x1_ref[i]
            out = mlp[at, :] + vecs[7:8, :]
            msum = msum + col_sum(jnp.where(ok, out * out, 0.0))
            y_ref[i] = jnp.where(ok, x1 + depth[i, 1] * out, 0.0).astype(BF16)[0:seq]
            cs[0:seq, :] = cot_ref[i].astype(F32)
            g = jnp.where(ok, cs[...], 0.0)
            gdown = gdown + col_sum(gm_ref[at, :].astype(F32))
            back = ga2[at, :]
            normed, rstd = normalize(x1)
            ggain = ggain + col_sum(back * normed)
            gshift = gshift + col_sum(back)
            e = back * vecs[5:6, :]
            gx = g + rstd * (e - mean_row(e) - normed * mean_row(e * normed))
            gx_ref[i] = gx
            ga = (depth[i, 0] * gx).astype(BF16)
            ga_ref[i] = ga
            gout = gout + col_sum(ga.astype(F32))
        vec_ref[0:1, :] = ggain
        vec_ref[1:2, :] = gshift
        vec_ref[2:3, :] = gdown
        vec_ref[3:4, :] = gout
        vec_ref[4:5, :] = msum
        vec_ref[5:8, :] = jnp.zeros((3, width), F32)


def feed(counts, depth, a2, gm, up, down, bu, x1, cot, vec, seq, pad, block):
    rows, width = a2.shape
    n = rows // pad
    hidden = up.shape[0]
    steps = hidden // block
    at = lambda j, *_: (j, 0)
    at3 = lambda j, *_: (j, 0, 0)
    grid_spec = pltpu.PrefetchScalarGridSpec(
        num_scalar_prefetch=2,
        grid=(steps,),
        in_specs=[
            whole(a2.shape), whole(gm.shape),
            pl.BlockSpec((block, width), at), pl.BlockSpec((block, width), at),
            pl.BlockSpec((1, 1, block), at3),
            whole(x1.shape), whole(cot.shape), whole(vec.shape),
        ],
        out_specs=[
            pl.BlockSpec((1, width, block), at3), pl.BlockSpec((1, width, block), at3),
            pl.BlockSpec((1, 1, block), at3),
            whole((n, seq, width)), whole((n, pad, width)), whole((n, pad, width)), whole((8, width)),
        ],
        scratch_shapes=[
            pltpu.VMEM((width, rows), BF16), pltpu.VMEM((width, rows), BF16),
            pltpu.VMEM((rows, width), F32), pltpu.VMEM((rows, width), F32),
            pltpu.VMEM((rows, block), BF16), pltpu.VMEM((rows, block), BF16),
            pltpu.VMEM((pad, width), F32),
        ],
    )
    return pl.pallas_call(
        functools.partial(feed_kernel, seq, pad),
        out_shape=[
            jax.ShapeDtypeStruct((steps, width, block), BF16),
            jax.ShapeDtypeStruct((steps, width, block), BF16),
            jax.ShapeDtypeStruct((steps, 1, block), F32),
            jax.ShapeDtypeStruct((n, seq, width), BF16),
            jax.ShapeDtypeStruct((n, pad, width), F32),
            jax.ShapeDtypeStruct((n, pad, width), BF16),
            jax.ShapeDtypeStruct((8, width), F32),
        ],
        grid_spec=grid_spec,
        compiler_params=params(60),
        cost_estimate=pl.CostEstimate(
            flops=12 * rows * width * hidden, bytes_accessed=40 * MIB, transcendentals=rows * hidden),
        name="feed",
    )(counts, depth, a2, gm, up, down, bu.reshape(steps, 1, block), x1, cot, vec)


def back_kernel(pad, counts, ga_ref, w_ref, qkv_ref, lse_ref, g_ref, go):
    back_image(pad, counts[pl.program_id(0)], ga_ref.at[0], w_ref, qkv_ref, lse_ref, g_ref.at[0], go)


def back_image(pad, count, ga_ref, w_ref, qkv_ref, lse_ref, g_ref, go):
    width = ga_ref.shape[-1]
    go[...] = nt(ga_ref[...], w_ref[...]).astype(BF16)
    ok = lax.broadcasted_iota(jnp.int32, (pad, pad), 0) < count
    lane = lax.broadcasted_iota(jnp.int32, (pad, 128), 1)

    def pair(p):
        at = pl.multiple_of(p * 128, 128)
        q = qkv_ref[0, :, pl.ds(at, 128)] * 0.125
        k = qkv_ref[0, :, pl.ds(width + at, 128)]
        v = qkv_ref[0, :, pl.ds(2 * width + at, 128)]
        g = go[:, pl.ds(at, 128)]
        gq = jnp.zeros((pad, 128), F32)
        gk = jnp.zeros((pad, 128), F32)
        gv = jnp.zeros((pad, 128), F32)
        for half in range(2):
            mine = (lane >= 64) if half else (lane < 64)
            qm = jnp.where(mine, q, 0)
            km = jnp.where(mine, k, 0) * 0.125
            gmine = jnp.where(mine, g, 0)
            scores = nt(k, qm)
            row = lse_ref[0, 2 * p + half:2 * p + half + 1, :]
            prob = jnp.where(ok, jnp.exp(scores - row), 0.0)
            dp = nt(v, gmine)
            inner = col_sum(prob * dp)
            ds = (prob * (dp - inner)).astype(BF16)
            gv = gv + nn(prob.astype(BF16), gmine)
            gk = gk + nn(ds, qm)
            gq = gq + tn(ds, km)
        g_ref[:, pl.ds(at, 128)] = gq.astype(BF16)
        g_ref[:, pl.ds(width + at, 128)] = gk.astype(BF16)
        g_ref[:, pl.ds(2 * width + at, 128)] = gv.astype(BF16)

    for p in range(width // 128):
        pair(p)


def back(counts, ga, w, qkv, lse):
    n, pad, width = ga.shape
    grid_spec = pltpu.PrefetchScalarGridSpec(
        num_scalar_prefetch=1,
        grid=(n,),
        in_specs=[by_image((pad, width)), whole(w.shape), by_image((pad, 3 * width)), by_image((16, pad))],
        out_specs=[by_image((pad, 3 * width))],
        scratch_shapes=[pltpu.VMEM((pad, width), BF16)],
    )
    return pl.pallas_call(
        functools.partial(back_kernel, pad),
        out_shape=[jax.ShapeDtypeStruct((n, pad, 3 * width), BF16)],
        grid_spec=grid_spec,
        compiler_params=params(60),
        cost_estimate=pl.CostEstimate(
            flops=2 * n * pad * width * (width + 10 * pad), bytes_accessed=16 * MIB,
            transcendentals=n * 12 * pad * pad),
        name="back",
    )(counts, ga, w, qkv, lse)[0]


def outgrad_kernel(o_ref, ga_ref, d_ref):
    d_ref[...] = tn(o_ref[...], ga_ref[...]).astype(BF16)


def outgrad(o, ga):
    rows, width = o.shape
    return pl.pallas_call(
        outgrad_kernel,
        out_shape=jax.ShapeDtypeStruct((width, width), BF16),
        grid=(2,),
        in_specs=[pl.BlockSpec((rows, width // 2), lambda j: (0, j)), whole(ga.shape)],
        out_specs=pl.BlockSpec((width // 2, width), lambda j: (j, 0)),
        compiler_params=params(60),
        cost_estimate=pl.CostEstimate(
            flops=2 * rows * width * width, bytes_accessed=6 * MIB, transcendentals=0),
        name="outgrad",
    )(o, ga)


def last_kernel(seq, pad, g_ref, a1_ref, w_ref, x_ref, gx_ref, vecs,
                d_ref, cols_ref, gi_ref, vec_ref, ga1, xs):
    c = pl.program_id(0)
    n = x_ref.shape[0]
    g = g_ref[...]
    d_ref[...] = tn(g, a1_ref[...]).astype(BF16)
    cols_ref[...] = col_sum(g.astype(F32))
    part = nn(g, w_ref[...])

    @pl.when(c == 0)
    def _():
        ga1[...] = part

    @pl.when(c > 0)
    def _():
        ga1[...] += part

    @pl.when(c == pl.num_programs(0) - 1)
    def _():
        width = x_ref.shape[-1]
        xs[pad - 8:pad, :] = jnp.zeros((8, width), F32)
        ggain = jnp.zeros((1, width), F32)
        gshift = jnp.zeros((1, width), F32)
        for i in range(n):
            xs[0:seq, :] = x_ref[i].astype(F32)
            normed, rstd = normalize(xs[...])
            grad = ga1[i * pad:(i + 1) * pad, :]
            ggain = ggain + col_sum(grad * normed)
            gshift = gshift + col_sum(grad)
            e = grad * vecs[0:1, :]
            gi = gx_ref[i] + rstd * (e - mean_row(e) - normed * mean_row(e * normed))
            gi_ref[i] = gi[0:seq]
        vec_ref[0:1, :] = ggain
        vec_ref[1:2, :] = gshift
        vec_ref[2:8, :] = jnp.zeros((6, width), F32)


def last(g, a1, w, images, gx, vec, pad, block=384):
    n, seq, width = images.shape
    rows, total = g.shape
    return pl.pallas_call(
        functools.partial(last_kernel, seq, pad),
        out_shape=[
            jax.ShapeDtypeStruct((total, width), BF16),
            jax.ShapeDtypeStruct((1, total), F32),
            jax.ShapeDtypeStruct((n, seq, width), F32),
            jax.ShapeDtypeStruct((8, width), F32),
        ],
        grid=(total // block,),
        in_specs=[
            pl.BlockSpec((rows, block), lambda c: (0, c)), whole(a1.shape),
            pl.BlockSpec((block, width), lambda c: (c, 0)), whole(images.shape), whole(gx.shape),
            whole(vec.shape),
        ],
        out_specs=[
            pl.BlockSpec((block, width), lambda c: (c, 0)), pl.BlockSpec((1, block), lambda c: (0, c)),
            whole((n, seq, width)), whole((8, width)),
        ],
        scratch_shapes=[pltpu.VMEM((rows, width), F32), pltpu.VMEM((pad, width), F32)],
        compiler_params=params(60),
        cost_estimate=pl.CostEstimate(
            flops=4 * rows * width * total, bytes_accessed=30 * MIB, transcendentals=0),
        name="last",
    )(g, a1, w, images, gx, vec)


def shards_any(
    images, grid_sizes, keep_flags, attn_gain, attn_shift, attend_weight, query_bias, value_bias,
    output_weight, output_bias, mlp_gain, mlp_shift, up_weight, up_bias, down_weight, down_bias,
    cotangent,
):
    n, seq, width = images.shape
    pad = -(-seq // 32) * 32
    counts = grid_sizes[:, 0] * grid_sizes[:, 1] + 2
    depth = keep_flags.astype(F32) / KEEP_PROB
    owners = width // attn_gain.shape[0]

    small = jnp.concatenate([
        attn_gain, attn_shift, query_bias, value_bias, output_bias, mlp_gain, mlp_shift, down_bias, up_bias])
    small = lax.all_gather(small.reshape(1, -1), "fsdp", axis=0, tiled=True).astype(F32)
    share = attn_gain.shape[0]
    vec = jnp.stack([small[:, k * share:(k + 1) * share].reshape(width) for k in range(8)])
    bu = small[:, 8 * share:].reshape(1, -1)

    attend = lax.all_gather(attend_weight.T, "fsdp", axis=0, tiled=True)
    out_w = lax.all_gather(output_weight, "fsdp", axis=0, tiled=True)
    up = lax.all_gather(up_weight.T, "fsdp", axis=0, tiled=True)
    down = lax.all_gather(down_weight, "fsdp", axis=0, tiled=True)

    a1, gm, qkv, o, lse = front(counts, depth, images, cotangent, attend, vec, pad)
    x1, a2, sums_two = middle(counts, depth, o, images, out_w, vec, pad)
    flat = lambda array: array.reshape(n * pad, array.shape[-1])
    block = up_weight.shape[1] if up_weight.shape[1] % 128 == 0 else 384
    dup, ddown, gbu, y, gx, ga, vec_feed = feed(
        counts, depth, flat(a2), flat(gm), up, down, bu, x1, cotangent, vec, seq, pad, block)
    dout = outgrad(flat(o), flat(ga))
    g = back(counts, ga, out_w, qkv, lse)
    dattend, cols, gi, vec_last = last(flat(g), flat(a1), attend, images, gx, vec, pad)

    sums = jnp.stack([jnp.sum(sums_two[:, 0]), jnp.sum(sums_two[:, 1]), jnp.sum(vec_feed[4]),
                      jnp.sum(counts).astype(F32)])

    def spread(array):
        return lax.psum(lax.psum_scatter(array, "fsdp", scatter_dimension=0, tiled=True), "dp")

    def columns(array):
        hidden = up.shape[0]
        array = jnp.swapaxes(array, 0, 1).reshape(width, owners, hidden // owners)
        return jnp.swapaxes(array, 0, 1)

    gup = spread(columns(dup))[0]
    gdown = spread(columns(ddown))[0].T
    gout = spread(dout)
    gattend = spread(dattend).T
    rows = jnp.concatenate([
        vec_last[0:2], cols[:, :width], cols[:, 2 * width:], vec_feed[3:4], vec_feed[0:3],
    ], 0)
    tiny = jnp.concatenate([
        jnp.swapaxes(rows.reshape(8, owners, share), 0, 1).reshape(owners, 8 * share),
        gbu.reshape(owners, -1)], 1)
    tiny = spread(tiny)[0]
    sums = lax.psum(sums, ("dp", "fsdp"))
    root_means = jnp.sqrt(sums[:3] / (sums[3] * width))
    tv = [tiny[k * share:(k + 1) * share] for k in range(8)]
    f = lambda array: array.astype(F32)
    return (y, gi, tv[0], tv[1], f(gattend), tv[2], tv[3], f(gout), tv[4], tv[5], tv[6],
            f(gup), tiny[8 * share:], f(gdown), tv[7], root_means)


def over_dp(array, m):
    return lax.ppermute(array, "dp", [(i, i ^ m) for i in range(4)])


def over_z(array, a):
    return lax.ppermute(array, "fsdp", [(i, i ^ (2 * a)) for i in range(8)])


def over_core(array):
    return lax.ppermute(array, "fsdp", [(i, i ^ 1) for i in range(8)])


def staged(kernel, ids, arrays, out_shape, name):
    size = sum(math.prod(s.shape) * s.dtype.itemsize for s in [*arrays, *out_shape])
    return pl.pallas_call(
        kernel,
        out_shape=out_shape,
        grid_spec=pltpu.PrefetchScalarGridSpec(
            num_scalar_prefetch=1, grid=(1,),
            in_specs=[whole(s.shape) for s in arrays],
            out_specs=[whole(s.shape) for s in out_shape]),
        compiler_params=params(60),
        cost_estimate=pl.CostEstimate(flops=0, bytes_accessed=size, transcendentals=0),
        name=name,
    )(ids, *arrays)


def simple(kernel, ids, arrays, out_shape, name, scratch=()):
    size = sum(math.prod(s.shape) * s.dtype.itemsize for s in [*arrays, *out_shape])
    inside = pl.BlockSpec(memory_space=pltpu.VMEM)
    return pl.pallas_call(
        kernel,
        out_shape=out_shape,
        in_specs=[SMEM] + [inside] * len(arrays),
        out_specs=[inside] * len(out_shape),
        scratch_shapes=list(scratch),
        compiler_params=pltpu.CompilerParams(vmem_limit_bytes=16 * MIB),
        cost_estimate=pl.CostEstimate(flops=0, bytes_accessed=size, transcendentals=0),
        name=name,
    )(ids, *arrays)


def pack_kernel(ids, at_ref, ow_ref, up_ref, down_ref, *refs):
    vectors, (own1, first1, own, first, rest) = refs[:9], refs[9:]
    q = ids[0]
    att = at_ref[...]
    up = jnp.transpose(up_ref[...])
    r = ow_ref.shape[0]
    for t in range(4):
        own1[t ^ q] = att[t * r:(t + 1) * r] if t < 3 else ow_ref[...]
        k = r // 3
        own[t ^ q, 0:k] = up[t * k:(t + 1) * k]
        own[t ^ q, k:2 * k] = down_ref[t * k:(t + 1) * k, :]
    k = 4 * (r // 3)
    rest[0] = up[k:]
    rest[1] = down_ref[k:, :]
    first1[0:r, :] = own1[0]
    pieces = [v[...].reshape(1, -1).astype(F32) for v in vectors]
    blank = jnp.zeros((1, first1.shape[1] - r), F32)
    rows = [jnp.concatenate([p, blank], 1) for p in pieces[:8]]
    rows += [jnp.concatenate([pieces[8][:, k * r:(k + 1) * r], blank], 1) for k in range(4)]
    rows.append(jnp.zeros((4, first1.shape[1]), F32))
    first1[r:r + 16, :] = jnp.concatenate(rows, 0).astype(BF16)
    first[...] = own[0]


def pack(ids, at, ow, up, down, vectors):
    r, width = ow.shape
    s = lambda *shape: jax.ShapeDtypeStruct(shape, BF16)
    return staged(pack_kernel, ids, [at, ow, up, down, *vectors],
                  [s(4, r, width), s(r + 16, width), s(4, 2 * r // 3, width), s(2 * r // 3, width), s(2, 8 * r // 3, width)],
                  "pack")


def after(value, *before):
    return lax.optimization_barrier((value, before))[0]


def line(ids, own, first, zr, xr):
    r, width = own.shape[1:]

    def kernel(ids, own, first, z1, z2, z3, x1, x2, x3, mine):
        zs, xs = (z1, z2, z3), (x1, x2, x3)
        for m in range(4):
            mine[m * r:(m + 1) * r] = own[m]
        mine[16 * r:16 * r + 16] = first[r:r + 16]
        for a in range(1, 4):
            at = 4 * a * r
            mine[at:at + r] = zs[a - 1][0:r]
            mine[16 * r + 16 * a:16 * r + 16 * a + 16] = zs[a - 1][r:r + 16]
            for m in range(1, 4):
                mine[at + m * r:at + (m + 1) * r] = xs[m - 1][a - 1]

    return simple(kernel, ids, [own, first, *zr, *xr], [jax.ShapeDtypeStruct((16 * r + 64, width), BF16)], "line")[0]


def stack_rows(ids, arrays, spans):
    width = arrays[0].shape[1]

    def kernel(ids, *refs):
        for out, (low, high) in zip(refs[3:], spans):
            for a in range(3):
                out[a] = refs[a][low:high]

    return simple(kernel, ids, arrays,
                  [jax.ShapeDtypeStruct((3, high - low, width), BF16) for low, high in spans], "stack")


def early_kernel(seq, pad, counts, depth, x_ref, cot_ref, norm_ref, gm_ref, xs):
    i = pl.program_id(0)
    width = x_ref.shape[-1]
    ok = lax.broadcasted_iota(jnp.int32, (pad, 1), 0) < counts[i]
    xs[pad - 8:pad, :] = jnp.zeros((8, width), F32)
    xs[0:seq, :] = cot_ref[0].astype(F32)
    gm_ref[0] = jnp.where(ok, xs[...] * depth[i, 1], 0.0).astype(BF16)
    xs[0:seq, :] = x_ref[0].astype(F32)
    norm_ref[0], _ = normalize(xs[...])


def early(counts, depth, images, cot, pad):
    n, seq, width = images.shape
    sd = jax.ShapeDtypeStruct
    return pl.pallas_call(
        functools.partial(early_kernel, seq, pad),
        out_shape=[sd((n, pad, width), F32), sd((n, pad, width), BF16)],
        grid_spec=pltpu.PrefetchScalarGridSpec(
            num_scalar_prefetch=2, grid=(n,),
            in_specs=[by_image((seq, width)), by_image((seq, width))],
            out_specs=[by_image((pad, width)), by_image((pad, width))],
            scratch_shapes=[pltpu.VMEM((pad, width), F32)]),
        compiler_params=params(16),
        cost_estimate=pl.CostEstimate(flops=10 ** 7, bytes_accessed=9 * MIB, transcendentals=0),
        name="early",
    )(counts, depth, images, cot)


def head_kernel(pad, ids, counts, mine, sib, norm_ref, at_out, ow_out, vec_ref, b2_ref, b3_ref,
                a1_ref, qkv_ref, o_ref, lse_ref, at_s, ow_s, lse_s, sems):
    q, z, c = ids[0], ids[1], ids[2]
    copies = [pltpu.make_async_copy(at_s, at_out, sems.at[0]), pltpu.make_async_copy(ow_s, ow_out, sems.at[1])]
    step = pl.program_id(0)

    @pl.when(step == 0)
    def _():
        r = ow_s.shape[0] // 8
        cut = b2_ref.shape[2]
        for j in range(8):
            a = (j >> 1) ^ z
            own = ((j & 1) ^ c) == 0

            def place(ref_in):
                small = ref_in[pl.ds(pl.multiple_of(16 * r + 16 * a, 16), 16), 0:r].astype(F32)
                vec_ref[0:8, j * r:(j + 1) * r] = small[0:8]
                for k in range(4):
                    row = small[8 + k:9 + k]
                    at, to = k * r, (k + 1) * r
                    if at < cut:
                        b2_ref[j, :, at:min(to, cut)] = row[:, 0:min(to, cut) - at]
                    if to > cut:
                        b3_ref[j, :, max(at, cut) - cut:to - cut] = row[:, max(at, cut) - at:]
                for t in range(4):
                    ref, at = (ow_s, j * r) if t == 3 else (at_s, (3 * j + t) * r)
                    ref[at:at + r, :] = ref_in[pl.ds(pl.multiple_of((4 * a + (t ^ q)) * r, r), r), :]

            @pl.when(own)
            def _():
                place(mine)

            @pl.when(jnp.logical_not(own))
            def _():
                place(sib)

        for copy in copies:
            copy.start()

    attend_image(pad, counts[step], norm_ref[0], at_s, vec_ref, a1_ref, qkv_ref, o_ref, lse_ref, lse_s)

    @pl.when(step == pl.num_programs(0) - 1)
    def _():
        for copy in copies:
            copy.wait()


def head(ids, counts, mine, sib, norm):
    n, pad, width = norm.shape
    r = width // 8
    cut = 4 * r // 3
    sd = jax.ShapeDtypeStruct
    far = pl.BlockSpec(memory_space=pl.ANY)
    return pl.pallas_call(
        functools.partial(head_kernel, pad),
        out_shape=[
            sd((24 * r, width), BF16), sd((8 * r, width), BF16), sd((8, width), F32), sd((8, 1, cut), F32),
            sd((8, 1, 4 * r - cut), F32),
            sd((n, pad, width), BF16), sd((n, pad, 3 * width), BF16),
            sd((n, pad, width), BF16), sd((n, 16, pad), F32),
        ],
        grid_spec=pltpu.PrefetchScalarGridSpec(
            num_scalar_prefetch=2, grid=(n,),
            in_specs=[whole(mine.shape), whole(sib.shape), by_image((pad, width))],
            out_specs=[
                far, far, whole((8, width)), whole((8, 1, cut)), whole((8, 1, 4 * r - cut)),
                by_image((pad, width)), by_image((pad, 3 * width)),
                by_image((pad, width)), by_image((16, pad)),
            ],
            scratch_shapes=[
                pltpu.VMEM((24 * r, width), BF16), pltpu.VMEM((8 * r, width), BF16),
                pltpu.VMEM((pad, 128), F32), pltpu.SemaphoreType.DMA((2,))]),
        compiler_params=params(60),
        cost_estimate=pl.CostEstimate(
            flops=2 * n * pad * width * (3 * width + 4 * pad), bytes_accessed=20 * MIB,
            transcendentals=n * 12 * pad * pad),
        name="head",
    )(ids, counts, mine, sib, norm)


def part_kernel(seq, pad, second, group, ids, counts, depth, a2_ref, gm_ref, *rest):
    if second:
        weights, bu_ref, *rest = rest
    else:
        sides, bu_ref, rest = (rest[0:5], rest[5:10]), rest[10], rest[11:]
    if second:
        (mlp_in, ga2_in, a2t_in, gmt_in, x1_in, cot_ref, vecs,
         both, gbu_ref, y_ref, vec_ref, gx_out, ga_out,
         a2t, gmt, mlp, ga2, hs, gus, mlp_s, ga2_s, x1_s, ga_s, cs, sems, out_sems) = rest
        loads = [pltpu.make_async_copy(a, b, sems.at[k]) for k, (a, b) in enumerate(
            ((a2t_in, a2t), (gmt_in, gmt), (mlp_in, mlp_s), (ga2_in, ga2_s), (x1_in, x1_s)))]
    else:
        both, gbu_ref, mlp_out, ga2_out, a2t_out, gmt_out, a2t, gmt, mlp, ga2, hs, gus, sems = rest
        stores = [pltpu.make_async_copy(a, b, sems.at[k]) for k, (a, b) in enumerate(
            ((a2t, a2t_out), (gmt, gmt_out), (mlp, mlp_out), (ga2, ga2_out)))]
    step = pl.program_id(0)
    end = pl.num_programs(0) - 1
    q, z, c = ids[0], ids[1], ids[2]
    rows, width = a2_ref.shape
    n = rows // pad
    block = bu_ref.shape[-1]

    @pl.when(step == 0)
    def _():
        if second:
            for copy in loads:
                copy.start()
        else:
            a2t[...] = jnp.transpose(a2_ref[...])
            gmt[...] = jnp.transpose(gm_ref[...])
            stores[0].start()
            stores[1].start()
        mlp[...] = jnp.zeros_like(mlp)
        ga2[...] = jnp.zeros_like(ga2)

    pairs = [(k, side) for k in range(group) for side in range(2)]
    owners = [(((step * group + k) ^ z) << 1) | (c ^ side) for k, side in pairs]
    def piece(k, side, t, low):
        own, message, *crossed = sides[side]
        slot, m = step * group + k, t ^ q
        at = slice(low, low + r)
        index = jnp.maximum(slot - 1, 0) if group > 1 else 0
        value = message[index, at]
        for x, ref in enumerate(crossed):
            value = jnp.where(m == x + 1, ref[index, at], value)
        return jnp.where(slot == 0, own[m, at], value)

    if second:
        up, down = (jnp.concatenate([weights[c, kind], weights[c ^ 1, kind]], 0) for kind in range(2))
    else:
        r = sides[0][0].shape[1] // 2
        up = jnp.concatenate([piece(k, side, t, 0) for k, side in pairs for t in range(4)], 0)
        down = jnp.concatenate([piece(k, side, t, r) for k, side in pairs for t in range(4)], 0)
    bu = jnp.concatenate([bu_ref[owner] for owner in owners], 1)
    gbu = jnp.zeros(bu.shape, F32)
    ready = None
    for i in range(n + 1):
        if i < n:
            at = slice(i * pad, (i + 1) * pad)
            fresh = nt(a2_ref[at, :], up) + bu, nt(gm_ref[at, :], down)
        if ready is not None:
            at = slice((i - 1) * pad, i * pad)
            u, t = ready
            act, slope = gelu_pair(u)
            h = act.astype(BF16)
            gu = (t * slope).astype(BF16)
            hs[at, :] = h
            gus[at, :] = gu
            gbu = gbu + col_sum(gu.astype(F32))
            mlp[at, :] += nn(h, down)
            ga2[at, :] += nn(gu, up)
        ready = fresh
    for p, owner in enumerate(owners):
        gbu_ref[owner] = gbu[:, p * block:(p + 1) * block]

    if second:
        @pl.when(step == 0)
        def _():
            loads[0].wait()
            loads[1].wait()
    else:
        @pl.when(step == end)
        def _():
            stores[2].start()
            stores[3].start()

    part = width // 4
    span = 2 * group
    for t in range(4):
        at = slice(t * part, (t + 1) * part)
        for kind, (left, right) in enumerate(((a2t, gus), (gmt, hs))):
            d = nn(left[at, :], right[...]).astype(BF16)
            for p, owner in enumerate(owners):
                both[owner % span, t, kind] = d[:, p * block:(p + 1) * block]

    if not second:
        @pl.when(step == end)
        def _():
            for copy in stores:
                copy.wait()
        return

    @pl.when(step == end)
    def _():
        for copy in loads[2:]:
            copy.wait()
        mask_rows = lax.broadcasted_iota(jnp.int32, (pad, 1), 0)
        cs[pad - 8:pad, :] = jnp.zeros((8, width), F32)
        sums = [jnp.zeros((1, width), F32)] * 5
        outs = []
        for i in range(n):
            at = slice(i * pad, (i + 1) * pad)
            ok = mask_rows < counts[i]
            x1 = x1_s[i]
            out = mlp[at, :] + mlp_s[at, :] + vecs[7:8, :]
            y_ref[i] = jnp.where(ok, x1 + depth[i, 1] * out, 0.0).astype(BF16)[0:seq]
            cs[0:seq, :] = cot_ref[i].astype(F32)
            g = jnp.where(ok, cs[...], 0.0)
            back = ga2[at, :] + ga2_s[at, :]
            normed, rstd = normalize(x1)
            e = back * vecs[5:6, :]
            gx = g + rstd * (e - mean_row(e) - normed * mean_row(e * normed))
            ga = (depth[i, 0] * gx).astype(BF16)
            x1_s[i] = gx
            ga_s[i] = ga
            for k, (ref, to) in enumerate(((x1_s, gx_out), (ga_s, ga_out))):
                copy = pltpu.make_async_copy(ref.at[i], to.at[i], out_sems.at[i, k])
                copy.start()
                outs.append(copy)
            terms = (back * normed, back, gm_ref[at, :].astype(F32), ga.astype(F32), jnp.where(ok, out * out, 0.0))
            sums = [total + col_sum(term) for total, term in zip(sums, terms)]
        for k, total in enumerate(sums):
            vec_ref[k:k + 1, :] = total
        vec_ref[5:8, :] = jnp.zeros((3, width), F32)
        for copy in outs:
            copy.wait()


def part(ids, counts, depth, a2, gm, weights, bu, pad, group, carry=(), x1=None, cot=None, vec=None):
    rows, width = a2.shape
    n = rows // pad
    block = bu.shape[-1]
    second = len(carry) > 0
    sd = jax.ShapeDtypeStruct
    if second:
        w_specs = [pl.BlockSpec((2, 2, block, width), lambda s, ids, *_: (s ^ ids[1], 0, 0, 0))]
    else:
        w_specs = [whole(w.shape) for w in weights]
    far = pl.BlockSpec(memory_space=pl.ANY)
    acc = sd((rows, width), F32)
    tr = sd((width, rows), BF16)
    in_specs = [whole(a2.shape), whole(gm.shape)] + w_specs + [whole(bu.shape)]
    args = [a2, gm, *weights, bu]
    outs = [sd((8, 4, 2, width // 4, block), BF16), sd((8, 1, block), F32)]
    out_specs = [
        pl.BlockSpec((2 * group, 4, 2, width // 4, block), lambda s, ids, *_: (s ^ (ids[1] // group), 0, 0, 0, 0)),
        whole((8, 1, block))]
    scratch = [pltpu.VMEM(tr.shape, BF16), pltpu.VMEM(tr.shape, BF16), pltpu.VMEM(acc.shape, F32),
               pltpu.VMEM(acc.shape, F32), pltpu.VMEM((rows, 2 * group * block), BF16),
               pltpu.VMEM((rows, 2 * group * block), BF16)]
    if second:
        seq = cot.shape[1]
        args += [*carry, x1, cot, vec]
        in_specs += [far] * 5 + [whole(cot.shape), whole(vec.shape)]
        outs += [sd((n, seq, width), BF16), sd((8, width), F32), sd((n, pad, width), F32), sd((n, pad, width), BF16)]
        out_specs += [whole((n, seq, width)), whole((8, width)), far, far]
        scratch += [pltpu.VMEM(acc.shape, F32), pltpu.VMEM(acc.shape, F32), pltpu.VMEM((n, pad, width), F32),
                    pltpu.VMEM((n, pad, width), BF16), pltpu.VMEM((pad, width), F32), pltpu.SemaphoreType.DMA((5,)),
                    pltpu.SemaphoreType.DMA((n, 2))]
    else:
        seq = 0
        outs += [acc, acc, tr, tr]
        out_specs += [far] * 4
        scratch += [pltpu.SemaphoreType.DMA((4,))]
    return pl.pallas_call(
        functools.partial(part_kernel, seq, pad, second, group),
        out_shape=outs,
        grid_spec=pltpu.PrefetchScalarGridSpec(
            num_scalar_prefetch=3, grid=(4 // group,), in_specs=in_specs, out_specs=out_specs,
            scratch_shapes=scratch),
        compiler_params=params(60),
        cost_estimate=pl.CostEstimate(
            flops=12 * rows * width * 8 * block, bytes_accessed=30 * MIB, transcendentals=0),
        name="feed_b" if second else "feed_a",
    )(ids, counts, depth, *args)


def back_first_kernel(pad, ids, counts, ga_ref, w_ref, qkv_ref, lse_ref, o_in, a1_in, g_out, near_p, far_p, near_q, far_q,
                      go, g_s, o_s, a1_s, sems, out_sems):
    i = pl.program_id(0)
    n, _, width = ga_ref.shape
    loads = [pltpu.make_async_copy(o_in, o_s, sems.at[0]), pltpu.make_async_copy(a1_in, a1_s, sems.at[1])]

    @pl.when(i == 0)
    def _():
        for copy in loads:
            copy.start()

    back_image(pad, counts[i], ga_ref.at[i], w_ref, qkv_ref, lse_ref, g_s.at[i], go)
    pltpu.make_async_copy(g_s.at[i], g_out.at[i], out_sems.at[i]).start()

    @pl.when(i == n - 1)
    def _():
        for copy in loads:
            copy.wait()
        q, z, c = ids[0], ids[1], ids[2]
        r = near_p.shape[2]

        def put(value, group, j, t):
            a, m = ((j >> 1) ^ z) & 1, t ^ q
            own = ((j & 1) ^ c) == 0

            @pl.when(own)
            def _():
                group[0][m, a] = value

            @pl.when(jnp.logical_not(own))
            def _():
                group[1][m, a] = value

        for group, side in (((near_p, far_p), 1 - (z >> 1)), ((near_q, far_q), z >> 1)):
            for s in range(4):
                if s < 3:
                    cols = pl.ds(pl.multiple_of(side * (12 * r) + s * (4 * r), 128), 4 * r)
                    left = g_s[:, :, cols].reshape(n * pad, 4 * r)
                    d = tn(left, a1_s[...].reshape(n * pad, width)).astype(BF16)
                else:
                    cols = pl.ds(pl.multiple_of(side * (4 * r), 128), 4 * r)
                    left = o_s[:, :, cols].reshape(n * pad, 4 * r)
                    d = tn(left, ga_ref[...].reshape(n * pad, width)).astype(BF16)
                for k in range(4):
                    chunk = 4 * s + k
                    value = d[k * r:(k + 1) * r]
                    if s < 3:
                        put(value, group, 4 * side + chunk // 3, chunk % 3)
                    else:
                        put(value, group, 4 * side + k, 3)
        for k in range(n):
            pltpu.make_async_copy(g_s.at[k], g_out.at[k], out_sems.at[k]).wait()


def back_first(ids, counts, ga, w, qkv, lse, o, a1):
    n, pad, width = ga.shape
    r = width // 8
    sd = jax.ShapeDtypeStruct
    far = pl.BlockSpec(memory_space=pl.ANY)
    group = sd((4, 2, r, width), BF16)
    return pl.pallas_call(
        functools.partial(back_first_kernel, pad),
        out_shape=[sd((n, pad, 3 * width), BF16)] + [group] * 4,
        grid_spec=pltpu.PrefetchScalarGridSpec(
            num_scalar_prefetch=2, grid=(n,),
            in_specs=[whole(ga.shape), whole(w.shape), by_image((pad, 3 * width)), by_image((16, pad)), far, far],
            out_specs=[far] + [whole(group.shape)] * 4,
            scratch_shapes=[
                pltpu.VMEM((pad, width), BF16), pltpu.VMEM((n, pad, 3 * width), BF16), pltpu.VMEM((n, pad, width), BF16),
                pltpu.VMEM((n, pad, width), BF16), pltpu.SemaphoreType.DMA((2,)), pltpu.SemaphoreType.DMA((n,))]),
        compiler_params=params(60),
        cost_estimate=pl.CostEstimate(
            flops=2 * n * pad * width * (3 * width + 10 * pad), bytes_accessed=16 * MIB,
            transcendentals=n * 12 * pad * pad),
        name="back",
    )(ids, counts, ga, w, qkv, lse, o, a1)


def final_kernel(seq, pad, g_ref, w_ref, x_ref, gx_ref, y_ref, vecs, gi_ref, y_out, vec_ref, cols_ref, xs):
    i = pl.program_id(0)
    width = x_ref.shape[-1]
    grad = nn(g_ref[0], w_ref[...])
    xs[pad - 8:pad, :] = jnp.zeros((8, width), F32)
    xs[0:seq, :] = x_ref[0].astype(F32)
    normed, rstd = normalize(xs[...])

    @pl.when(i == 0)
    def _():
        vec_ref[...] = jnp.zeros_like(vec_ref)
        cols_ref[...] = jnp.zeros_like(cols_ref)

    vec_ref[0:1, :] += col_sum(grad * normed)
    vec_ref[1:2, :] += col_sum(grad)
    cols_ref[...] += col_sum(g_ref[0].astype(F32))
    e = grad * vecs[0:1, :]
    gi = gx_ref[0] + rstd * (e - mean_row(e) - normed * mean_row(e * normed))
    for k in range(gi_ref.shape[1]):
        @pl.when(i == k)
        def _():
            gi_ref[:, k, :] = gi[0:seq]
            y_out[:, k, :] = y_ref[0]


def final(g, w, images, gx, y, vec, pad):
    n, seq, width = images.shape
    sd = jax.ShapeDtypeStruct
    return pl.pallas_call(
        functools.partial(final_kernel, seq, pad),
        out_shape=[sd((seq, n, width), F32), sd((seq, n, width), BF16), sd((8, width), F32), sd((1, 3 * width), F32)],
        grid=(n,),
        in_specs=[by_image((pad, 3 * width)), whole(w.shape), by_image((seq, width)), by_image((pad, width)),
                  by_image((seq, width)), whole(vec.shape)],
        out_specs=[whole((seq, n, width)), whole((seq, n, width)), whole((8, width)), whole((1, 3 * width))],
        scratch_shapes=[pltpu.VMEM((pad, width), F32)],
        compiler_params=params(60),
        cost_estimate=pl.CostEstimate(
            flops=6 * n * pad * width * width, bytes_accessed=18 * MIB, transcendentals=0),
        name="final",
    )(g, w, images, gx, y, vec)


def add_pair(ids, near, got):
    slots, parts = near.shape[:2]
    shape = near.shape[1:]
    block = pl.BlockSpec((slots, 1) + shape[1:], lambda a, *_: (0, a) + (0,) * (len(shape) - 1))

    def kernel(a_ref, b_ref, *outs):
        for m in range(4):
            outs[m][...] = (a_ref[m].astype(F32) + b_ref[m].astype(F32)).astype(BF16)

    return pl.pallas_call(
        kernel,
        out_shape=[jax.ShapeDtypeStruct(shape, BF16)] * slots,
        grid=(parts,),
        in_specs=[block, block],
        out_specs=[pl.BlockSpec((1,) + shape[1:], lambda a: (a,) + (0,) * (len(shape) - 1))] * slots,
        compiler_params=params(60),
        cost_estimate=pl.CostEstimate(flops=0, bytes_accessed=6 * near.size, transcendentals=0),
        name="add_pair",
    )(near, got)


def add_four(ids, parts, split):
    shape = parts[0].shape

    def kernel(ids, a, b, c, d, *outs):
        if split:
            for k in range(shape[0]):
                outs[k][...] = ((a[k].astype(F32) + b[k].astype(F32)) + (c[k].astype(F32) + d[k].astype(F32))).astype(BF16)
        else:
            outs[0][...] = ((a[...].astype(F32) + b[...].astype(F32)) + (c[...].astype(F32) + d[...].astype(F32))).astype(BF16)

    count = shape[0] if split else 1
    out = jax.ShapeDtypeStruct(shape[1:] if split else shape, BF16)
    return simple(kernel, ids, parts, [out] * count, "add_four")


def merge(ids, s2, s3):
    _, _, rows, k2 = s2.shape
    k3 = s3.shape[3]

    def kernel(ids, a, b, out):
        for ref, at, to in ((a, 0, k2), (b, k2, k2 + k3)):
            out[:, :, at:to] = ((ref[0].astype(F32) + ref[1].astype(F32)) + (ref[2].astype(F32) + ref[3].astype(F32))).astype(BF16)

    return simple(kernel, ids, [s2, s3], [jax.ShapeDtypeStruct((2, rows, k2 + k3), BF16)], "merge")[0]


def place_feed_kernel(ids, p0, p1, p2, p3, up_ref, down_ref, cs):
    q = ids[0]
    rows = p0.shape[1]
    for m, p in enumerate((p0, p1, p2, p3)):
        to = pl.ds(pl.multiple_of((q ^ m) * rows, rows), rows)
        up_ref[to, :] = p[0].astype(F32)
        cs[to, :] = p[1].astype(F32)
    down_ref[...] = jnp.transpose(cs[...])


def place_feed(ids, parts):
    _, rows, block = parts[0].shape
    sd = jax.ShapeDtypeStruct
    return simple(place_feed_kernel, ids, parts, [sd((4 * rows, block), F32), sd((block, 4 * rows), F32)],
                  "place_feed", scratch=[pltpu.VMEM((4 * rows, block), F32)])


def place_attend_kernel(ids, p0, p1, p2, p3, at_ref, ow_ref, cs):
    q = ids[0]
    r = p0.shape[0]
    for m, p in enumerate((p0, p1, p2, p3)):
        cs[pl.ds(pl.multiple_of((q ^ m) * r, r), r), :] = p[...].astype(F32)
    at_ref[...] = cs[0:3 * r, :]
    ow_ref[...] = cs[3 * r:4 * r, :]


def place_attend(ids, parts):
    r, width = parts[0].shape
    sd = jax.ShapeDtypeStruct
    return simple(place_attend_kernel, ids, parts, [sd((3 * r, width), F32), sd((r, width), F32)],
                  "place_attend", scratch=[pltpu.VMEM((4 * r, width), F32)])


def cut_vectors(ids, rows, share):
    width = rows.shape[1]
    parts = width // share

    def kernel(ids, rows_ref, *outs):
        owner = 2 * ids[1] + ids[2]
        vectors, bias = outs[:8], outs[8]
        for j in range(parts):
            @pl.when(owner == j)
            def _():
                for k in range(8):
                    vectors[k][...] = rows_ref[k:k + 1, j * share:(j + 1) * share].reshape(share)
                at = j * 4 * share
                bias[...] = rows_ref[8 + at // width:9 + at // width, at % width:at % width + 4 * share].reshape(4 * share)

    sd = jax.ShapeDtypeStruct
    return simple(kernel, ids, [rows], [sd((share,), F32)] * 8 + [sd((4 * share,), F32)], "cut_vectors")


def shards_grid(
    images, grid_sizes, keep_flags, attn_gain, attn_shift, attend_weight, query_bias, value_bias,
    output_weight, output_bias, mlp_gain, mlp_shift, up_weight, up_bias, down_weight, down_bias,
    cotangent,
):
    n, seq, width = images.shape
    pad = -(-seq // 32) * 32
    counts = grid_sizes[:, 0] * grid_sizes[:, 1] + 2
    depth = keep_flags.astype(F32) / KEEP_PROB
    owners = 8
    share = attn_gain.shape[0]
    f = lax.axis_index("fsdp")
    ids = jnp.stack([lax.axis_index("dp"), f >> 1, f & 1]).astype(jnp.int32)

    z_all = lambda array: [over_z(array, a) for a in (1, 2, 3)]
    dp_all = lambda array: [over_dp(array, m) for m in (1, 2, 3)]
    dp_out = lambda s: [s[0]] + [over_dp(s[m], m) for m in (1, 2, 3)]
    z_out = lambda s: [s[0]] + [over_z(s[a], a) for a in (1, 2, 3)]
    tied = lax.optimization_barrier
    flat = lambda array: array.reshape(n * pad, array.shape[-1])

    own1, first1, own, first, rest = pack(
        ids, attend_weight.T, output_weight, up_weight, down_weight,
        [attn_gain, attn_shift, query_bias, value_bias, output_bias, mlp_gain, mlp_shift, down_bias, up_bias])
    zr1 = z_all(first1)
    own_other = over_core(own)
    first, rest, zr1, own_other = tied((first, rest, zr1, own_other))
    message1, = stack_rows(ids, zr1, [(0, share)])
    xr1 = dp_all(message1)
    zr = z_all(first)
    weights_b = lax.all_gather(rest[None], "fsdp", axis=0, tiled=True)
    norm, gm = early(counts, depth, images, cotangent, pad)
    xr1, zr, norm, gm = tied((xr1, zr, norm, gm))
    mine1 = line(ids, own1, first1, zr1, xr1)
    sib1 = over_core(mine1)
    message, = stack_rows(ids, zr, [(0, first.shape[0])])
    message_other = over_core(message)
    xr = dp_all(message)
    sib1, message_other = tied((sib1, message_other))
    attend, out_w, vec, bu2, bu3, a1, qkv, o, lse = head(ids, counts, mine1, sib1, norm)
    o, xr = tied((o, xr))
    sib = [own_other, message_other, *(over_core(x) for x in xr)]
    x1, a2, sums_two = middle(counts, depth, o, images, out_w, vec, pad)
    x1, a2, sib = tied((x1, a2, sib))
    a2, gm = flat(a2), flat(gm)
    both2, gbu2, mlp, ga2, a2t, gmt = part(
        ids, counts, depth, a2, gm, [own, message, *xr, *sib], bu2, pad, 2)
    mlp, weights_b = tied((mlp, weights_b))

    own_sum = lambda both: lax.psum_scatter(
        both.reshape(-1, both.shape[-1]), "fsdp", scatter_dimension=0, tiled=True).reshape(both.shape[1:])
    quarter = lambda shard: lax.all_to_all(shard, "dp", 0, 0, tiled=True)
    shard2 = own_sum(both2)
    both3, gbu3, y, vec_feed, gx, ga = part(
        ids, counts, depth, a2, gm, [weights_b], bu3, pad, 1, (mlp, ga2, a2t, gmt), x1, cotangent, vec)
    shard3 = own_sum(both3)
    quarter2 = quarter(after(shard2, ga))
    g, near_p, far_p, near_q, far_q = back_first(ids, counts, ga, out_w, qkv, lse, o, a1)
    g, near_p, far_p, near_q, far_q, quarter2 = tied((g, near_p, far_p, near_q, far_q, quarter2))
    got_p = over_core(far_p)
    got_q = over_core(far_q)
    s_p = add_pair(ids, near_p, got_p)
    dr_p = dp_out(s_p)
    gi, y, vec_last, cols = final(after(g, s_p), attend, images, gx, y, vec, pad)
    y, gi = y.swapaxes(0, 1), gi.swapaxes(0, 1)
    rows = jnp.concatenate([
        vec_last[0:2], cols[:, :width], cols[:, 2 * width:], vec_feed[3:4], vec_feed[0:3],
        jnp.concatenate([gbu2[:, 0], gbu3[:, 0]], 1).reshape(4, width), sums_two[:, 0:2].sum(0), vec_feed[4:5],
        jnp.full((1, width), jnp.sum(counts).astype(F32)),
    ], 0)
    rows = rows + over_core(rows)
    rows, got_q, dr_p = tied((rows, got_q, dr_p))
    s_q = add_pair(ids, near_q, got_q)
    rows = rows + over_dp(rows, 1)
    s_q, rows = tied((s_q, rows))
    dr_q = dp_out(s_q)
    quarter3 = quarter(after(shard3, s_q))
    e_p = add_four(ids, after(dr_p, s_q), True)
    er_p = [over_z(x, a) for a, x in zip((2, 3), e_p)]
    er_p, dr_q, rows, quarter3 = tied((er_p, dr_q, rows, quarter3))
    e_q = add_four(ids, dr_q, True)
    er_q = over_z(e_q[1], 1)
    rows = after(rows, e_q)
    rows = rows + over_dp(rows, 2)
    f3 = merge(ids, quarter2, after(quarter3, e_q))
    fr3 = [f3] + dp_all(f3)
    er_q, fr3[1], fr3[2] = tied((er_q, fr3[1], fr3[2]))
    f1 = add_four(ids, [e_q[0], er_q, *er_p], False)[0]
    fr1 = [f1] + dp_all(f1)
    got = z_all(after(rows, f1))
    rows = (rows + got[0]) + (got[1] + got[2])
    root_means = jnp.sqrt(jnp.sum(rows[12:15], 1) / (rows[15, 0] * width))
    *tv, gub = cut_vectors(ids, rows, share)
    gup, gdown = place_feed(ids, fr3)
    gattend, gout = place_attend(ids, fr1)
    gattend = gattend.T
    return (y, gi, tv[0], tv[1], gattend, tv[2], tv[3], gout, tv[4], tv[5], tv[6],
            gup, gub, gdown, tv[7], root_means)


def shards(on_grid, *args):
    images, attn_gain, up_weight = args[0], args[3], args[12]
    share = attn_gain.shape[0]
    fits = on_grid and share % 48 == 0 and up_weight.shape[1] == 4 * share and images.shape[2] == 8 * share
    return (shards_grid if fits else shards_any)(*args)


def solution(mesh):
    images = P(("dp", "fsdp"), None, None)
    flags = P(("dp", "fsdp"), None)
    vec, rows, cols = P("fsdp"), P("fsdp", None), P(None, "fsdp")
    return jax.shard_map(
        functools.partial(shards, dict(mesh.shape) == {"dp": 4, "fsdp": 8}),
        mesh=mesh,
        in_specs=(images, flags, flags, vec, vec, cols, vec, vec, rows, vec, vec, vec, cols, vec, rows,
                  vec, images),
        out_specs=(images, images, vec, vec, cols, vec, vec, rows, vec, vec, vec, cols, vec, rows, vec,
                   P()),
        check_vma=False,
    )
```

```python
import functools
import math

import jax
import jax.numpy as jnp
from jax import lax
from jax.experimental import pallas as pl
from jax.experimental.pallas import tpu as pltpu
from jax.sharding import PartitionSpec as P

HEAD_DIM = 64
EPS = 1e-06
KEEP_PROB = 0.9
MASKED = -1e30
INV_ROOT_TWO = 0.7071067811865476
INV_ROOT_TWO_PI = 0.3989422804014327
F32 = jnp.float32
BF16 = jnp.bfloat16
MIB = 1024 * 1024


def nn(left, right):
    return lax.dot_general(left, right, (((1,), (0,)), ((), ())), preferred_element_type=F32)


def nt(left, right):
    return lax.dot_general(left, right, (((1,), (1,)), ((), ())), preferred_element_type=F32)


def tn(left, right):
    return lax.dot_general(left, right, (((0,), (0,)), ((), ())), preferred_element_type=F32)


def mean_row(values):
    return jnp.sum(values, -1, keepdims=True) * (1.0 / values.shape[-1])


def normalize(values):
    center = values - mean_row(values)
    rstd = lax.rsqrt(mean_row(center * center) + EPS)
    return center * rstd, rstd


def col_sum(values):
    return jnp.sum(values, 0, keepdims=True)


def params(limit, steps=1):
    return pltpu.CompilerParams(
        dimension_semantics=("arbitrary",) * steps, vmem_limit_bytes=limit * MIB
    )


def whole(shape, buffers=1):
    zeros = (0,) * len(shape)
    return pl.BlockSpec(shape, lambda *_: zeros, pipeline_mode=pl.Buffered(buffers))


def by_image(shape):
    rest = (0,) * len(shape)
    return pl.BlockSpec((1,) + shape, lambda i, *_: (i,) + rest)


SMEM = pl.BlockSpec(memory_space=pltpu.SMEM)


def front_kernel(seq, pad, counts, depth, x_ref, cot_ref, w_ref, vec_ref,
                 a1_ref, gm_ref, qkv_ref, o_ref, lse_ref, xs, lse_s):
    i = pl.program_id(0)
    width = x_ref.shape[-1]
    count = counts[i]
    rows = lax.broadcasted_iota(jnp.int32, (pad, 1), 0)
    xs[pad - 8:pad, :] = jnp.zeros((8, width), F32)
    xs[0:seq, :] = cot_ref[0].astype(F32)
    gm_ref[0] = jnp.where(rows < count, xs[...] * depth[i, 1], 0.0).astype(BF16)
    xs[0:seq, :] = x_ref[0].astype(F32)
    normed, _ = normalize(xs[...])
    attend_image(pad, count, normed, w_ref, vec_ref, a1_ref, qkv_ref, o_ref, lse_ref, lse_s)


def attend_image(pad, count, normed, w_ref, vec_ref, a1_ref, qkv_ref, o_ref, lse_ref, lse_s):
    width = normed.shape[-1]
    pairs = width // 128
    a1 = (normed * vec_ref[0:1, :] + vec_ref[1:2, :]).astype(BF16)
    a1_ref[0] = a1
    for c in range(0, 3 * width, 768):
        part = nt(a1, w_ref[c:c + 768, :])
        if c < width:
            part = part + vec_ref[2:3, c:c + 768]
        elif c >= 2 * width:
            part = part + vec_ref[3:4, c - 2 * width:c - 2 * width + 768]
        qkv_ref[0, :, c:c + 768] = part.astype(BF16)
    ok = lax.broadcasted_iota(jnp.int32, (pad, pad), 1) < count
    lane = lax.broadcasted_iota(jnp.int32, (pad, 128), 1)
    lse_s[...] = jnp.zeros((pad, 128), F32)

    def mine(half):
        return (lane >= 64) if half else (lane < 64)

    def products(p):
        at = p * 128
        q = qkv_ref[0, :, at:at + 128] * 0.125
        k = qkv_ref[0, :, width + at:width + at + 128]
        return [nt(jnp.where(mine(half), q, 0), k) for half in range(2)]

    ready = None
    for p in range(pairs + 1):
        fresh = products(p) if p < pairs else None
        if ready is not None:
            at = (p - 1) * 128
            values = qkv_ref[0, :, 2 * width + at:2 * width + at + 128]
            total = jnp.zeros((pad, 128), F32)
            for half in range(2):
                scores = jnp.where(ok, ready[half], MASKED)
                top = jnp.max(scores, -1, keepdims=True)
                e = jnp.exp(scores - top)
                s = jnp.sum(e, -1, keepdims=True)
                prob = (e * (1.0 / s)).astype(BF16)
                total = total + nn(prob, jnp.where(mine(half), values, 0))
                lse_s[...] = jnp.where(lane == 2 * (p - 1) + half, top + jnp.log(s), lse_s[...])
            o_ref[0, :, at:at + 128] = total.astype(BF16)
        ready = fresh
    lse_ref[0] = jnp.transpose(lse_s[...])[0:16, :]


def front(counts, depth, images, cot, w, vec, pad):
    n, seq, width = images.shape
    grid_spec = pltpu.PrefetchScalarGridSpec(
        num_scalar_prefetch=2,
        grid=(n,),
        in_specs=[
            by_image((seq, width)), by_image((seq, width)),
            whole(w.shape), whole(vec.shape),
        ],
        out_specs=[
            by_image((pad, width)), by_image((pad, width)), by_image((pad, 3 * width)),
            by_image((pad, width)), by_image((16, pad)),
        ],
        scratch_shapes=[pltpu.VMEM((pad, width), F32), pltpu.VMEM((pad, 128), F32)],
    )
    return pl.pallas_call(
        functools.partial(front_kernel, seq, pad),
        out_shape=[
            jax.ShapeDtypeStruct((n, pad, width), BF16),
            jax.ShapeDtypeStruct((n, pad, width), BF16),
            jax.ShapeDtypeStruct((n, pad, 3 * width), BF16),
            jax.ShapeDtypeStruct((n, pad, width), BF16),
            jax.ShapeDtypeStruct((n, 16, pad), F32),
        ],
        grid_spec=grid_spec,
        compiler_params=params(60),
        cost_estimate=pl.CostEstimate(
            flops=2 * n * pad * width * (3 * width + 4 * pad), bytes_accessed=20 * MIB,
            transcendentals=n * 12 * pad * pad),
        name="front",
    )(counts, depth, images, cot, w, vec)


def middle_kernel(seq, pad, counts, depth, o_ref, x_ref, w_ref, vec_ref,
                  x1_ref, a2_ref, sums_ref, xs):
    i = pl.program_id(0)
    width = x_ref.shape[-1]
    rows = lax.broadcasted_iota(jnp.int32, (pad, 1), 0)
    ok = rows < counts[i]
    xs[pad - 8:pad, :] = jnp.zeros((8, width), F32)
    xs[0:seq, :] = x_ref[0].astype(F32)
    attn = nn(o_ref[0], w_ref[...]) + vec_ref[4:5, :]
    x1 = xs[...] + depth[i, 0] * attn
    x1_ref[0] = x1
    sums_ref[0, 0:1, :] = col_sum(jnp.where(ok, x1 * x1, 0.0))
    sums_ref[0, 1:2, :] = col_sum(jnp.where(ok, attn * attn, 0.0))
    sums_ref[0, 2:8, :] = jnp.zeros((6, width), F32)
    normed, _ = normalize(x1)
    a2_ref[0] = (normed * vec_ref[5:6, :] + vec_ref[6:7, :]).astype(BF16)


def middle(counts, depth, o, images, w, vec, pad):
    n, seq, width = images.shape
    grid_spec = pltpu.PrefetchScalarGridSpec(
        num_scalar_prefetch=2,
        grid=(n,),
        in_specs=[
            by_image((pad, width)), by_image((seq, width)),
            whole(w.shape), whole(vec.shape),
        ],
        out_specs=[by_image((pad, width)), by_image((pad, width)), by_image((8, width))],
        scratch_shapes=[pltpu.VMEM((pad, width), F32)],
    )
    return pl.pallas_call(
        functools.partial(middle_kernel, seq, pad),
        out_shape=[
            jax.ShapeDtypeStruct((n, pad, width), F32),
            jax.ShapeDtypeStruct((n, pad, width), BF16),
            jax.ShapeDtypeStruct((n, 8, width), F32),
        ],
        grid_spec=grid_spec,
        compiler_params=params(60),
        cost_estimate=pl.CostEstimate(
            flops=2 * n * pad * width * width, bytes_accessed=10 * MIB, transcendentals=0),
        name="middle",
    )(counts, depth, o, images, w, vec)


def gelu_pair(u):
    size = jnp.abs(u)
    t = 1.0 / (1.0 + (0.3275911 * INV_ROOT_TWO) * size)
    bell = jnp.exp(-0.5 * (u * u))
    series = t * (0.5 * 0.254829592 + t * (0.5 * -0.284496736 + t * (
        0.5 * 1.421413741 + t * (0.5 * -1.453152027 + t * (0.5 * 1.061405429)))))
    tail = series * bell
    phi = jnp.where(u >= 0, 1.0 - tail, tail)
    return u * phi, phi + u * (bell * INV_ROOT_TWO_PI)


def feed_kernel(seq, pad, counts, depth, a2_ref, gm_ref, up_ref, down_ref, bu_ref, x1_ref, cot_ref,
                vecs,
                dup_ref, ddown_ref, gbu_ref, y_ref, gx_ref, ga_ref, vec_ref,
                a2t, gmt, mlp, ga2, hs, gus, cs):
    j = pl.program_id(0)
    n = x1_ref.shape[0]

    @pl.when(j == 0)
    def _():
        a2t[...] = jnp.transpose(a2_ref[...])
        gmt[...] = jnp.transpose(gm_ref[...])
        mlp[...] = jnp.zeros_like(mlp)
        ga2[...] = jnp.zeros_like(ga2)

    gbu = jnp.zeros(bu_ref.shape[1:], F32)
    for i in range(n):
        at = slice(i * pad, (i + 1) * pad)
        u = nt(a2_ref[at, :], up_ref[...]) + bu_ref[0]
        t = nt(gm_ref[at, :], down_ref[...])
        act, slope = gelu_pair(u)
        h = act.astype(BF16)
        gu = (t * slope).astype(BF16)
        hs[at, :] = h
        gus[at, :] = gu
        gbu = gbu + col_sum(gu.astype(F32))
        mlp[at, :] += nn(h, down_ref[...])
        ga2[at, :] += nn(gu, up_ref[...])
    gbu_ref[0] = gbu
    dup_ref[0] = nn(a2t[...], gus[...]).astype(BF16)
    ddown_ref[0] = nn(gmt[...], hs[...]).astype(BF16)

    @pl.when(j == pl.num_programs(0) - 1)
    def _():
        width = x1_ref.shape[-1]
        rows = lax.broadcasted_iota(jnp.int32, (pad, 1), 0)
        cs[pad - 8:pad, :] = jnp.zeros((8, width), F32)
        msum = jnp.zeros((1, width), F32)
        ggain = jnp.zeros((1, width), F32)
        gshift = jnp.zeros((1, width), F32)
        gdown = jnp.zeros((1, width), F32)
        gout = jnp.zeros((1, width), F32)
        for i in range(n):
            at = slice(i * pad, (i + 1) * pad)
            ok = rows < counts[i]
            x1 = x1_ref[i]
            out = mlp[at, :] + vecs[7:8, :]
            msum = msum + col_sum(jnp.where(ok, out * out, 0.0))
            y_ref[i] = jnp.where(ok, x1 + depth[i, 1] * out, 0.0).astype(BF16)[0:seq]
            cs[0:seq, :] = cot_ref[i].astype(F32)
            g = jnp.where(ok, cs[...], 0.0)
            gdown = gdown + col_sum(gm_ref[at, :].astype(F32))
            back = ga2[at, :]
            normed, rstd = normalize(x1)
            ggain = ggain + col_sum(back * normed)
            gshift = gshift + col_sum(back)
            e = back * vecs[5:6, :]
            gx = g + rstd * (e - mean_row(e) - normed * mean_row(e * normed))
            gx_ref[i] = gx
            ga = (depth[i, 0] * gx).astype(BF16)
            ga_ref[i] = ga
            gout = gout + col_sum(ga.astype(F32))
        vec_ref[0:1, :] = ggain
        vec_ref[1:2, :] = gshift
        vec_ref[2:3, :] = gdown
        vec_ref[3:4, :] = gout
        vec_ref[4:5, :] = msum
        vec_ref[5:8, :] = jnp.zeros((3, width), F32)


def feed(counts, depth, a2, gm, up, down, bu, x1, cot, vec, seq, pad, block):
    rows, width = a2.shape
    n = rows // pad
    hidden = up.shape[0]
    steps = hidden // block
    at = lambda j, *_: (j, 0)
    at3 = lambda j, *_: (j, 0, 0)
    grid_spec = pltpu.PrefetchScalarGridSpec(
        num_scalar_prefetch=2,
        grid=(steps,),
        in_specs=[
            whole(a2.shape), whole(gm.shape),
            pl.BlockSpec((block, width), at), pl.BlockSpec((block, width), at),
            pl.BlockSpec((1, 1, block), at3),
            whole(x1.shape), whole(cot.shape), whole(vec.shape),
        ],
        out_specs=[
            pl.BlockSpec((1, width, block), at3), pl.BlockSpec((1, width, block), at3),
            pl.BlockSpec((1, 1, block), at3),
            whole((n, seq, width)), whole((n, pad, width)), whole((n, pad, width)), whole((8, width)),
        ],
        scratch_shapes=[
            pltpu.VMEM((width, rows), BF16), pltpu.VMEM((width, rows), BF16),
            pltpu.VMEM((rows, width), F32), pltpu.VMEM((rows, width), F32),
            pltpu.VMEM((rows, block), BF16), pltpu.VMEM((rows, block), BF16),
            pltpu.VMEM((pad, width), F32),
        ],
    )
    return pl.pallas_call(
        functools.partial(feed_kernel, seq, pad),
        out_shape=[
            jax.ShapeDtypeStruct((steps, width, block), BF16),
            jax.ShapeDtypeStruct((steps, width, block), BF16),
            jax.ShapeDtypeStruct((steps, 1, block), F32),
            jax.ShapeDtypeStruct((n, seq, width), BF16),
            jax.ShapeDtypeStruct((n, pad, width), F32),
            jax.ShapeDtypeStruct((n, pad, width), BF16),
            jax.ShapeDtypeStruct((8, width), F32),
        ],
        grid_spec=grid_spec,
        compiler_params=params(60),
        cost_estimate=pl.CostEstimate(
            flops=12 * rows * width * hidden, bytes_accessed=40 * MIB, transcendentals=rows * hidden),
        name="feed",
    )(counts, depth, a2, gm, up, down, bu.reshape(steps, 1, block), x1, cot, vec)


def back_kernel(pad, counts, ga_ref, w_ref, qkv_ref, lse_ref, g_ref, go):
    back_image(pad, counts[pl.program_id(0)], ga_ref.at[0], w_ref, qkv_ref, lse_ref, g_ref.at[0], go)


def back_image(pad, count, ga_ref, w_ref, qkv_ref, lse_ref, g_ref, go):
    width = ga_ref.shape[-1]
    go[...] = nt(ga_ref[...], w_ref[...]).astype(BF16)
    ok = lax.broadcasted_iota(jnp.int32, (pad, pad), 0) < count
    lane = lax.broadcasted_iota(jnp.int32, (pad, 128), 1)

    def pair(p):
        at = pl.multiple_of(p * 128, 128)
        q = qkv_ref[0, :, pl.ds(at, 128)] * 0.125
        k = qkv_ref[0, :, pl.ds(width + at, 128)]
        v = qkv_ref[0, :, pl.ds(2 * width + at, 128)]
        g = go[:, pl.ds(at, 128)]
        gq = jnp.zeros((pad, 128), F32)
        gk = jnp.zeros((pad, 128), F32)
        gv = jnp.zeros((pad, 128), F32)
        for half in range(2):
            mine = (lane >= 64) if half else (lane < 64)
            qm = jnp.where(mine, q, 0)
            km = jnp.where(mine, k, 0) * 0.125
            gmine = jnp.where(mine, g, 0)
            scores = nt(k, qm)
            row = lse_ref[0, 2 * p + half:2 * p + half + 1, :]
            prob = jnp.where(ok, jnp.exp(scores - row), 0.0)
            dp = nt(v, gmine)
            inner = col_sum(prob * dp)
            ds = (prob * (dp - inner)).astype(BF16)
            gv = gv + nn(prob.astype(BF16), gmine)
            gk = gk + nn(ds, qm)
            gq = gq + tn(ds, km)
        g_ref[:, pl.ds(at, 128)] = gq.astype(BF16)
        g_ref[:, pl.ds(width + at, 128)] = gk.astype(BF16)
        g_ref[:, pl.ds(2 * width + at, 128)] = gv.astype(BF16)

    for p in range(width // 128):
        pair(p)


def back(counts, ga, w, qkv, lse):
    n, pad, width = ga.shape
    grid_spec = pltpu.PrefetchScalarGridSpec(
        num_scalar_prefetch=1,
        grid=(n,),
        in_specs=[by_image((pad, width)), whole(w.shape), by_image((pad, 3 * width)), by_image((16, pad))],
        out_specs=[by_image((pad, 3 * width))],
        scratch_shapes=[pltpu.VMEM((pad, width), BF16)],
    )
    return pl.pallas_call(
        functools.partial(back_kernel, pad),
        out_shape=[jax.ShapeDtypeStruct((n, pad, 3 * width), BF16)],
        grid_spec=grid_spec,
        compiler_params=params(60),
        cost_estimate=pl.CostEstimate(
            flops=2 * n * pad * width * (width + 10 * pad), bytes_accessed=16 * MIB,
            transcendentals=n * 12 * pad * pad),
        name="back",
    )(counts, ga, w, qkv, lse)[0]


def outgrad_kernel(o_ref, ga_ref, d_ref):
    d_ref[...] = tn(o_ref[...], ga_ref[...]).astype(BF16)


def outgrad(o, ga):
    rows, width = o.shape
    return pl.pallas_call(
        outgrad_kernel,
        out_shape=jax.ShapeDtypeStruct((width, width), BF16),
        grid=(2,),
        in_specs=[pl.BlockSpec((rows, width // 2), lambda j: (0, j)), whole(ga.shape)],
        out_specs=pl.BlockSpec((width // 2, width), lambda j: (j, 0)),
        compiler_params=params(60),
        cost_estimate=pl.CostEstimate(
            flops=2 * rows * width * width, bytes_accessed=6 * MIB, transcendentals=0),
        name="outgrad",
    )(o, ga)


def last_kernel(seq, pad, g_ref, a1_ref, w_ref, x_ref, gx_ref, vecs,
                d_ref, cols_ref, gi_ref, vec_ref, ga1, xs):
    c = pl.program_id(0)
    n = x_ref.shape[0]
    g = g_ref[...]
    d_ref[...] = tn(g, a1_ref[...]).astype(BF16)
    cols_ref[...] = col_sum(g.astype(F32))
    part = nn(g, w_ref[...])

    @pl.when(c == 0)
    def _():
        ga1[...] = part

    @pl.when(c > 0)
    def _():
        ga1[...] += part

    @pl.when(c == pl.num_programs(0) - 1)
    def _():
        width = x_ref.shape[-1]
        xs[pad - 8:pad, :] = jnp.zeros((8, width), F32)
        ggain = jnp.zeros((1, width), F32)
        gshift = jnp.zeros((1, width), F32)
        for i in range(n):
            xs[0:seq, :] = x_ref[i].astype(F32)
            normed, rstd = normalize(xs[...])
            grad = ga1[i * pad:(i + 1) * pad, :]
            ggain = ggain + col_sum(grad * normed)
            gshift = gshift + col_sum(grad)
            e = grad * vecs[0:1, :]
            gi = gx_ref[i] + rstd * (e - mean_row(e) - normed * mean_row(e * normed))
            gi_ref[i] = gi[0:seq]
        vec_ref[0:1, :] = ggain
        vec_ref[1:2, :] = gshift
        vec_ref[2:8, :] = jnp.zeros((6, width), F32)


def last(g, a1, w, images, gx, vec, pad, block=384):
    n, seq, width = images.shape
    rows, total = g.shape
    return pl.pallas_call(
        functools.partial(last_kernel, seq, pad),
        out_shape=[
            jax.ShapeDtypeStruct((total, width), BF16),
            jax.ShapeDtypeStruct((1, total), F32),
            jax.ShapeDtypeStruct((n, seq, width), F32),
            jax.ShapeDtypeStruct((8, width), F32),
        ],
        grid=(total // block,),
        in_specs=[
            pl.BlockSpec((rows, block), lambda c: (0, c)), whole(a1.shape),
            pl.BlockSpec((block, width), lambda c: (c, 0)), whole(images.shape), whole(gx.shape),
            whole(vec.shape),
        ],
        out_specs=[
            pl.BlockSpec((block, width), lambda c: (c, 0)), pl.BlockSpec((1, block), lambda c: (0, c)),
            whole((n, seq, width)), whole((8, width)),
        ],
        scratch_shapes=[pltpu.VMEM((rows, width), F32), pltpu.VMEM((pad, width), F32)],
        compiler_params=params(60),
        cost_estimate=pl.CostEstimate(
            flops=4 * rows * width * total, bytes_accessed=30 * MIB, transcendentals=0),
        name="last",
    )(g, a1, w, images, gx, vec)


def shards_any(
    images, grid_sizes, keep_flags, attn_gain, attn_shift, attend_weight, query_bias, value_bias,
    output_weight, output_bias, mlp_gain, mlp_shift, up_weight, up_bias, down_weight, down_bias,
    cotangent,
):
    n, seq, width = images.shape
    pad = -(-seq // 32) * 32
    counts = grid_sizes[:, 0] * grid_sizes[:, 1] + 2
    depth = keep_flags.astype(F32) / KEEP_PROB
    owners = width // attn_gain.shape[0]

    small = jnp.concatenate([
        attn_gain, attn_shift, query_bias, value_bias, output_bias, mlp_gain, mlp_shift, down_bias, up_bias])
    small = lax.all_gather(small.reshape(1, -1), "fsdp", axis=0, tiled=True).astype(F32)
    share = attn_gain.shape[0]
    vec = jnp.stack([small[:, k * share:(k + 1) * share].reshape(width) for k in range(8)])
    bu = small[:, 8 * share:].reshape(1, -1)

    attend = lax.all_gather(attend_weight.T, "fsdp", axis=0, tiled=True)
    out_w = lax.all_gather(output_weight, "fsdp", axis=0, tiled=True)
    up = lax.all_gather(up_weight.T, "fsdp", axis=0, tiled=True)
    down = lax.all_gather(down_weight, "fsdp", axis=0, tiled=True)

    a1, gm, qkv, o, lse = front(counts, depth, images, cotangent, attend, vec, pad)
    x1, a2, sums_two = middle(counts, depth, o, images, out_w, vec, pad)
    flat = lambda array: array.reshape(n * pad, array.shape[-1])
    block = up_weight.shape[1] if up_weight.shape[1] % 128 == 0 else 384
    dup, ddown, gbu, y, gx, ga, vec_feed = feed(
        counts, depth, flat(a2), flat(gm), up, down, bu, x1, cotangent, vec, seq, pad, block)
    dout = outgrad(flat(o), flat(ga))
    g = back(counts, ga, out_w, qkv, lse)
    dattend, cols, gi, vec_last = last(flat(g), flat(a1), attend, images, gx, vec, pad)

    sums = jnp.stack([jnp.sum(sums_two[:, 0]), jnp.sum(sums_two[:, 1]), jnp.sum(vec_feed[4]),
                      jnp.sum(counts).astype(F32)])

    def spread(array):
        return lax.psum(lax.psum_scatter(array, "fsdp", scatter_dimension=0, tiled=True), "dp")

    def columns(array):
        hidden = up.shape[0]
        array = jnp.swapaxes(array, 0, 1).reshape(width, owners, hidden // owners)
        return jnp.swapaxes(array, 0, 1)

    gup = spread(columns(dup))[0]
    gdown = spread(columns(ddown))[0].T
    gout = spread(dout)
    gattend = spread(dattend).T
    rows = jnp.concatenate([
        vec_last[0:2], cols[:, :width], cols[:, 2 * width:], vec_feed[3:4], vec_feed[0:3],
    ], 0)
    tiny = jnp.concatenate([
        jnp.swapaxes(rows.reshape(8, owners, share), 0, 1).reshape(owners, 8 * share),
        gbu.reshape(owners, -1)], 1)
    tiny = spread(tiny)[0]
    sums = lax.psum(sums, ("dp", "fsdp"))
    root_means = jnp.sqrt(sums[:3] / (sums[3] * width))
    tv = [tiny[k * share:(k + 1) * share] for k in range(8)]
    f = lambda array: array.astype(F32)
    return (y, gi, tv[0], tv[1], f(gattend), tv[2], tv[3], f(gout), tv[4], tv[5], tv[6],
            f(gup), tiny[8 * share:], f(gdown), tv[7], root_means)


def over_dp(array, m):
    return lax.ppermute(array, "dp", [(i, i ^ m) for i in range(4)])


def over_z(array, a):
    return lax.ppermute(array, "fsdp", [(i, i ^ (2 * a)) for i in range(8)])


def over_core(array):
    return lax.ppermute(array, "fsdp", [(i, i ^ 1) for i in range(8)])


def staged(kernel, ids, arrays, out_shape, name):
    size = sum(math.prod(s.shape) * s.dtype.itemsize for s in [*arrays, *out_shape])
    return pl.pallas_call(
        kernel,
        out_shape=out_shape,
        grid_spec=pltpu.PrefetchScalarGridSpec(
            num_scalar_prefetch=1, grid=(1,),
            in_specs=[whole(s.shape) for s in arrays],
            out_specs=[whole(s.shape) for s in out_shape]),
        compiler_params=params(60),
        cost_estimate=pl.CostEstimate(flops=0, bytes_accessed=size, transcendentals=0),
        name=name,
    )(ids, *arrays)


def simple(kernel, ids, arrays, out_shape, name, scratch=()):
    size = sum(math.prod(s.shape) * s.dtype.itemsize for s in [*arrays, *out_shape])
    inside = pl.BlockSpec(memory_space=pltpu.VMEM)
    return pl.pallas_call(
        kernel,
        out_shape=out_shape,
        in_specs=[SMEM] + [inside] * len(arrays),
        out_specs=[inside] * len(out_shape),
        scratch_shapes=list(scratch),
        compiler_params=pltpu.CompilerParams(vmem_limit_bytes=16 * MIB),
        cost_estimate=pl.CostEstimate(flops=0, bytes_accessed=size, transcendentals=0),
        name=name,
    )(ids, *arrays)


def pack_kernel(ids, at_ref, ow_ref, up_ref, down_ref, *refs):
    vectors, (own1, first1, own, first, rest) = refs[:9], refs[9:]
    q = ids[0]
    att = at_ref[...]
    up = jnp.transpose(up_ref[...])
    r = ow_ref.shape[0]
    for t in range(4):
        own1[t ^ q] = att[t * r:(t + 1) * r] if t < 3 else ow_ref[...]
        k = r // 3
        own[t ^ q, 0:k] = up[t * k:(t + 1) * k]
        own[t ^ q, k:2 * k] = down_ref[t * k:(t + 1) * k, :]
    k = 4 * (r // 3)
    rest[0] = up[k:]
    rest[1] = down_ref[k:, :]
    first1[0:r, :] = own1[0]
    pieces = [v[...].reshape(1, -1).astype(F32) for v in vectors]
    blank = jnp.zeros((1, first1.shape[1] - r), F32)
    rows = [jnp.concatenate([p, blank], 1) for p in pieces[:8]]
    rows += [jnp.concatenate([pieces[8][:, k * r:(k + 1) * r], blank], 1) for k in range(4)]
    rows.append(jnp.zeros((4, first1.shape[1]), F32))
    first1[r:r + 16, :] = jnp.concatenate(rows, 0).astype(BF16)
    first[...] = own[0]


def pack(ids, at, ow, up, down, vectors):
    r, width = ow.shape
    s = lambda *shape: jax.ShapeDtypeStruct(shape, BF16)
    return staged(pack_kernel, ids, [at, ow, up, down, *vectors],
                  [s(4, r, width), s(r + 16, width), s(4, 2 * r // 3, width), s(2 * r // 3, width), s(2, 8 * r // 3, width)],
                  "pack")


def after(value, *before):
    return lax.optimization_barrier((value, before))[0]


def line(ids, own, first, zr, xr):
    r, width = own.shape[1:]

    def kernel(ids, own, first, z1, z2, z3, x1, x2, x3, mine):
        zs, xs = (z1, z2, z3), (x1, x2, x3)
        for m in range(4):
            mine[m * r:(m + 1) * r] = own[m]
        mine[16 * r:16 * r + 16] = first[r:r + 16]
        for a in range(1, 4):
            at = 4 * a * r
            mine[at:at + r] = zs[a - 1][0:r]
            mine[16 * r + 16 * a:16 * r + 16 * a + 16] = zs[a - 1][r:r + 16]
            for m in range(1, 4):
                mine[at + m * r:at + (m + 1) * r] = xs[m - 1][a - 1]

    return simple(kernel, ids, [own, first, *zr, *xr], [jax.ShapeDtypeStruct((16 * r + 64, width), BF16)], "line")[0]


def stack_rows(ids, arrays, spans):
    width = arrays[0].shape[1]

    def kernel(ids, *refs):
        for out, (low, high) in zip(refs[3:], spans):
            for a in range(3):
                out[a] = refs[a][low:high]

    return simple(kernel, ids, arrays,
                  [jax.ShapeDtypeStruct((3, high - low, width), BF16) for low, high in spans], "stack")


def early_kernel(seq, pad, counts, depth, x_ref, cot_ref, norm_ref, gm_ref, xs):
    i = pl.program_id(0)
    width = x_ref.shape[-1]
    ok = lax.broadcasted_iota(jnp.int32, (pad, 1), 0) < counts[i]
    xs[pad - 8:pad, :] = jnp.zeros((8, width), F32)
    xs[0:seq, :] = cot_ref[0].astype(F32)
    gm_ref[0] = jnp.where(ok, xs[...] * depth[i, 1], 0.0).astype(BF16)
    xs[0:seq, :] = x_ref[0].astype(F32)
    norm_ref[0], _ = normalize(xs[...])


def early(counts, depth, images, cot, pad):
    n, seq, width = images.shape
    sd = jax.ShapeDtypeStruct
    return pl.pallas_call(
        functools.partial(early_kernel, seq, pad),
        out_shape=[sd((n, pad, width), F32), sd((n, pad, width), BF16)],
        grid_spec=pltpu.PrefetchScalarGridSpec(
            num_scalar_prefetch=2, grid=(n,),
            in_specs=[by_image((seq, width)), by_image((seq, width))],
            out_specs=[by_image((pad, width)), by_image((pad, width))],
            scratch_shapes=[pltpu.VMEM((pad, width), F32)]),
        compiler_params=params(16),
        cost_estimate=pl.CostEstimate(flops=10 ** 7, bytes_accessed=9 * MIB, transcendentals=0),
        name="early",
    )(counts, depth, images, cot)


def head_kernel(pad, ids, counts, mine, sib, norm_ref, at_out, ow_out, vec_ref, b2_ref, b3_ref,
                a1_ref, qkv_ref, o_ref, lse_ref, at_s, ow_s, lse_s, sems):
    q, z, c = ids[0], ids[1], ids[2]
    copies = [pltpu.make_async_copy(at_s, at_out, sems.at[0]), pltpu.make_async_copy(ow_s, ow_out, sems.at[1])]
    step = pl.program_id(0)

    @pl.when(step == 0)
    def _():
        r = ow_s.shape[0] // 8
        cut = b2_ref.shape[2]
        for j in range(8):
            a = (j >> 1) ^ z
            own = ((j & 1) ^ c) == 0

            def place(ref_in):
                small = ref_in[pl.ds(pl.multiple_of(16 * r + 16 * a, 16), 16), 0:r].astype(F32)
                vec_ref[0:8, j * r:(j + 1) * r] = small[0:8]
                for k in range(4):
                    row = small[8 + k:9 + k]
                    at, to = k * r, (k + 1) * r
                    if at < cut:
                        b2_ref[j, :, at:min(to, cut)] = row[:, 0:min(to, cut) - at]
                    if to > cut:
                        b3_ref[j, :, max(at, cut) - cut:to - cut] = row[:, max(at, cut) - at:]
                for t in range(4):
                    ref, at = (ow_s, j * r) if t == 3 else (at_s, (3 * j + t) * r)
                    ref[at:at + r, :] = ref_in[pl.ds(pl.multiple_of((4 * a + (t ^ q)) * r, r), r), :]

            @pl.when(own)
            def _():
                place(mine)

            @pl.when(jnp.logical_not(own))
            def _():
                place(sib)

        for copy in copies:
            copy.start()

    attend_image(pad, counts[step], norm_ref[0], at_s, vec_ref, a1_ref, qkv_ref, o_ref, lse_ref, lse_s)

    @pl.when(step == pl.num_programs(0) - 1)
    def _():
        for copy in copies:
            copy.wait()


def head(ids, counts, mine, sib, norm):
    n, pad, width = norm.shape
    r = width // 8
    cut = 4 * r // 3
    sd = jax.ShapeDtypeStruct
    far = pl.BlockSpec(memory_space=pl.ANY)
    return pl.pallas_call(
        functools.partial(head_kernel, pad),
        out_shape=[
            sd((24 * r, width), BF16), sd((8 * r, width), BF16), sd((8, width), F32), sd((8, 1, cut), F32),
            sd((8, 1, 4 * r - cut), F32),
            sd((n, pad, width), BF16), sd((n, pad, 3 * width), BF16),
            sd((n, pad, width), BF16), sd((n, 16, pad), F32),
        ],
        grid_spec=pltpu.PrefetchScalarGridSpec(
            num_scalar_prefetch=2, grid=(n,),
            in_specs=[whole(mine.shape), whole(sib.shape), by_image((pad, width))],
            out_specs=[
                far, far, whole((8, width)), whole((8, 1, cut)), whole((8, 1, 4 * r - cut)),
                by_image((pad, width)), by_image((pad, 3 * width)),
                by_image((pad, width)), by_image((16, pad)),
            ],
            scratch_shapes=[
                pltpu.VMEM((24 * r, width), BF16), pltpu.VMEM((8 * r, width), BF16),
                pltpu.VMEM((pad, 128), F32), pltpu.SemaphoreType.DMA((2,))]),
        compiler_params=params(60),
        cost_estimate=pl.CostEstimate(
            flops=2 * n * pad * width * (3 * width + 4 * pad), bytes_accessed=20 * MIB,
            transcendentals=n * 12 * pad * pad),
        name="head",
    )(ids, counts, mine, sib, norm)


def part_kernel(seq, pad, second, group, ids, counts, depth, a2_ref, gm_ref, *rest):
    if second:
        weights, bu_ref, *rest = rest
    else:
        sides, bu_ref, rest = (rest[0:5], rest[5:10]), rest[10], rest[11:]
    if second:
        (mlp_in, ga2_in, a2t_in, gmt_in, x1_in, cot_ref, vecs,
         both, gbu_ref, y_ref, vec_ref, gx_out, ga_out,
         a2t, gmt, mlp, ga2, hs, gus, mlp_s, ga2_s, x1_s, ga_s, cs, sems, out_sems) = rest
        loads = [pltpu.make_async_copy(a, b, sems.at[k]) for k, (a, b) in enumerate(
            ((a2t_in, a2t), (gmt_in, gmt), (mlp_in, mlp_s), (ga2_in, ga2_s), (x1_in, x1_s)))]
    else:
        both, gbu_ref, mlp_out, ga2_out, a2t_out, gmt_out, a2t, gmt, mlp, ga2, hs, gus, sems = rest
        stores = [pltpu.make_async_copy(a, b, sems.at[k]) for k, (a, b) in enumerate(
            ((a2t, a2t_out), (gmt, gmt_out), (mlp, mlp_out), (ga2, ga2_out)))]
    step = pl.program_id(0)
    end = pl.num_programs(0) - 1
    q, z, c = ids[0], ids[1], ids[2]
    rows, width = a2_ref.shape
    n = rows // pad
    block = bu_ref.shape[-1]

    @pl.when(step == 0)
    def _():
        if second:
            for copy in loads:
                copy.start()
        else:
            a2t[...] = jnp.transpose(a2_ref[...])
            gmt[...] = jnp.transpose(gm_ref[...])
            stores[0].start()
            stores[1].start()
        mlp[...] = jnp.zeros_like(mlp)
        ga2[...] = jnp.zeros_like(ga2)

    pairs = [(k, side) for k in range(group) for side in range(2)]
    owners = [(((step * group + k) ^ z) << 1) | (c ^ side) for k, side in pairs]
    def piece(k, side, t, low):
        own, message, *crossed = sides[side]
        slot, m = step * group + k, t ^ q
        at = slice(low, low + r)
        index = jnp.maximum(slot - 1, 0) if group > 1 else 0
        value = message[index, at]
        for x, ref in enumerate(crossed):
            value = jnp.where(m == x + 1, ref[index, at], value)
        return jnp.where(slot == 0, own[m, at], value)

    if second:
        up, down = (jnp.concatenate([weights[c, kind], weights[c ^ 1, kind]], 0) for kind in range(2))
    else:
        r = sides[0][0].shape[1] // 2
        up = jnp.concatenate([piece(k, side, t, 0) for k, side in pairs for t in range(4)], 0)
        down = jnp.concatenate([piece(k, side, t, r) for k, side in pairs for t in range(4)], 0)
    bu = jnp.concatenate([bu_ref[owner] for owner in owners], 1)
    gbu = jnp.zeros(bu.shape, F32)
    ready = None
    for i in range(n + 1):
        if i < n:
            at = slice(i * pad, (i + 1) * pad)
            fresh = nt(a2_ref[at, :], up) + bu, nt(gm_ref[at, :], down)
        if ready is not None:
            at = slice((i - 1) * pad, i * pad)
            u, t = ready
            act, slope = gelu_pair(u)
            h = act.astype(BF16)
            gu = (t * slope).astype(BF16)
            hs[at, :] = h
            gus[at, :] = gu
            gbu = gbu + col_sum(gu.astype(F32))
            mlp[at, :] += nn(h, down)
            ga2[at, :] += nn(gu, up)
        ready = fresh
    for p, owner in enumerate(owners):
        gbu_ref[owner] = gbu[:, p * block:(p + 1) * block]

    if second:
        @pl.when(step == 0)
        def _():
            loads[0].wait()
            loads[1].wait()
    else:
        @pl.when(step == end)
        def _():
            stores[2].start()
            stores[3].start()

    part = width // 4
    span = 2 * group
    for t in range(4):
        at = slice(t * part, (t + 1) * part)
        for kind, (left, right) in enumerate(((a2t, gus), (gmt, hs))):
            d = nn(left[at, :], right[...]).astype(BF16)
            for p, owner in enumerate(owners):
                both[owner % span, t, kind] = d[:, p * block:(p + 1) * block]

    if not second:
        @pl.when(step == end)
        def _():
            for copy in stores:
                copy.wait()
        return

    @pl.when(step == end)
    def _():
        for copy in loads[2:]:
            copy.wait()
        mask_rows = lax.broadcasted_iota(jnp.int32, (pad, 1), 0)
        cs[pad - 8:pad, :] = jnp.zeros((8, width), F32)
        sums = [jnp.zeros((1, width), F32)] * 5
        outs = []
        for i in range(n):
            at = slice(i * pad, (i + 1) * pad)
            ok = mask_rows < counts[i]
            x1 = x1_s[i]
            out = mlp[at, :] + mlp_s[at, :] + vecs[7:8, :]
            y_ref[i] = jnp.where(ok, x1 + depth[i, 1] * out, 0.0).astype(BF16)[0:seq]
            cs[0:seq, :] = cot_ref[i].astype(F32)
            g = jnp.where(ok, cs[...], 0.0)
            back = ga2[at, :] + ga2_s[at, :]
            normed, rstd = normalize(x1)
            e = back * vecs[5:6, :]
            gx = g + rstd * (e - mean_row(e) - normed * mean_row(e * normed))
            ga = (depth[i, 0] * gx).astype(BF16)
            x1_s[i] = gx
            ga_s[i] = ga
            for k, (ref, to) in enumerate(((x1_s, gx_out), (ga_s, ga_out))):
                copy = pltpu.make_async_copy(ref.at[i], to.at[i], out_sems.at[i, k])
                copy.start()
                outs.append(copy)
            terms = (back * normed, back, gm_ref[at, :].astype(F32), ga.astype(F32), jnp.where(ok, out * out, 0.0))
            sums = [total + col_sum(term) for total, term in zip(sums, terms)]
        for k, total in enumerate(sums):
            vec_ref[k:k + 1, :] = total
        vec_ref[5:8, :] = jnp.zeros((3, width), F32)
        for copy in outs:
            copy.wait()


def part(ids, counts, depth, a2, gm, weights, bu, pad, group, carry=(), x1=None, cot=None, vec=None):
    rows, width = a2.shape
    n = rows // pad
    block = bu.shape[-1]
    second = len(carry) > 0
    sd = jax.ShapeDtypeStruct
    if second:
        w_specs = [pl.BlockSpec((2, 2, block, width), lambda s, ids, *_: (s ^ ids[1], 0, 0, 0))]
    else:
        w_specs = [whole(w.shape) for w in weights]
    far = pl.BlockSpec(memory_space=pl.ANY)
    acc = sd((rows, width), F32)
    tr = sd((width, rows), BF16)
    in_specs = [whole(a2.shape), whole(gm.shape)] + w_specs + [whole(bu.shape)]
    args = [a2, gm, *weights, bu]
    outs = [sd((8, 4, 2, width // 4, block), BF16), sd((8, 1, block), F32)]
    out_specs = [
        pl.BlockSpec((2 * group, 4, 2, width // 4, block), lambda s, ids, *_: (s ^ (ids[1] // group), 0, 0, 0, 0)),
        whole((8, 1, block))]
    scratch = [pltpu.VMEM(tr.shape, BF16), pltpu.VMEM(tr.shape, BF16), pltpu.VMEM(acc.shape, F32),
               pltpu.VMEM(acc.shape, F32), pltpu.VMEM((rows, 2 * group * block), BF16),
               pltpu.VMEM((rows, 2 * group * block), BF16)]
    if second:
        seq = cot.shape[1]
        args += [*carry, x1, cot, vec]
        in_specs += [far] * 5 + [whole(cot.shape), whole(vec.shape)]
        outs += [sd((n, seq, width), BF16), sd((8, width), F32), sd((n, pad, width), F32), sd((n, pad, width), BF16)]
        out_specs += [whole((n, seq, width)), whole((8, width)), far, far]
        scratch += [pltpu.VMEM(acc.shape, F32), pltpu.VMEM(acc.shape, F32), pltpu.VMEM((n, pad, width), F32),
                    pltpu.VMEM((n, pad, width), BF16), pltpu.VMEM((pad, width), F32), pltpu.SemaphoreType.DMA((5,)),
                    pltpu.SemaphoreType.DMA((n, 2))]
    else:
        seq = 0
        outs += [acc, acc, tr, tr]
        out_specs += [far] * 4
        scratch += [pltpu.SemaphoreType.DMA((4,))]
    return pl.pallas_call(
        functools.partial(part_kernel, seq, pad, second, group),
        out_shape=outs,
        grid_spec=pltpu.PrefetchScalarGridSpec(
            num_scalar_prefetch=3, grid=(4 // group,), in_specs=in_specs, out_specs=out_specs,
            scratch_shapes=scratch),
        compiler_params=params(60),
        cost_estimate=pl.CostEstimate(
            flops=12 * rows * width * 8 * block, bytes_accessed=30 * MIB, transcendentals=0),
        name="feed_b" if second else "feed_a",
    )(ids, counts, depth, *args)


def back_first_kernel(pad, ids, counts, ga_ref, w_ref, qkv_ref, lse_ref, o_in, a1_in, g_out, near_p, far_p, near_q, far_q,
                      go, g_s, o_s, a1_s, sems, out_sems):
    i = pl.program_id(0)
    n, _, width = ga_ref.shape
    loads = [pltpu.make_async_copy(o_in, o_s, sems.at[0]), pltpu.make_async_copy(a1_in, a1_s, sems.at[1])]

    @pl.when(i == 0)
    def _():
        for copy in loads:
            copy.start()

    back_image(pad, counts[i], ga_ref.at[i], w_ref, qkv_ref, lse_ref, g_s.at[i], go)
    pltpu.make_async_copy(g_s.at[i], g_out.at[i], out_sems.at[i]).start()

    @pl.when(i == n - 1)
    def _():
        for copy in loads:
            copy.wait()
        q, z, c = ids[0], ids[1], ids[2]
        r = near_p.shape[2]

        def put(value, group, j, t):
            a, m = ((j >> 1) ^ z) & 1, t ^ q
            own = ((j & 1) ^ c) == 0

            @pl.when(own)
            def _():
                group[0][m, a] = value

            @pl.when(jnp.logical_not(own))
            def _():
                group[1][m, a] = value

        for group, side in (((near_p, far_p), 1 - (z >> 1)), ((near_q, far_q), z >> 1)):
            for s in range(4):
                if s < 3:
                    cols = pl.ds(pl.multiple_of(side * (12 * r) + s * (4 * r), 128), 4 * r)
                    left = g_s[:, :, cols].reshape(n * pad, 4 * r)
                    d = tn(left, a1_s[...].reshape(n * pad, width)).astype(BF16)
                else:
                    cols = pl.ds(pl.multiple_of(side * (4 * r), 128), 4 * r)
                    left = o_s[:, :, cols].reshape(n * pad, 4 * r)
                    d = tn(left, ga_ref[...].reshape(n * pad, width)).astype(BF16)
                for k in range(4):
                    chunk = 4 * s + k
                    value = d[k * r:(k + 1) * r]
                    if s < 3:
                        put(value, group, 4 * side + chunk // 3, chunk % 3)
                    else:
                        put(value, group, 4 * side + k, 3)
        for k in range(n):
            pltpu.make_async_copy(g_s.at[k], g_out.at[k], out_sems.at[k]).wait()


def back_first(ids, counts, ga, w, qkv, lse, o, a1):
    n, pad, width = ga.shape
    r = width // 8
    sd = jax.ShapeDtypeStruct
    far = pl.BlockSpec(memory_space=pl.ANY)
    group = sd((4, 2, r, width), BF16)
    return pl.pallas_call(
        functools.partial(back_first_kernel, pad),
        out_shape=[sd((n, pad, 3 * width), BF16)] + [group] * 4,
        grid_spec=pltpu.PrefetchScalarGridSpec(
            num_scalar_prefetch=2, grid=(n,),
            in_specs=[whole(ga.shape), whole(w.shape), by_image((pad, 3 * width)), by_image((16, pad)), far, far],
            out_specs=[far] + [whole(group.shape)] * 4,
            scratch_shapes=[
                pltpu.VMEM((pad, width), BF16), pltpu.VMEM((n, pad, 3 * width), BF16), pltpu.VMEM((n, pad, width), BF16),
                pltpu.VMEM((n, pad, width), BF16), pltpu.SemaphoreType.DMA((2,)), pltpu.SemaphoreType.DMA((n,))]),
        compiler_params=params(60),
        cost_estimate=pl.CostEstimate(
            flops=2 * n * pad * width * (3 * width + 10 * pad), bytes_accessed=16 * MIB,
            transcendentals=n * 12 * pad * pad),
        name="back",
    )(ids, counts, ga, w, qkv, lse, o, a1)


def final_kernel(seq, pad, g_ref, w_ref, x_ref, gx_ref, y_ref, vecs, gi_ref, y_out, vec_ref, cols_ref, xs):
    i = pl.program_id(0)
    width = x_ref.shape[-1]
    grad = nn(g_ref[0], w_ref[...])
    xs[pad - 8:pad, :] = jnp.zeros((8, width), F32)
    xs[0:seq, :] = x_ref[0].astype(F32)
    normed, rstd = normalize(xs[...])

    @pl.when(i == 0)
    def _():
        vec_ref[...] = jnp.zeros_like(vec_ref)
        cols_ref[...] = jnp.zeros_like(cols_ref)

    vec_ref[0:1, :] += col_sum(grad * normed)
    vec_ref[1:2, :] += col_sum(grad)
    cols_ref[...] += col_sum(g_ref[0].astype(F32))
    e = grad * vecs[0:1, :]
    gi = gx_ref[0] + rstd * (e - mean_row(e) - normed * mean_row(e * normed))
    for k in range(gi_ref.shape[1]):
        @pl.when(i == k)
        def _():
            gi_ref[:, k, :] = gi[0:seq]
            y_out[:, k, :] = y_ref[0]


def final(g, w, images, gx, y, vec, pad):
    n, seq, width = images.shape
    sd = jax.ShapeDtypeStruct
    return pl.pallas_call(
        functools.partial(final_kernel, seq, pad),
        out_shape=[sd((seq, n, width), F32), sd((seq, n, width), BF16), sd((8, width), F32), sd((1, 3 * width), F32)],
        grid=(n,),
        in_specs=[by_image((pad, 3 * width)), whole(w.shape), by_image((seq, width)), by_image((pad, width)),
                  by_image((seq, width)), whole(vec.shape)],
        out_specs=[whole((seq, n, width)), whole((seq, n, width)), whole((8, width)), whole((1, 3 * width))],
        scratch_shapes=[pltpu.VMEM((pad, width), F32)],
        compiler_params=params(60),
        cost_estimate=pl.CostEstimate(
            flops=6 * n * pad * width * width, bytes_accessed=18 * MIB, transcendentals=0),
        name="final",
    )(g, w, images, gx, y, vec)


def add_pair(ids, near, got):
    slots, parts = near.shape[:2]
    shape = near.shape[1:]
    block = pl.BlockSpec((slots, 1) + shape[1:], lambda a, *_: (0, a) + (0,) * (len(shape) - 1))

    def kernel(a_ref, b_ref, *outs):
        for m in range(4):
            outs[m][...] = (a_ref[m].astype(F32) + b_ref[m].astype(F32)).astype(BF16)

    return pl.pallas_call(
        kernel,
        out_shape=[jax.ShapeDtypeStruct(shape, BF16)] * slots,
        grid=(parts,),
        in_specs=[block, block],
        out_specs=[pl.BlockSpec((1,) + shape[1:], lambda a: (a,) + (0,) * (len(shape) - 1))] * slots,
        compiler_params=params(60),
        cost_estimate=pl.CostEstimate(flops=0, bytes_accessed=6 * near.size, transcendentals=0),
        name="add_pair",
    )(near, got)


def add_four(ids, parts, split):
    shape = parts[0].shape

    def kernel(ids, a, b, c, d, *outs):
        if split:
            for k in range(shape[0]):
                outs[k][...] = ((a[k].astype(F32) + b[k].astype(F32)) + (c[k].astype(F32) + d[k].astype(F32))).astype(BF16)
        else:
            outs[0][...] = ((a[...].astype(F32) + b[...].astype(F32)) + (c[...].astype(F32) + d[...].astype(F32))).astype(BF16)

    count = shape[0] if split else 1
    out = jax.ShapeDtypeStruct(shape[1:] if split else shape, BF16)
    return simple(kernel, ids, parts, [out] * count, "add_four")


def merge(ids, s2, s3):
    _, _, rows, k2 = s2.shape
    k3 = s3.shape[3]

    def kernel(ids, a, b, out):
        for ref, at, to in ((a, 0, k2), (b, k2, k2 + k3)):
            out[:, :, at:to] = ((ref[0].astype(F32) + ref[1].astype(F32)) + (ref[2].astype(F32) + ref[3].astype(F32))).astype(BF16)

    return simple(kernel, ids, [s2, s3], [jax.ShapeDtypeStruct((2, rows, k2 + k3), BF16)], "merge")[0]


def place_feed_kernel(ids, p0, p1, p2, p3, up_ref, down_ref, cs):
    q = ids[0]
    rows = p0.shape[1]
    for m, p in enumerate((p0, p1, p2, p3)):
        to = pl.ds(pl.multiple_of((q ^ m) * rows, rows), rows)
        up_ref[to, :] = p[0].astype(F32)
        cs[to, :] = p[1].astype(F32)
    down_ref[...] = jnp.transpose(cs[...])


def place_feed(ids, parts):
    _, rows, block = parts[0].shape
    sd = jax.ShapeDtypeStruct
    return simple(place_feed_kernel, ids, parts, [sd((4 * rows, block), F32), sd((block, 4 * rows), F32)],
                  "place_feed", scratch=[pltpu.VMEM((4 * rows, block), F32)])


def place_attend_kernel(ids, p0, p1, p2, p3, at_ref, ow_ref, cs):
    q = ids[0]
    r = p0.shape[0]
    for m, p in enumerate((p0, p1, p2, p3)):
        cs[pl.ds(pl.multiple_of((q ^ m) * r, r), r), :] = p[...].astype(F32)
    at_ref[...] = cs[0:3 * r, :]
    ow_ref[...] = cs[3 * r:4 * r, :]


def place_attend(ids, parts):
    r, width = parts[0].shape
    sd = jax.ShapeDtypeStruct
    return simple(place_attend_kernel, ids, parts, [sd((3 * r, width), F32), sd((r, width), F32)],
                  "place_attend", scratch=[pltpu.VMEM((4 * r, width), F32)])


def cut_vectors(ids, rows, share):
    width = rows.shape[1]
    parts = width // share

    def kernel(ids, rows_ref, *outs):
        owner = 2 * ids[1] + ids[2]
        vectors, bias = outs[:8], outs[8]
        for j in range(parts):
            @pl.when(owner == j)
            def _():
                for k in range(8):
                    vectors[k][...] = rows_ref[k:k + 1, j * share:(j + 1) * share].reshape(share)
                at = j * 4 * share
                bias[...] = rows_ref[8 + at // width:9 + at // width, at % width:at % width + 4 * share].reshape(4 * share)

    sd = jax.ShapeDtypeStruct
    return simple(kernel, ids, [rows], [sd((share,), F32)] * 8 + [sd((4 * share,), F32)], "cut_vectors")


def shards_grid(
    images, grid_sizes, keep_flags, attn_gain, attn_shift, attend_weight, query_bias, value_bias,
    output_weight, output_bias, mlp_gain, mlp_shift, up_weight, up_bias, down_weight, down_bias,
    cotangent,
):
    n, seq, width = images.shape
    pad = -(-seq // 32) * 32
    counts = grid_sizes[:, 0] * grid_sizes[:, 1] + 2
    depth = keep_flags.astype(F32) / KEEP_PROB
    owners = 8
    share = attn_gain.shape[0]
    f = lax.axis_index("fsdp")
    ids = jnp.stack([lax.axis_index("dp"), f >> 1, f & 1]).astype(jnp.int32)

    z_all = lambda array: [over_z(array, a) for a in (1, 2, 3)]
    dp_all = lambda array: [over_dp(array, m) for m in (1, 2, 3)]
    dp_out = lambda s: [s[0]] + [over_dp(s[m], m) for m in (1, 2, 3)]
    z_out = lambda s: [s[0]] + [over_z(s[a], a) for a in (1, 2, 3)]
    tied = lax.optimization_barrier
    flat = lambda array: array.reshape(n * pad, array.shape[-1])

    own1, first1, own, first, rest = pack(
        ids, attend_weight.T, output_weight, up_weight, down_weight,
        [attn_gain, attn_shift, query_bias, value_bias, output_bias, mlp_gain, mlp_shift, down_bias, up_bias])
    zr1 = z_all(first1)
    own_other = over_core(own)
    first, rest, zr1, own_other = tied((first, rest, zr1, own_other))
    message1, = stack_rows(ids, zr1, [(0, share)])
    xr1 = dp_all(message1)
    zr = z_all(first)
    weights_b = lax.all_gather(rest[None], "fsdp", axis=0, tiled=True)
    norm, gm = early(counts, depth, images, cotangent, pad)
    xr1, zr, norm, gm = tied((xr1, zr, norm, gm))
    mine1 = line(ids, own1, first1, zr1, xr1)
    sib1 = over_core(mine1)
    message, = stack_rows(ids, zr, [(0, first.shape[0])])
    message_other = over_core(message)
    xr = dp_all(message)
    sib1, message_other = tied((sib1, message_other))
    attend, out_w, vec, bu2, bu3, a1, qkv, o, lse = head(ids, counts, mine1, sib1, norm)
    o, xr = tied((o, xr))
    sib = [own_other, message_other, *(over_core(x) for x in xr)]
    x1, a2, sums_two = middle(counts, depth, o, images, out_w, vec, pad)
    x1, a2, sib = tied((x1, a2, sib))
    a2, gm = flat(a2), flat(gm)
    both2, gbu2, mlp, ga2, a2t, gmt = part(
        ids, counts, depth, a2, gm, [own, message, *xr, *sib], bu2, pad, 2)
    mlp, weights_b = tied((mlp, weights_b))

    own_sum = lambda both: lax.psum_scatter(
        both.reshape(-1, both.shape[-1]), "fsdp", scatter_dimension=0, tiled=True).reshape(both.shape[1:])
    quarter = lambda shard: lax.all_to_all(shard, "dp", 0, 0, tiled=True)
    shard2 = own_sum(both2)
    both3, gbu3, y, vec_feed, gx, ga = part(
        ids, counts, depth, a2, gm, [weights_b], bu3, pad, 1, (mlp, ga2, a2t, gmt), x1, cotangent, vec)
    shard3 = own_sum(both3)
    quarter2 = quarter(after(shard2, ga))
    g, near_p, far_p, near_q, far_q = back_first(ids, counts, ga, out_w, qkv, lse, o, a1)
    g, near_p, far_p, near_q, far_q, quarter2 = tied((g, near_p, far_p, near_q, far_q, quarter2))
    got_p = over_core(far_p)
    got_q = over_core(far_q)
    s_p = add_pair(ids, near_p, got_p)
    dr_p = dp_out(s_p)
    gi, y, vec_last, cols = final(after(g, s_p), attend, images, gx, y, vec, pad)
    y, gi = y.swapaxes(0, 1), gi.swapaxes(0, 1)
    rows = jnp.concatenate([
        vec_last[0:2], cols[:, :width], cols[:, 2 * width:], vec_feed[3:4], vec_feed[0:3],
        jnp.concatenate([gbu2[:, 0], gbu3[:, 0]], 1).reshape(4, width), sums_two[:, 0:2].sum(0), vec_feed[4:5],
        jnp.full((1, width), jnp.sum(counts).astype(F32)),
    ], 0)
    rows = rows + over_core(rows)
    rows, got_q, dr_p = tied((rows, got_q, dr_p))
    s_q = add_pair(ids, near_q, got_q)
    rows = rows + over_dp(rows, 1)
    s_q, rows = tied((s_q, rows))
    dr_q = dp_out(s_q)
    quarter3 = quarter(after(shard3, s_q))
    e_p = add_four(ids, after(dr_p, s_q), True)
    er_p = [over_z(x, a) for a, x in zip((2, 3), e_p)]
    er_p, dr_q, rows, quarter3 = tied((er_p, dr_q, rows, quarter3))
    e_q = add_four(ids, dr_q, True)
    er_q = over_z(e_q[1], 1)
    rows = after(rows, e_q)
    rows = rows + over_dp(rows, 2)
    f3 = merge(ids, quarter2, after(quarter3, e_q))
    fr3 = [f3] + dp_all(f3)
    er_q, fr3[1], fr3[2] = tied((er_q, fr3[1], fr3[2]))
    f1 = add_four(ids, [e_q[0], er_q, *er_p], False)[0]
    fr1 = [f1] + dp_all(f1)
    got = z_all(after(rows, f1))
    rows = (rows + got[0]) + (got[1] + got[2])
    root_means = jnp.sqrt(jnp.sum(rows[12:15], 1) / (rows[15, 0] * width))
    *tv, gub = cut_vectors(ids, rows, share)
    gup, gdown = place_feed(ids, fr3)
    gattend, gout = place_attend(ids, fr1)
    gattend = gattend.T
    return (y, gi, tv[0], tv[1], gattend, tv[2], tv[3], gout, tv[4], tv[5], tv[6],
            gup, gub, gdown, tv[7], root_means)


def shards(on_grid, *args):
    images, attn_gain, up_weight = args[0], args[3], args[12]
    share = attn_gain.shape[0]
    fits = on_grid and share % 48 == 0 and up_weight.shape[1] == 4 * share and images.shape[2] == 8 * share
    return (shards_grid if fits else shards_any)(*args)


def solution(mesh):
    images = P(("dp", "fsdp"), None, None)
    flags = P(("dp", "fsdp"), None)
    vec, rows, cols = P("fsdp"), P("fsdp", None), P(None, "fsdp")
    return jax.shard_map(
        functools.partial(shards, dict(mesh.shape) == {"dp": 4, "fsdp": 8}),
        mesh=mesh,
        in_specs=(images, flags, flags, vec, vec, cols, vec, vec, rows, vec, vec, vec, cols, vec, rows,
                  vec, images),
        out_specs=(images, images, vec, vec, cols, vec, vec, rows, vec, vec, vec, cols, vec, rows, vec,
                   P()),
        check_vma=False,
    )
```
